256 devices in a mesh: row: 8 (over x, y_hi), col: 32 (over z, y_lo, core).
Axes of the slice: x: 4, y: 4 (y_hi: 2, y_lo: 2; y = y_hi * 2 + y_lo), z: 8, core: 2. Of those that a mesh axis runs over, the one named last changes fastest.
Arguments:
- position: float32 [3, 1048576], P(None, ('row', 'col')), may hold values from -6 to 6
- velocity: float32 [3, 1048576], P(None, ('row', 'col')), may hold values from -4 to 4
- accel_old: float32 [3, 1048576], P(None, ('row', 'col')), may hold values from -6 to 6
- jerk_old: float32 [3, 1048576], P(None, ('row', 'col')), may hold values from -12 to 12
- mass: float32 [1048576], P(('row', 'col')), may hold values from 4.7683716e-07 to 4.7683716e-06
- elapsed: float32 [1048576], P(('row', 'col')), may hold values from 0.05 to 0.5
- active_index: int32 [2048], P(('row', 'col')), may hold values from 0 to 4095, as said below
- active_count: int32 [256], P(('row', 'col')), may hold values from 1 to 8, as said below
Outputs:
- accel_new: float32 [3, 2048], P(None, ('row', 'col'))
- jerk_new: float32 [3, 2048], P(None, ('row', 'col'))
The draws below stay inside these ranges and needn't reach their ends.
Inputs may be any that keep to these rules, and one draw needn't show every extreme that they name: `active_index`: within each device's 8 slots the entries are distinct indices into that device's 4096 stars; entries of slots that are not live are ignored. `active_count`: most devices have few live slots; some device fills all of them.
All inputs are finite; a program needn't handle non-finite values.
Results may differ from the reference program's by a relative error of at most 0.0003.
Values sent between devices are 32-bit elements; how exact they have to be, the bound alone decides.
A program may use at most 64 MiB of HBM per device.

```python
import math
import jax
import jax.numpy as jnp
from jax import lax

STAR_DEV = 4096
ACT_MAX = 8
NSTARS = 1048576
SLOTS = 2048


def draw_active_index(key, part):
    key = jax.random.fold_in(key, 11)
    owners = SLOTS // ACT_MAX
    many_keys = jax.random.split(key, owners + 1)
    orders = jax.vmap(lambda single: jax.random.permutation(single, STAR_DEV))(many_keys[:owners])[:, :ACT_MAX]
    chosen = jax.random.randint(many_keys[owners], (), 0, owners)
    owner_ids = jnp.arange(owners)
    leading = orders[:, 0]
    top_shift = STAR_DEV - 1 - leading
    low_shift = (STAR_DEV - leading) % STAR_DEV
    offsets = jnp.where(owner_ids == chosen, top_shift, jnp.where(owner_ids == (chosen + 1) % owners, low_shift, 0))
    return ((orders + offsets[:, None]) % STAR_DEV).reshape(-1).astype(jnp.int32)


def draw_active_count(key, part):
    key = jax.random.fold_in(key, 23)
    first_key, second_key = jax.random.split(key)
    owners = SLOTS // ACT_MAX
    levels = jax.random.randint(first_key, (owners,), 0, 1024)
    counts = 1 + (ACT_MAX - 1) * levels * levels // (1023 * 1023)
    chosen = jax.random.randint(second_key, (), 0, owners)
    owner_ids = jnp.arange(owners)
    counts = jnp.where(owner_ids == chosen, ACT_MAX, counts)
    counts = jnp.where(owner_ids == (chosen + 1) % owners, 1, counts)
    return counts.astype(jnp.int32)


def shard_levels(stream_key, shape, cuts, least, high):
    level = 1.0
    for dim, parts in cuts:
        steps = jax.random.uniform(jax.random.fold_in(jax.random.fold_in(stream_key, 6), dim), (parts,), jnp.float32, least / len(cuts), high / len(cuts))
        level = level * jnp.repeat(jnp.exp(steps), shape[dim] // parts).reshape((-1,) + (1,) * (len(shape) - 1 - dim))
    return level


def normal_values(stream_key, shape, spread, most, shards=(), held_as=jnp.bfloat16):
    loudness = shard_levels(stream_key, shape, shards, -0.22, 0.18) if shards else 1.0
    entries = jax.random.normal(stream_key, shape, jnp.float32) * spread * loudness
    return jnp.minimum(jnp.maximum(entries, -most), most).astype(held_as)


def setup_inputs(seed: int = 0) -> dict:
    seeds = jax.random.split(jax.random.key(seed), 9)
    return {
        "position": normal_values(seeds[0], (3, NSTARS), 1.0, 6.0, ((1, 256),), jnp.float32),
        "velocity": normal_values(seeds[1], (3, NSTARS), 0.5, 4.0, ((1, 256),), jnp.float32),
        "accel_old": normal_values(seeds[2], (3, NSTARS), 1.0, 6.0, ((1, 256),), jnp.float32),
        "jerk_old": normal_values(seeds[3], (3, NSTARS), 2.0, 12.0, ((1, 256),), jnp.float32),
        "mass": jnp.clip(jnp.exp(math.log(4.76837158203125e-06) - 2.3025851 * jax.random.uniform(seeds[4], (NSTARS,), jnp.float32) ** shard_levels(seeds[4], (NSTARS,), ((0, 256),), -0.2, 0.2)), 4.76837158203125e-07, 4.76837158203125e-06),
        "elapsed": jnp.clip(0.05 + 0.45 * jax.random.uniform(seeds[5], (NSTARS,), jnp.float32) ** shard_levels(seeds[5], (NSTARS,), ((0, 256),), -0.2, 0.2), 0.05, 0.5),
        "active_index": draw_active_index(jax.random.fold_in(seeds[8], 71), 0),
        "active_count": draw_active_count(jax.random.fold_in(seeds[8], 71), 0),
    }


SOFTENING = 0.0025

def predict(position, velocity, accel_old, jerk_old, elapsed):
    step_dt = elapsed[None, :]
    pos_pred = position + step_dt * (velocity + step_dt * (0.5 * accel_old + step_dt * (jerk_old / 6.0)))
    vel_pred = velocity + step_dt * (accel_old + step_dt * (0.5 * jerk_old))
    return (pos_pred, vel_pred)

def pair_terms(targets, sources):
    delta_x = sources[0:3, None, :] - targets[0:3, :, None]
    delta_v = sources[3:6, None, :] - targets[3:6, :, None]
    dist_sq = SOFTENING + lax.optimization_barrier(jnp.sum(delta_x * delta_x, axis=0))
    inv_dist = lax.rsqrt(dist_sq)
    mass_r3 = sources[6][None, :] * inv_dist * inv_dist * inv_dist
    radial = 3.0 * lax.optimization_barrier(jnp.sum(delta_x * delta_v, axis=0)) / dist_sq
    accel_sum = lax.optimization_barrier(jnp.sum(mass_r3[None] * delta_x, axis=2))
    jerk_sum = lax.optimization_barrier(jnp.sum(mass_r3[None] * (delta_v - radial[None] * delta_x), axis=2))
    return jnp.concatenate([accel_sum, jerk_sum], axis=0)

def reference(position, velocity, accel_old, jerk_old, mass, elapsed, active_index, active_count):
    pos_pred, vel_pred = predict(position, velocity, accel_old, jerk_old, elapsed)
    sources = jnp.concatenate([pos_pred, vel_pred, mass[None, :]], axis=0)
    slot_ids = jnp.arange(SLOTS, dtype=jnp.int32)
    owner_ids = (slot_ids // ACT_MAX).astype(jnp.int32)
    global_ids = (owner_ids * STAR_DEV + active_index).astype(jnp.int32)
    targets = jnp.take(sources[0:6], global_ids, axis=1)
    live_mask = slot_ids % ACT_MAX < jnp.take(active_count, owner_ids)
    target_rows = math.gcd(SLOTS, 512)
    source_rows = math.gcd(NSTARS, 8192)
    tile_stack = targets.reshape(6, SLOTS // target_rows, target_rows).transpose(1, 0, 2)

    def one_tile(tile_targets):

        def advance(running, index):
            segment = lax.dynamic_slice_in_dim(sources, (index * source_rows).astype(jnp.int32), source_rows, 1)
            return (running + pair_terms(tile_targets, segment), None)
        running, _ = lax.scan(advance, jnp.zeros((6, target_rows), jnp.float32), jnp.arange(NSTARS // source_rows, dtype=jnp.int32))
        return running
    forces = lax.map(one_tile, tile_stack)
    forces = forces.transpose(1, 0, 2).reshape(6, SLOTS)
    forces = jnp.where(live_mask[None, :], forces, 0.0)
    return (forces[0:3], forces[3:6])
```

```python
import functools

import jax
import jax.numpy as jnp
from jax import lax
from jax.experimental import pallas as pl
from jax.experimental.pallas import tpu as pltpu
from jax.sharding import PartitionSpec as P

SOFTENING = 0.0025
MESH = pl.DeviceIdType.MESH
LANES = 128
GROUP = 16
DEVICES = GROUP * GROUP
SLOT_LANES = 16
ACT = 8
STARS = 4096
TILES = STARS // LANES
SLOTS = DEVICES * ACT
ROWS = SLOTS + 16


def place():
    row = lax.axis_index("row")
    col = lax.axis_index("col")
    core = lax.rem(col, 2)
    return row, col, core, lax.div(col, 2), row * 2 + core


def zy_peer(step):
    row, col, core, zy, rc = place()
    peer = lax.rem(zy + step, GROUP)
    return peer, (row, peer * 2 + core)


def rc_peer(step):
    row, col, core, zy, rc = place()
    peer = lax.rem(rc + step, GROUP)
    return peer, (lax.div(peer, 2), zy * 2 + lax.rem(peer, 2))


def greet():
    barrier = pltpu.get_barrier_semaphore()
    for step in range(1, GROUP):
        for peer in (zy_peer, rc_peer):
            pl.semaphore_signal(barrier, inc=1, device_id=peer(step)[1], device_id_type=MESH)


def await_greetings():
    pl.semaphore_wait(pltpu.get_barrier_semaphore(), 2 * (GROUP - 1))


def wait_bytes(ref, sem):
    pltpu.make_async_copy(ref, ref, sem).wait()


def gather_kernel(index_ref, count_ref, pos_ref, vel_ref, acc_ref, jerk_ref, elapsed_ref,
                  p_ref, v_ref, all_ref, offset_ref, mine, send_sem, recv_sem):
    row, col, core, zy, rc = place()
    greet()
    for tile in range(TILES):
        cols = pl.ds(tile * LANES, LANES)
        dt = elapsed_ref[tile:tile + 1, :]
        vel, acc, jerk = vel_ref[:, cols], acc_ref[:, cols], jerk_ref[:, cols]
        p_ref[:, cols] = pos_ref[:, cols] + dt * (vel + dt * (0.5 * acc + dt * (jerk * (1.0 / 6.0))))
        v_ref[:, cols] = vel + dt * (acc + dt * (0.5 * jerk))
    lane = lax.broadcasted_iota(jnp.int32, (3, LANES), 1)
    sub = lax.broadcasted_iota(jnp.int32, (3, LANES), 0)
    total = jnp.zeros((3, LANES), jnp.float32)
    for slot in range(ACT):
        away = lane - index_ref[slot]
        picked = [jnp.zeros((3, LANES), jnp.float32)] * 2
        for tile in range(TILES):
            cols = pl.ds(tile * LANES, LANES)
            hit = away == -tile * LANES
            picked = [jnp.where(hit, ref[:, cols], old) for ref, old in zip((p_ref, v_ref), picked)]
        for first, value in zip((0, 3), picked):
            value = jnp.sum(value, axis=1, keepdims=True)
            lead = (ACT - slot) % ACT * SLOT_LANES + first
            total = total + jnp.where(lane == sub + lead, value, 0.0)
    packed = jnp.sum(total, axis=0, keepdims=True)
    count = count_ref[0].astype(jnp.float32)
    packed = jnp.where(lane[0:1] == 6, count, packed)
    mine[...] = packed
    me = rc * GROUP + zy
    all_ref[pl.ds(me, 1), :] = packed
    await_greetings()
    for step in range(1, GROUP):
        peer, device = zy_peer(step)
        pltpu.make_async_remote_copy(
            src_ref=mine, dst_ref=all_ref.at[pl.ds(me, 1)],
            send_sem=send_sem.at[0], recv_sem=recv_sem.at[0],
            device_id=device, device_id_type=MESH).start()
    wait_bytes(all_ref.at[pl.ds(0, GROUP - 1)], recv_sem.at[0])
    block = all_ref.at[pl.ds(pl.multiple_of(rc * GROUP, GROUP), GROUP)]
    for step in range(1, GROUP):
        peer, device = rc_peer(step)
        pltpu.make_async_remote_copy(
            src_ref=block, dst_ref=block,
            send_sem=send_sem.at[1], recv_sem=recv_sem.at[1],
            device_id=device, device_id_type=MESH).start()
    wait_bytes(all_ref.at[pl.ds(0, GROUP - 1)], send_sem.at[0])
    wait_bytes(all_ref.at[pl.ds(0, (GROUP - 1) * GROUP)], recv_sem.at[1])
    counts = all_ref[...].astype(jnp.bfloat16)
    before = lax.broadcasted_iota(jnp.int32, (DEVICES, DEVICES), 0)
    after = lax.broadcasted_iota(jnp.int32, (DEVICES, DEVICES), 1)
    ahead = jnp.where(before < after, 1.0, 0.0).astype(jnp.bfloat16)
    whole = jnp.where(before >= 0, 1.0, 0.0).astype(jnp.bfloat16)
    column = lax.broadcasted_iota(jnp.int32, (DEVICES, LANES), 1)
    counts = jnp.where(column == 6, all_ref[...], 0.0).astype(jnp.bfloat16)
    dims = (((0,), (0,)), ((), ()))
    starts = lax.dot_general(counts, ahead, dims, preferred_element_type=jnp.float32)
    totals = lax.dot_general(counts, whole, dims, preferred_element_type=jnp.float32)
    offset_ref[0:1, :] = starts[6:7, :].astype(jnp.int32)
    offset_ref[1:2, :] = totals[6:7, :].astype(jnp.int32)
    wait_bytes(all_ref.at[pl.ds(0, (GROUP - 1) * GROUP)], send_sem.at[1])


def force_kernel(offset_ref, p_ref, v_ref, mass_ref, all_ref, out_ref, targets, results):
    live = offset_ref[1, 0]
    targets[...] = jnp.zeros_like(targets)

    def pack(device, carry):
        spread = jnp.broadcast_to(all_ref[pl.ds(device, 1), :], (ACT, LANES))
        spread = pltpu.roll(spread, 0, 1, stride=SLOT_LANES, stride_axis=0)
        targets[pl.ds(offset_ref[0, device], ACT), :] = spread
        return carry

    lax.fori_loop(0, DEVICES, pack, 0, unroll=8)
    lane = lax.broadcasted_iota(jnp.int32, (ACT, LANES), 1)

    def group(index, carry):
        rows = pl.ds(pl.multiple_of(index * ACT, ACT), ACT)
        block = targets[rows, :]
        mine = [jnp.broadcast_to(block[:, f:f + 1], (ACT, LANES)) for f in range(6)]
        sums = [jnp.zeros((ACT, LANES), jnp.float32) for _ in range(9)]
        for tile in range(TILES):
            cols = pl.ds(tile * LANES, LANES)
            dx = [p_ref[f:f + 1, cols] - mine[f] for f in range(3)]
            dv = [v_ref[f:f + 1, cols] - mine[3 + f] for f in range(3)]
            r2 = dx[0] * dx[0] + dx[1] * dx[1] + dx[2] * dx[2] + SOFTENING
            dot = dx[0] * dv[0] + dx[1] * dv[1] + dx[2] * dv[2]
            inv = lax.rsqrt(r2)
            inv2 = inv * inv
            w = mass_ref[tile:tile + 1, :] * inv * inv2
            u = w * (dot * inv2)
            for f in range(3):
                sums[f] = sums[f] + w * dx[f]
                sums[3 + f] = sums[3 + f] + w * dv[f]
                sums[6 + f] = sums[6 + f] + u * dx[f]
        value = jnp.zeros((ACT, LANES), jnp.float32)
        for f in range(3):
            value = jnp.where(lane == f, jnp.sum(sums[f], axis=1, keepdims=True), value)
            both = sums[3 + f] - 3.0 * sums[6 + f]
            value = jnp.where(lane == 3 + f, jnp.sum(both, axis=1, keepdims=True), value)
        results[rows, :] = value
        return carry

    lax.fori_loop(0, lax.div(live + (ACT - 1), ACT), group, 0)
    slot = lax.broadcasted_iota(jnp.int32, (ACT, LANES), 0)
    own = lax.div(lane, SLOT_LANES) == slot

    def unpack(device, carry):
        block = results[pl.ds(offset_ref[0, device], ACT), :]
        block = pltpu.roll(block, 0, 1, stride=SLOT_LANES, stride_axis=0)
        out_ref[pl.ds(device, 1), :] = jnp.sum(jnp.where(own, block, 0.0), axis=0, keepdims=True)
        return carry

    lax.fori_loop(0, DEVICES, unpack, 0, unroll=8)


def scatter_kernel(count_ref, part_ref, accel_ref, jerk_ref, first, second, summed, send_sem, recv_sem):
    row, col, core, zy, rc = place()
    greet()
    await_greetings()
    for step in range(1, GROUP):
        peer, device = rc_peer(step)
        pltpu.make_async_remote_copy(
            src_ref=part_ref.at[pl.ds(pl.multiple_of(peer * GROUP, GROUP), GROUP)],
            dst_ref=first.at[step - 1],
            send_sem=send_sem.at[0], recv_sem=recv_sem.at[0],
            device_id=device, device_id_type=MESH).start()
    total = part_ref[pl.ds(pl.multiple_of(rc * GROUP, GROUP), GROUP), :]
    wait_bytes(first, recv_sem.at[0])
    for step in range(1, GROUP):
        total = total + first[step - 1]
    summed[...] = total
    for step in range(1, GROUP):
        peer, device = zy_peer(step)
        pltpu.make_async_remote_copy(
            src_ref=summed.at[pl.ds(peer, 1)],
            dst_ref=second.at[pl.ds(step - 1, 1)],
            send_sem=send_sem.at[1], recv_sem=recv_sem.at[1],
            device_id=device, device_id_type=MESH).start()
    final = summed[pl.ds(zy, 1), :]
    wait_bytes(second.at[pl.ds(0, GROUP - 1)], recv_sem.at[1])
    final = final + jnp.sum(second[0:GROUP - 1, :], axis=0, keepdims=True)
    sub = lax.broadcasted_iota(jnp.int32, (8, LANES), 0)
    lane = lax.broadcasted_iota(jnp.int32, (8, LANES), 1)
    spread = jnp.where(lax.rem(lane, SLOT_LANES) == sub, jnp.broadcast_to(final, (8, LANES)), 0.0)
    at = lax.broadcasted_iota(jnp.int32, (8, ACT), 1)
    out = jnp.zeros((8, ACT), jnp.float32)
    for s in range(ACT):
        part = jnp.where(lax.div(lane, SLOT_LANES) == s, spread, 0.0)
        out = jnp.where(at == s, jnp.sum(part, axis=1, keepdims=True), out)
    out = jnp.where(at < count_ref[0], out, 0.0)
    accel_ref[...] = out[0:3]
    jerk_ref[...] = out[3:6]
    wait_bytes(first, send_sem.at[0])
    wait_bytes(second.at[pl.ds(0, GROUP - 1)], send_sem.at[1])


def local(position, velocity, accel_old, jerk_old, mass, elapsed, active_index, active_count):
    f32 = jnp.float32
    vmem = pl.BlockSpec(memory_space=pltpu.VMEM)
    smem = pl.BlockSpec(memory_space=pltpu.SMEM)
    pos, vel, everyone, offsets = pl.pallas_call(
        gather_kernel,
        out_shape=(
            jax.ShapeDtypeStruct((3, STARS), f32),
            jax.ShapeDtypeStruct((3, STARS), f32),
            jax.ShapeDtypeStruct((DEVICES, LANES), f32),
            jax.ShapeDtypeStruct((2, DEVICES), jnp.int32),
        ),
        in_specs=[smem, smem] + [vmem] * 5,
        out_specs=(vmem,) * 4,
        scratch_shapes=[
            pltpu.VMEM((1, LANES), f32),
            pltpu.SemaphoreType.DMA((2,)),
            pltpu.SemaphoreType.DMA((2,)),
        ],
        compiler_params=pltpu.CompilerParams(collective_id=0, has_side_effects=True),
        name="gather_targets",
    )(active_index, active_count, position, velocity, accel_old, jerk_old, elapsed.reshape(TILES, LANES))
    parts = pl.pallas_call(
        force_kernel,
        out_shape=jax.ShapeDtypeStruct((DEVICES, LANES), f32),
        in_specs=[smem] + [vmem] * 4,
        out_specs=vmem,
        scratch_shapes=[pltpu.VMEM((ROWS, LANES), f32), pltpu.VMEM((ROWS, LANES), f32)],
        name="forces",
    )(offsets, pos, vel, mass.reshape(TILES, LANES), everyone)
    return pl.pallas_call(
        scatter_kernel,
        out_shape=(jax.ShapeDtypeStruct((3, ACT), f32), jax.ShapeDtypeStruct((3, ACT), f32)),
        in_specs=[smem, vmem],
        out_specs=(vmem, vmem),
        scratch_shapes=[
            pltpu.VMEM((GROUP - 1, GROUP, LANES), f32),
            pltpu.VMEM((GROUP, LANES), f32),
            pltpu.VMEM((GROUP, LANES), f32),
            pltpu.SemaphoreType.DMA((2,)),
            pltpu.SemaphoreType.DMA((2,)),
        ],
        compiler_params=pltpu.CompilerParams(collective_id=1, has_side_effects=True),
        name="scatter_forces",
    )(active_count, parts)


def solution(mesh):
    split = P(None, ("row", "col"))
    flat = P(("row", "col"))
    return jax.shard_map(
        local,
        mesh=mesh,
        in_specs=(split, split, split, split, flat, flat, flat, flat),
        out_specs=(split, split),
        check_vma=False,
    )
```

```python
import functools

import jax
import jax.numpy as jnp
from jax import lax
from jax.experimental import pallas as pl
from jax.experimental.pallas import tpu as pltpu
from jax.sharding import PartitionSpec as P

SOFTENING = 0.0025
MESH = pl.DeviceIdType.MESH
F32, BF16 = jnp.float32, jnp.bfloat16
LANES = 128
GROUP = 16
ACT = 8
STARS = 4096
TILES = STARS // LANES
SLOTS = GROUP * LANES
BLOCK = 256
CHUNK = 2048


def place():
    row = lax.axis_index("row")
    col = lax.axis_index("col")
    core = lax.rem(col, 2)
    return row, col, core, lax.div(col, 2), row * 2 + core


def zy_peer(step):
    row, col, core, zy, rc = place()
    peer = lax.rem(zy + step, GROUP)
    return peer, (row, peer * 2 + core)


def rc_peer(step):
    row, col, core, zy, rc = place()
    peer = lax.rem(rc + step, GROUP)
    return peer, (lax.div(peer, 2), zy * 2 + lax.rem(peer, 2))


def greet():
    barrier = pltpu.get_barrier_semaphore()
    for step in range(1, GROUP):
        for peer in (zy_peer, rc_peer):
            pl.semaphore_signal(barrier, inc=1, device_id=peer(step)[1], device_id_type=MESH)


def await_greetings():
    pl.semaphore_wait(pltpu.get_barrier_semaphore(), 2 * (GROUP - 1))


def wait_bytes(ref, sem):
    pltpu.make_async_copy(ref, ref, sem).wait()


def mm(a, b):
    return jnp.dot(a, b, preferred_element_type=F32)


def mm_t(a, b):
    return lax.dot_general(a, b, (((1,), (1,)), ((), ())), preferred_element_type=F32)


def pieces(value):
    first = value.astype(BF16).astype(F32)
    rest = value - first
    second = rest.astype(BF16).astype(F32)
    return first, second, rest - second


def coordinates(group):
    coarse = jnp.floor(group * 16.0 + 0.5) * 0.0625
    return coarse, pieces(group - coarse)


def scalars(group, coarse, shift):
    sub = lax.broadcasted_iota(jnp.int32, group.shape, 0)
    upper = sub < 3

    def pair(exact, whole):
        exact = jnp.sum(jnp.where(upper, exact, 0.0), axis=0, keepdims=True)
        whole = jnp.sum(jnp.where(upper, whole, 0.0), axis=0, keepdims=True)
        high = exact.astype(BF16).astype(F32)
        return (high, exact - high) + pieces(whole)

    fine = group - coarse
    vel, vel_coarse = pltpu.roll(group, 4, 0), pltpu.roll(coarse, 4, 0)
    square = pair(coarse * coarse, fine * (group + coarse) + jnp.where(sub == 0, shift, 0.0))
    cross = pair(coarse * vel_coarse, fine * vel + coarse * (vel - vel_coarse))
    return square, cross


def stack(rows, shape):
    sub = lax.broadcasted_iota(jnp.int32, shape, 0)
    total = jnp.zeros(shape, F32)
    for at, row in enumerate(rows):
        total = jnp.where(sub == at, row, total)
    return total


def source_features(group):
    coarse, (one, two, three) = coordinates(group)
    square, cross = scalars(group, coarse, 0.0)
    exact = stack(square[0:2] + (1.0, 1.0) + cross[0:2] + (1.0, 1.0), group.shape)
    rest = stack(square[2:5] + (1.0,) + cross[2:5] + (1.0,), group.shape)
    more = stack((1.0, 1.0, 0.0, 0.0, 1.0, 1.0, 0.0, 0.0), group.shape)
    none = jnp.zeros_like(group)
    return [exact, coarse, rest, more, coarse, coarse, coarse, one, two, three, one, one, two, two, none, none]


def target_features(group):
    coarse, (one, two, three) = coordinates(group)
    square, cross = scalars(group, coarse, SOFTENING)
    sub = lax.broadcasted_iota(jnp.int32, group.shape, 0)
    none = jnp.zeros_like(group)

    def tail(scalar, at):
        pad, rest = (0.0,) * at, (0.0,) * (4 - at)
        exact = stack(pad + (1.0, 1.0) + scalar[0:2] + rest, group.shape)
        fine = stack(pad + (1.0, 1.0, 1.0) + scalar[2:3] + rest, group.shape)
        more = stack(pad + scalar[3:5] + (0.0, 0.0) + rest, group.shape)
        return exact, fine, more

    def weights(change, scalar, at):
        exact, fine, more = tail(scalar, at)
        c, o, t, h = change(coarse), change(one), change(two), change(three)
        rows = [exact, c, fine, more, o, t, h, c, c, c, o, t, o, t, none, none]
        return jnp.concatenate(rows, 0).astype(BF16)

    near = weights(lambda v: jnp.where(sub < 3, -2.0 * v, 0.0), square, 0)
    along = weights(lambda v: -pltpu.roll(v, 4, 0), cross, 4)
    return near, along


def prepare_tile(tile, stars, mass_ref, feature_ref, moment_ref):
    cols = pl.ds(pl.multiple_of(tile * LANES, LANES), LANES)
    group = stars[:, cols]
    rows = jnp.concatenate(source_features(group), 0)
    feature_ref[cols, :] = rows.T.astype(BF16)
    sub = lax.broadcasted_iota(jnp.int32, group.shape, 0)
    moment = mass_ref[pl.ds(tile, 1), :] * jnp.where(sub == 3, 1.0, group)
    one, two, three = pieces(moment)
    moment_ref[:, cols] = jnp.concatenate([one, two, three, jnp.zeros_like(one)], 0).astype(BF16)


def gather_kernel(index_ref, count_ref, pos_ref, vel_ref, acc_ref, jerk_ref, mass_ref, elapsed_ref,
                  feature_ref, moment_ref, all_ref, rank_ref, live_ref,
                  stars, mine, near, send_sem, recv_sem):
    row, col, core, zy, rc = place()
    greet()
    stars[...] = jnp.zeros_like(stars)
    for tile in range(TILES):
        cols = pl.ds(tile * LANES, LANES)
        dt = elapsed_ref[tile:tile + 1, :]
        vel, acc, jerk = vel_ref[:, cols], acc_ref[:, cols], jerk_ref[:, cols]
        stars[0:3, cols] = pos_ref[:, cols] + dt * (vel + dt * (0.5 * acc + dt * (jerk * (1.0 / 6.0))))
        stars[4:7, cols] = vel + dt * (acc + dt * (0.5 * jerk))
    lane = lax.broadcasted_iota(jnp.int32, (8, LANES), 1)
    sub = lax.broadcasted_iota(jnp.int32, (8, LANES), 0)
    total = jnp.zeros((8, LANES), F32)
    for slot in range(ACT):
        away = lane - index_ref[slot]
        picked = jnp.zeros((8, LANES), F32)
        for tile in range(TILES):
            picked = jnp.where(away == -tile * LANES, stars[:, pl.ds(tile * LANES, LANES)], picked)
        value = jnp.sum(picked, axis=1, keepdims=True)
        value = jnp.where(sub == 3, jnp.where(slot < count_ref[0], 1.0, 0.0), value)
        total = jnp.where(lane == zy * ACT + slot, value, total)
    mine[...] = total
    await_greetings()
    for step in range(1, GROUP):
        peer, device = zy_peer(step)
        pltpu.make_async_remote_copy(
            src_ref=mine, dst_ref=near.at[step - 1],
            send_sem=send_sem.at[0], recv_sem=recv_sem.at[0],
            device_id=device, device_id_type=MESH).start()

    def prepare(tile, carry):
        prepare_tile(tile, stars, mass_ref, feature_ref, moment_ref)
        return carry

    lax.fori_loop(0, TILES // 2, prepare, 0, unroll=2)
    wait_bytes(near, recv_sem.at[0])
    for step in range(1, GROUP):
        total = total + near[step - 1]
    all_ref[pl.ds(rc, 1)] = total[None]
    for step in range(1, GROUP):
        peer, device = rc_peer(step)
        pltpu.make_async_remote_copy(
            src_ref=all_ref.at[rc], dst_ref=all_ref.at[rc],
            send_sem=send_sem.at[1], recv_sem=recv_sem.at[1],
            device_id=device, device_id_type=MESH).start()
    lax.fori_loop(TILES // 2, TILES, prepare, 0, unroll=2)
    wait_bytes(near, send_sem.at[0])
    wait_bytes(near, recv_sem.at[1])
    alive = jnp.concatenate([all_ref[g, 3:4, :] for g in range(GROUP)], 0)
    before = lax.broadcasted_iota(jnp.int32, (LANES, LANES), 0)
    after = lax.broadcasted_iota(jnp.int32, (LANES, LANES), 1)
    inside = mm(alive.astype(BF16), jnp.where(before < after, 1.0, 0.0).astype(BF16))
    sums = mm(alive.astype(BF16), jnp.ones((LANES, LANES), BF16))
    earlier = jnp.where((after < before) & (after < GROUP), 1.0, 0.0)[0:GROUP, 0:GROUP]
    ahead = mm(earlier.astype(BF16), sums.astype(BF16))
    rank_ref[...] = jnp.where(alive > 0.0, inside + ahead, -1.0)
    live_ref[...] = (ahead + sums)[GROUP - 1:GROUP, :].astype(jnp.int32)
    wait_bytes(near, send_sem.at[1])


def force_kernel(live_ref, feature_ref, moment_ref, all_ref, rank_ref, out_ref, hot):
    out_ref[...] = jnp.zeros_like(out_ref)
    spread = jnp.concatenate([all_ref[g] for g in range(GROUP)], 1)
    slots = jnp.concatenate(list(pieces(spread)) + [jnp.zeros_like(spread)], 0).astype(BF16)
    target = lax.broadcasted_iota(jnp.int32, (BLOCK, LANES), 0).astype(F32)
    sub = lax.broadcasted_iota(jnp.int32, (8, BLOCK), 0)

    def block(index, carry):
        wanted = target + (index * BLOCK).astype(F32)
        for g in range(GROUP):
            hot[:, g * LANES:(g + 1) * LANES] = jnp.where(
                wanted == rank_ref[g:g + 1, :], 1.0, 0.0).astype(BF16)
        packed = mm_t(slots, hot[...])
        packed = packed[0:8] + packed[8:16] + packed[16:24]
        packed = jnp.where((sub == 3) | (sub == 7), 0.0, packed)
        near, along = target_features(packed)

        def chunk(step, sums):
            rows = pl.ds(pl.multiple_of(step * CHUNK, CHUNK), CHUNK)
            r2 = mm(feature_ref[rows, :], near)
            dot = mm(feature_ref[rows, :], along)
            inv = lax.rsqrt(r2)
            inv2 = inv * inv
            w = inv * inv2
            u = (w * inv2) * dot
            moments = moment_ref[:, rows]
            new = []
            for value, old in zip((w, u), sums):
                high = value.astype(BF16)
                low = (value - high.astype(F32)).astype(BF16)
                new.append(old + (mm(moments, high) + mm(moments, low)))
            return tuple(new)

        zero = jnp.zeros((32, BLOCK), F32)
        sums = lax.fori_loop(0, STARS // CHUNK, chunk, (zero, zero))
        first, second = [s[0:8] + s[8:16] + s[16:24] for s in sums]
        first = first - packed * first[3:4, :]
        second = second - packed * second[3:4, :]
        force = first - 3.0 * jnp.where(sub >= 4, pltpu.roll(second, 4, 0), 0.0)
        force = jnp.concatenate(list(pieces(force)) + [jnp.zeros_like(force)], 0).astype(BF16)
        back = mm(force, hot[...])
        back = back[0:8] + back[8:16] + back[16:24]
        for g in range(GROUP):
            out_ref[g] += back[:, g * LANES:(g + 1) * LANES]
        return carry

    lax.fori_loop(0, lax.div(live_ref[0, 0] + (BLOCK - 1), BLOCK), block, 0)


def scatter_kernel(count_ref, part_ref, accel_ref, jerk_ref, first, second, summed, send_sem, recv_sem):
    row, col, core, zy, rc = place()
    greet()
    await_greetings()
    for step in range(1, GROUP):
        peer, device = rc_peer(step)
        pltpu.make_async_remote_copy(
            src_ref=part_ref.at[peer], dst_ref=first.at[step - 1],
            send_sem=send_sem.at[0], recv_sem=recv_sem.at[0],
            device_id=device, device_id_type=MESH).start()
    total = part_ref[rc]
    wait_bytes(first, recv_sem.at[0])
    for step in range(1, GROUP):
        total = total + first[step - 1]
    summed[...] = total
    for step in range(1, GROUP):
        peer, device = zy_peer(step)
        pltpu.make_async_remote_copy(
            src_ref=summed, dst_ref=second.at[step - 1],
            send_sem=send_sem.at[1], recv_sem=recv_sem.at[1],
            device_id=device, device_id_type=MESH).start()
    wait_bytes(second, recv_sem.at[1])
    for step in range(1, GROUP):
        total = total + second[step - 1]
    mine = pltpu.roll(total, lax.rem(LANES - zy * ACT, LANES), 1)
    lane = lax.broadcasted_iota(jnp.int32, (8, LANES), 1)
    mine = jnp.where(lane < count_ref[0], mine, 0.0)
    accel_ref[...] = mine[0:3, 0:ACT]
    jerk_ref[...] = mine[4:7, 0:ACT]
    wait_bytes(first, send_sem.at[0])
    wait_bytes(second, send_sem.at[1])


def local(position, velocity, accel_old, jerk_old, mass, elapsed, active_index, active_count):
    vmem = pl.BlockSpec(memory_space=pltpu.VMEM)
    smem = pl.BlockSpec(memory_space=pltpu.SMEM)
    tiles = (GROUP, 8, LANES)
    features, moments, everyone, rank, live = pl.pallas_call(
        gather_kernel,
        out_shape=(
            jax.ShapeDtypeStruct((STARS, LANES), BF16),
            jax.ShapeDtypeStruct((32, STARS), BF16),
            jax.ShapeDtypeStruct(tiles, F32),
            jax.ShapeDtypeStruct((GROUP, LANES), F32),
            jax.ShapeDtypeStruct((1, LANES), jnp.int32),
        ),
        in_specs=[smem, smem] + [vmem] * 6,
        out_specs=(vmem,) * 5,
        scratch_shapes=[
            pltpu.VMEM((8, STARS), F32),
            pltpu.VMEM((8, LANES), F32),
            pltpu.VMEM((GROUP - 1, 8, LANES), F32),
            pltpu.SemaphoreType.DMA((2,)),
            pltpu.SemaphoreType.DMA((2,)),
        ],
        compiler_params=pltpu.CompilerParams(collective_id=0, has_side_effects=True),
        name="gather_targets",
    )(active_index, active_count, position, velocity, accel_old, jerk_old,
      mass.reshape(TILES, LANES), elapsed.reshape(TILES, LANES))
    parts = pl.pallas_call(
        force_kernel,
        out_shape=jax.ShapeDtypeStruct(tiles, F32),
        in_specs=[smem] + [vmem] * 4,
        out_specs=vmem,
        scratch_shapes=[pltpu.VMEM((BLOCK, SLOTS), BF16)],
        compiler_params=pltpu.CompilerParams(vmem_limit_bytes=40 * 2**20),
        name="forces",
    )(live, features, moments, everyone, rank)
    return pl.pallas_call(
        scatter_kernel,
        out_shape=(jax.ShapeDtypeStruct((3, ACT), F32), jax.ShapeDtypeStruct((3, ACT), F32)),
        in_specs=[smem, vmem],
        out_specs=(vmem, vmem),
        scratch_shapes=[
            pltpu.VMEM((GROUP - 1, 8, LANES), F32),
            pltpu.VMEM((GROUP - 1, 8, LANES), F32),
            pltpu.VMEM((8, LANES), F32),
            pltpu.SemaphoreType.DMA((2,)),
            pltpu.SemaphoreType.DMA((2,)),
        ],
        compiler_params=pltpu.CompilerParams(collective_id=1, has_side_effects=True),
        name="scatter_forces",
    )(active_count, parts)


def solution(mesh):
    split = P(None, ("row", "col"))
    flat = P(("row", "col"))
    return jax.shard_map(
        local,
        mesh=mesh,
        in_specs=(split, split, split, split, flat, flat, flat, flat),
        out_specs=(split, split),
        check_vma=False,
    )
```

```python
import functools

import jax
import jax.numpy as jnp
from jax import lax
from jax.experimental import pallas as pl
from jax.experimental.pallas import tpu as pltpu
from jax.sharding import PartitionSpec as P

SOFTENING = 0.0025
MESH = pl.DeviceIdType.MESH
F32, BF16 = jnp.float32, jnp.bfloat16
LANES = 128
GROUP = 16
ACT = 8
STARS = 4096
TILES = STARS // LANES
SLOTS = GROUP * LANES
BLOCK = 256
CHUNK = 4096
SIZES = (3, 4, 8)


def place():
    row = lax.axis_index("row")
    col = lax.axis_index("col")
    core = lax.rem(col, 2)
    return row, col, core, lax.div(col, 2), row * 2 + core


def zy_peer(step):
    row, col, core, zy, rc = place()
    peer = lax.rem(zy + step, GROUP)
    return peer, (row, peer * 2 + core)


def rc_peer(step):
    row, col, core, zy, rc = place()
    peer = lax.rem(rc + step, GROUP)
    return peer, (lax.div(peer, 2), zy * 2 + lax.rem(peer, 2))


def greet():
    barrier = pltpu.get_barrier_semaphore()
    for step in range(1, GROUP):
        for peer in (zy_peer, rc_peer):
            pl.semaphore_signal(barrier, inc=1, device_id=peer(step)[1], device_id_type=MESH)


def await_greetings():
    pl.semaphore_wait(pltpu.get_barrier_semaphore(), 2 * (GROUP - 1))


def wait_bytes(ref, sem):
    pltpu.make_async_copy(ref, ref, sem).wait()


def mm(a, b):
    return jnp.dot(a, b, preferred_element_type=F32)


def mm_t(a, b):
    return lax.dot_general(a, b, (((1,), (1,)), ((), ())), preferred_element_type=F32)


def pieces(value):
    first = value.astype(BF16).astype(F32)
    rest = value - first
    second = rest.astype(BF16).astype(F32)
    return first, second, rest - second


def coordinates(group):
    coarse = jnp.floor(group * 16.0 + 0.5) * 0.0625
    return coarse, pieces(group - coarse)


def scalars(group, coarse, shift):
    sub = lax.broadcasted_iota(jnp.int32, group.shape, 0)
    upper = sub < 3

    def pair(exact, whole):
        exact = jnp.sum(jnp.where(upper, exact, 0.0), axis=0, keepdims=True)
        whole = jnp.sum(jnp.where(upper, whole, 0.0), axis=0, keepdims=True)
        high = exact.astype(BF16).astype(F32)
        return (high, exact - high) + pieces(whole)

    fine = group - coarse
    vel, vel_coarse = pltpu.roll(group, 4, 0), pltpu.roll(coarse, 4, 0)
    square = pair(coarse * coarse, fine * (group + coarse) + jnp.where(sub == 0, shift, 0.0))
    cross = pair(coarse * vel_coarse, fine * vel + coarse * (vel - vel_coarse))
    return square, cross


def stack(rows, shape):
    sub = lax.broadcasted_iota(jnp.int32, shape, 0)
    total = jnp.zeros(shape, F32)
    for at, row in enumerate(rows):
        total = jnp.where(sub == at, row, total)
    return total


def source_features(group):
    coarse, (one, two, three) = coordinates(group)
    square, cross = scalars(group, coarse, 0.0)
    exact = stack(square[0:2] + (1.0, 1.0) + cross[0:2] + (1.0, 1.0), group.shape)
    rest = stack(square[2:5] + (1.0,) + cross[2:5] + (1.0,), group.shape)
    more = stack((1.0, 1.0, 0.0, 0.0, 1.0, 1.0, 0.0, 0.0), group.shape)
    none = jnp.zeros_like(group)
    return [exact, coarse, rest, more, coarse, coarse, coarse, one, two, three, one, one, two, two, none, none]


def target_features(group):
    coarse, (one, two, three) = coordinates(group)
    square, cross = scalars(group, coarse, SOFTENING)
    sub = lax.broadcasted_iota(jnp.int32, group.shape, 0)
    none = jnp.zeros_like(group)

    def tail(scalar, at):
        pad, rest = (0.0,) * at, (0.0,) * (4 - at)
        exact = stack(pad + (1.0, 1.0) + scalar[0:2] + rest, group.shape)
        fine = stack(pad + (1.0, 1.0, 1.0) + scalar[2:3] + rest, group.shape)
        more = stack(pad + scalar[3:5] + (0.0, 0.0) + rest, group.shape)
        return exact, fine, more

    def weights(change, scalar, at):
        exact, fine, more = tail(scalar, at)
        c, o, t, h = change(coarse), change(one), change(two), change(three)
        rows = [exact, c, fine, more, o, t, h, c, c, c, o, t, o, t, none, none]
        return jnp.concatenate(rows, 0).astype(BF16)

    near = weights(lambda v: jnp.where(sub < 3, -2.0 * v, 0.0), square, 0)
    along = weights(lambda v: -pltpu.roll(v, 4, 0), cross, 4)
    return near, along


def prepare_tile(tile, stars, mass_ref, feature_ref, moment_ref):
    cols = pl.ds(pl.multiple_of(tile * LANES, LANES), LANES)
    group = stars[:, cols]
    rows = jnp.concatenate(source_features(group), 0)
    feature_ref[cols, :] = rows.T.astype(BF16)
    sub = lax.broadcasted_iota(jnp.int32, group.shape, 0)
    moment = mass_ref[pl.ds(tile, 1), :] * jnp.where(sub == 3, 1.0, group)
    one, two, three = pieces(moment)
    moment_ref[:, cols] = jnp.concatenate([one, two, three, jnp.zeros_like(one)], 0).astype(BF16)


def gather_kernel(index_ref, count_ref, pos_hbm, vel_hbm, acc_hbm, jerk_hbm, mass_hbm, elapsed_hbm,
                  feature_ref, moment_ref, all_ref, rank_ref, choice_ref,
                  pos_ref, vel_ref, acc_ref, jerk_ref, mass_ref, elapsed_ref,
                  stars, mine, near, load_sem, send_sem, recv_sem):
    loads = [
        pltpu.make_async_copy(src, dst, load_sem.at[at])
        for at, (src, dst) in enumerate((
            (pos_hbm, pos_ref), (vel_hbm, vel_ref), (acc_hbm, acc_ref), (jerk_hbm, jerk_ref),
            (mass_hbm, mass_ref), (elapsed_hbm, elapsed_ref)))
    ]
    for load in loads:
        load.start()
    row, col, core, zy, rc = place()
    greet()
    for load in loads:
        load.wait()
    stars[...] = jnp.zeros_like(stars)
    for tile in range(TILES):
        cols = pl.ds(tile * LANES, LANES)
        dt = elapsed_ref[tile:tile + 1, :]
        vel, acc, jerk = vel_ref[:, cols], acc_ref[:, cols], jerk_ref[:, cols]
        stars[0:3, cols] = pos_ref[:, cols] + dt * (vel + dt * (0.5 * acc + dt * (jerk * (1.0 / 6.0))))
        stars[4:7, cols] = vel + dt * (acc + dt * (0.5 * jerk))
    lane = lax.broadcasted_iota(jnp.int32, (8, LANES), 1)
    sub = lax.broadcasted_iota(jnp.int32, (8, LANES), 0)
    total = jnp.zeros((8, LANES), F32)
    for slot in range(ACT):
        away = lane - index_ref[slot]
        picked = jnp.zeros((8, LANES), F32)
        for tile in range(TILES):
            picked = jnp.where(away == -tile * LANES, stars[:, pl.ds(tile * LANES, LANES)], picked)
        value = jnp.sum(picked, axis=1, keepdims=True)
        value = jnp.where(sub == 3, jnp.where(slot < count_ref[0], 1.0, 0.0), value)
        total = jnp.where(lane == zy * ACT + slot, value, total)
    mine[...] = total
    await_greetings()
    for step in range(1, GROUP):
        peer, device = zy_peer(step)
        pltpu.make_async_remote_copy(
            src_ref=mine, dst_ref=near.at[step - 1],
            send_sem=send_sem.at[0], recv_sem=recv_sem.at[0],
            device_id=device, device_id_type=MESH).start()

    def prepare(tile, carry):
        prepare_tile(tile, stars, mass_ref, feature_ref, moment_ref)
        return carry

    lax.fori_loop(0, TILES // 2, prepare, 0, unroll=2)
    wait_bytes(near, recv_sem.at[0])
    for step in range(1, GROUP):
        total = total + near[step - 1]
    all_ref[pl.ds(rc, 1)] = total[None]
    for step in range(1, GROUP):
        peer, device = rc_peer(step)
        pltpu.make_async_remote_copy(
            src_ref=all_ref.at[rc], dst_ref=all_ref.at[rc],
            send_sem=send_sem.at[1], recv_sem=recv_sem.at[1],
            device_id=device, device_id_type=MESH).start()
    lax.fori_loop(TILES // 2, TILES, prepare, 0, unroll=2)
    wait_bytes(near, send_sem.at[0])
    wait_bytes(near, recv_sem.at[1])
    alive = jnp.concatenate([all_ref[g, 3:4, :] for g in range(GROUP)], 0)
    before = lax.broadcasted_iota(jnp.int32, (LANES, LANES), 0)
    after = lax.broadcasted_iota(jnp.int32, (LANES, LANES), 1)
    inside = mm(alive.astype(BF16), jnp.where(before < after, 1.0, 0.0).astype(BF16))
    sums = mm(alive.astype(BF16), jnp.ones((LANES, LANES), BF16))
    earlier = jnp.where((after < before) & (after < GROUP), 1.0, 0.0)[0:GROUP, 0:GROUP]
    ahead = mm(earlier.astype(BF16), sums.astype(BF16))
    rank_ref[...] = jnp.where(alive > 0.0, inside + ahead, -1.0)
    live = (ahead + sums)[GROUP - 1, 0].astype(jnp.int32)
    choice_ref[0] = sum((live > BLOCK * size).astype(jnp.int32) for size in SIZES[:-1])
    wait_bytes(near, send_sem.at[1])


def force_kernel(blocks, count_ref, feature_ref, moment_ref, all_ref, rank_ref, out_ref,
                 part_ref, hot, first, second, summed, send_sem, recv_sem):
    greet()
    part_ref[...] = jnp.zeros_like(part_ref)
    spread = jnp.concatenate([all_ref[g] for g in range(GROUP)], 1)
    slots = jnp.concatenate(list(pieces(spread)) + [jnp.zeros_like(spread)], 0).astype(BF16)
    target = lax.broadcasted_iota(jnp.int32, (BLOCK, LANES), 0).astype(F32)
    sub = lax.broadcasted_iota(jnp.int32, (8, BLOCK), 0)

    def block(index, carry):
        wanted = target + lax.convert_element_type(index * BLOCK, F32)
        for g in range(GROUP):
            hot[:, g * LANES:(g + 1) * LANES] = jnp.where(
                wanted == rank_ref[g:g + 1, :], 1.0, 0.0).astype(BF16)
        packed = mm_t(slots, hot[...])
        packed = packed[0:8] + packed[8:16] + packed[16:24]
        packed = jnp.where((sub == 3) | (sub == 7), 0.0, packed)
        near, along = target_features(packed)

        def chunk(step, sums):
            rows = pl.ds(pl.multiple_of(step * CHUNK, CHUNK), CHUNK)
            r2 = mm(feature_ref[rows, :], near)
            dot = mm(feature_ref[rows, :], along)
            inv = lax.rsqrt(r2)
            inv2 = inv * inv
            w = inv * inv2
            u = (w * inv2) * dot
            moments = moment_ref[:, rows]
            new = []
            for value, old in zip((w, u), sums):
                high = value.astype(BF16)
                low = (value - high.astype(F32)).astype(BF16)
                new.append(old + (mm(moments, high) + mm(moments, low)))
            return tuple(new)

        zero = jnp.zeros((32, BLOCK), F32)
        sums = chunk(0, (zero, zero))
        by_w, by_u = [s[0:8] + s[8:16] + s[16:24] for s in sums]
        by_w = by_w - packed * by_w[3:4, :]
        by_u = by_u - packed * by_u[3:4, :]
        force = by_w - 3.0 * jnp.where(sub >= 4, pltpu.roll(by_u, 4, 0), 0.0)
        force = jnp.concatenate(list(pieces(force)) + [jnp.zeros_like(force)], 0).astype(BF16)
        back = mm(force, hot[...])
        back = back[0:8] + back[8:16] + back[16:24]
        for g in range(GROUP):
            part_ref[g] += back[:, g * LANES:(g + 1) * LANES]
        return carry

    lax.fori_loop(0, blocks, block, 0)
    row, col, core, zy, rc = place()
    await_greetings()
    for step in range(1, GROUP):
        peer, device = rc_peer(step)
        pltpu.make_async_remote_copy(
            src_ref=part_ref.at[peer], dst_ref=first.at[step - 1],
            send_sem=send_sem.at[0], recv_sem=recv_sem.at[0],
            device_id=device, device_id_type=MESH).start()
    total = part_ref[rc]
    wait_bytes(first, recv_sem.at[0])
    for step in range(1, GROUP):
        total = total + first[step - 1]
    summed[...] = total
    for step in range(1, GROUP):
        peer, device = zy_peer(step)
        pltpu.make_async_remote_copy(
            src_ref=summed, dst_ref=second.at[step - 1],
            send_sem=send_sem.at[1], recv_sem=recv_sem.at[1],
            device_id=device, device_id_type=MESH).start()
    wait_bytes(second, recv_sem.at[1])
    for step in range(1, GROUP):
        total = total + second[step - 1]
    mine = pltpu.roll(total, lax.rem(LANES - zy * ACT, LANES), 1)
    lane = lax.broadcasted_iota(jnp.int32, (8, LANES), 1)
    out_ref[...] = jnp.where(lane < count_ref[0], mine, 0.0)
    wait_bytes(first, send_sem.at[0])
    wait_bytes(second, send_sem.at[1])


def finish_kernel(force_ref, accel_ref, jerk_ref):
    accel_ref[...] = force_ref[0:3, 0:ACT]
    jerk_ref[...] = force_ref[4:7, 0:ACT]


def local(position, velocity, accel_old, jerk_old, mass, elapsed, active_index, active_count):
    vmem = pl.BlockSpec(memory_space=pltpu.VMEM)
    smem = pl.BlockSpec(memory_space=pltpu.SMEM)
    hbm = pl.BlockSpec(memory_space=pltpu.HBM)
    tiles = (GROUP, 8, LANES)
    features, moments, everyone, rank, choice = pl.pallas_call(
        gather_kernel,
        out_shape=(
            jax.ShapeDtypeStruct((STARS, LANES), BF16),
            jax.ShapeDtypeStruct((32, STARS), BF16),
            jax.ShapeDtypeStruct(tiles, F32),
            jax.ShapeDtypeStruct((GROUP, LANES), F32),
            jax.ShapeDtypeStruct((1,), jnp.int32),
        ),
        in_specs=[smem, smem] + [hbm] * 6,
        out_specs=(vmem,) * 4 + (smem,),
        scratch_shapes=[pltpu.VMEM((3, STARS), F32)] * 4 + [pltpu.VMEM((TILES, LANES), F32)] * 2 + [
            pltpu.VMEM((8, STARS), F32),
            pltpu.VMEM((8, LANES), F32),
            pltpu.VMEM((GROUP - 1, 8, LANES), F32),
            pltpu.SemaphoreType.DMA((6,)),
            pltpu.SemaphoreType.DMA((2,)),
            pltpu.SemaphoreType.DMA((2,)),
        ],
        compiler_params=pltpu.CompilerParams(
            collective_id=0, has_side_effects=True, vmem_limit_bytes=8 * 2**20),
        name="gather_targets",
    )(active_index, active_count, position, velocity, accel_old, jerk_old,
      mass.reshape(TILES, LANES), elapsed.reshape(TILES, LANES))

    def forces(at):
        return pl.pallas_call(
            functools.partial(force_kernel, SIZES[at]),
            out_shape=jax.ShapeDtypeStruct((8, LANES), F32),
            in_specs=[smem] + [vmem] * 4,
            out_specs=vmem,
            scratch_shapes=[
                pltpu.VMEM(tiles, F32),
                pltpu.VMEM((BLOCK, SLOTS), BF16),
                pltpu.VMEM((GROUP - 1, 8, LANES), F32),
                pltpu.VMEM((GROUP - 1, 8, LANES), F32),
                pltpu.VMEM((8, LANES), F32),
                pltpu.SemaphoreType.DMA((2,)),
                pltpu.SemaphoreType.DMA((2,)),
            ],
            compiler_params=pltpu.CompilerParams(
                collective_id=1 + at, has_side_effects=True, vmem_limit_bytes=24 * 2**20),
            name="forces_%d" % SIZES[at],
        )

    branches = [forces(at) for at in range(len(SIZES))]
    mine = lax.switch(choice[0], branches, active_count, features, moments, everyone, rank)
    return pl.pallas_call(
        finish_kernel,
        out_shape=(jax.ShapeDtypeStruct((3, ACT), F32), jax.ShapeDtypeStruct((3, ACT), F32)),
        in_specs=[vmem],
        out_specs=(vmem, vmem),
        name="finish",
    )(mine)


def solution(mesh):
    split = P(None, ("row", "col"))
    flat = P(("row", "col"))
    return jax.shard_map(
        local,
        mesh=mesh,
        in_specs=(split, split, split, split, flat, flat, flat, flat),
        out_specs=(split, split),
        check_vma=False,
    )
```

```python
import functools

import jax
import jax.numpy as jnp
from jax import lax
from jax.experimental import pallas as pl
from jax.experimental.pallas import tpu as pltpu
from jax.sharding import PartitionSpec as P

SOFTENING = 0.0025
MESH = pl.DeviceIdType.MESH
F32, BF16 = jnp.float32, jnp.bfloat16
LANES = 128
GROUP = 16
ACT = 8
STARS = 4096
TILES = STARS // LANES
BLOCK = 256
SIZES = (3, 4, 8)


def place():
    row = lax.axis_index("row")
    col = lax.axis_index("col")
    core = lax.rem(col, 2)
    return row, col, core, lax.div(col, 2), row * 2 + core


def zy_peer(step):
    row, col, core, zy, rc = place()
    peer = lax.rem(zy + step, GROUP)
    return peer, (row, peer * 2 + core)


def rc_peer(step):
    row, col, core, zy, rc = place()
    peer = lax.rem(rc + step, GROUP)
    return peer, (lax.div(peer, 2), zy * 2 + lax.rem(peer, 2))


def greet():
    barrier = pltpu.get_barrier_semaphore()
    for step in range(1, GROUP):
        for peer in (zy_peer, rc_peer):
            pl.semaphore_signal(barrier, inc=1, device_id=peer(step)[1], device_id_type=MESH)


def await_greetings():
    pl.semaphore_wait(pltpu.get_barrier_semaphore(), 2 * (GROUP - 1))


def wait_bytes(ref, sem):
    pltpu.make_async_copy(ref, ref, sem).wait()


def mm(a, b):
    return jnp.dot(a, b, preferred_element_type=F32)


def mm_t(a, b):
    return lax.dot_general(a, b, (((1,), (1,)), ((), ())), preferred_element_type=F32)


def pieces(value):
    first = value.astype(BF16).astype(F32)
    rest = value - first
    second = rest.astype(BF16).astype(F32)
    return first, second, rest - second


def coordinates(group):
    coarse = jnp.floor(group * 16.0 + 0.5) * 0.0625
    return coarse, pieces(group - coarse)


def scalars(group, coarse, shift):
    sub = lax.broadcasted_iota(jnp.int32, group.shape, 0)
    upper = sub < 3

    def pair(exact, whole):
        exact = jnp.sum(jnp.where(upper, exact, 0.0), axis=0, keepdims=True)
        whole = jnp.sum(jnp.where(upper, whole, 0.0), axis=0, keepdims=True)
        high = exact.astype(BF16).astype(F32)
        return (high, exact - high) + pieces(whole)

    fine = group - coarse
    vel, vel_coarse = pltpu.roll(group, 4, 0), pltpu.roll(coarse, 4, 0)
    square = pair(coarse * coarse, fine * (group + coarse) + jnp.where(sub == 0, shift, 0.0))
    cross = pair(coarse * vel_coarse, fine * vel + coarse * (vel - vel_coarse))
    return square, cross


def stack(rows, shape):
    sub = lax.broadcasted_iota(jnp.int32, shape, 0)
    total = jnp.zeros(shape, F32)
    for at, row in enumerate(rows):
        total = jnp.where(sub == at, row, total)
    return total


def source_features(group):
    coarse, (one, two, three) = coordinates(group)
    square, cross = scalars(group, coarse, 0.0)
    exact = stack(square[0:2] + (1.0, 1.0) + cross[0:2] + (1.0, 1.0), group.shape)
    rest = stack(square[2:5] + (1.0,) + cross[2:5] + (1.0,), group.shape)
    more = stack((1.0, 1.0, 0.0, 0.0, 1.0, 1.0, 0.0, 0.0), group.shape)
    none = jnp.zeros_like(group)
    return [exact, coarse, rest, more, coarse, coarse, coarse, one, two, three, one, one, two, two, none, none]


def target_features(group):
    coarse, (one, two, three) = coordinates(group)
    square, cross = scalars(group, coarse, SOFTENING)
    sub = lax.broadcasted_iota(jnp.int32, group.shape, 0)
    none = jnp.zeros_like(group)

    def tail(scalar, at):
        pad, rest = (0.0,) * at, (0.0,) * (4 - at)
        exact = stack(pad + (1.0, 1.0) + scalar[0:2] + rest, group.shape)
        fine = stack(pad + (1.0, 1.0, 1.0) + scalar[2:3] + rest, group.shape)
        more = stack(pad + scalar[3:5] + (0.0, 0.0) + rest, group.shape)
        return exact, fine, more

    def weights(change, scalar, at):
        exact, fine, more = tail(scalar, at)
        c, o, t, h = change(coarse), change(one), change(two), change(three)
        rows = [exact, c, fine, more, o, t, h, c, c, c, o, t, o, t, none, none]
        return jnp.concatenate(rows, 0).astype(BF16)

    near = weights(lambda v: jnp.where(sub < 3, -2.0 * v, 0.0), square, 0)
    along = weights(lambda v: -pltpu.roll(v, 4, 0), cross, 4)
    return near, along


def prepare_tile(tile, stars, mass_ref, feature_ref, moment_ref):
    cols = pl.ds(pl.multiple_of(tile * LANES, LANES), LANES)
    group = stars[:, cols]
    rows = jnp.concatenate(source_features(group), 0)
    feature_ref[cols, :] = rows.T.astype(BF16)
    sub = lax.broadcasted_iota(jnp.int32, group.shape, 0)
    moment = mass_ref[pl.ds(tile, 1), :] * jnp.where(sub == 3, 1.0, group)
    one, two, three = pieces(moment)
    moment_ref[:, cols] = jnp.concatenate([one, two, three, jnp.zeros_like(one)], 0).astype(BF16)


def gather_kernel(index_ref, count_ref, pos_hbm, vel_hbm, acc_hbm, jerk_hbm, mass_hbm, elapsed_hbm,
                  feature_ref, moment_ref, all_ref, rank_ref, choice_ref,
                  pos_ref, vel_ref, acc_ref, jerk_ref, mass_ref, elapsed_ref,
                  stars, mine, near, load_sem, send_sem, recv_sem):
    loads = [
        pltpu.make_async_copy(src, dst, load_sem.at[at])
        for at, (src, dst) in enumerate((
            (pos_hbm, pos_ref), (vel_hbm, vel_ref), (acc_hbm, acc_ref), (jerk_hbm, jerk_ref),
            (mass_hbm, mass_ref), (elapsed_hbm, elapsed_ref)))
    ]
    for load in loads:
        load.start()
    row, col, core, zy, rc = place()
    greet()
    for load in loads:
        load.wait()
    stars[...] = jnp.zeros_like(stars)
    for tile in range(TILES):
        cols = pl.ds(tile * LANES, LANES)
        dt = elapsed_ref[tile:tile + 1, :]
        vel, acc, jerk = vel_ref[:, cols], acc_ref[:, cols], jerk_ref[:, cols]
        stars[0:3, cols] = pos_ref[:, cols] + dt * (vel + dt * (0.5 * acc + dt * (jerk * (1.0 / 6.0))))
        stars[4:7, cols] = vel + dt * (acc + dt * (0.5 * jerk))
    lane = lax.broadcasted_iota(jnp.int32, (8, LANES), 1)
    sub = lax.broadcasted_iota(jnp.int32, (8, LANES), 0)
    total = jnp.zeros((8, LANES), F32)
    for slot in range(ACT):
        away = lane - index_ref[slot]
        picked = jnp.zeros((8, LANES), F32)
        for tile in range(TILES):
            picked = jnp.where(away == -tile * LANES, stars[:, pl.ds(tile * LANES, LANES)], picked)
        value = jnp.sum(picked, axis=1, keepdims=True)
        value = jnp.where(sub == 3, jnp.where(slot < count_ref[0], 1.0, 0.0), value)
        total = jnp.where(lane == zy * ACT + slot, value, total)
    mine[...] = total
    await_greetings()
    for step in range(1, GROUP):
        peer, device = zy_peer(step)
        pltpu.make_async_remote_copy(
            src_ref=mine, dst_ref=near.at[step - 1],
            send_sem=send_sem.at[0], recv_sem=recv_sem.at[0],
            device_id=device, device_id_type=MESH).start()

    def prepare(tile, carry):
        prepare_tile(tile, stars, mass_ref, feature_ref, moment_ref)
        return carry

    lax.fori_loop(0, TILES // 2, prepare, 0, unroll=2)
    wait_bytes(near, recv_sem.at[0])
    for step in range(1, GROUP):
        total = total + near[step - 1]
    all_ref[pl.ds(rc, 1)] = total[None]
    for step in range(1, GROUP):
        peer, device = rc_peer(step)
        pltpu.make_async_remote_copy(
            src_ref=all_ref.at[rc], dst_ref=all_ref.at[rc],
            send_sem=send_sem.at[1], recv_sem=recv_sem.at[1],
            device_id=device, device_id_type=MESH).start()
    lax.fori_loop(TILES // 2, TILES, prepare, 0, unroll=2)
    wait_bytes(near, send_sem.at[0])
    wait_bytes(near, recv_sem.at[1])
    alive = jnp.concatenate([all_ref[g, 3:4, :] for g in range(GROUP)], 0)
    before = lax.broadcasted_iota(jnp.int32, (LANES, LANES), 0)
    after = lax.broadcasted_iota(jnp.int32, (LANES, LANES), 1)
    inside = mm(alive.astype(BF16), jnp.where(before < after, 1.0, 0.0).astype(BF16))
    sums = mm(alive.astype(BF16), jnp.ones((LANES, LANES), BF16))
    earlier = jnp.where((after < before) & (after < GROUP), 1.0, 0.0)[0:GROUP, 0:GROUP]
    ahead = mm(earlier.astype(BF16), sums.astype(BF16))
    first = ahead - LANES * jnp.floor(ahead * (1.0 / LANES))
    lead = inside + first
    rank_ref[0] = jnp.where(alive > 0.0, lead - LANES * jnp.floor(lead * (1.0 / LANES)), -1.0)
    spot = lax.broadcasted_iota(jnp.int32, (GROUP, LANES), 1).astype(F32)
    rank_ref[1] = jnp.floor(ahead * (1.0 / LANES)) + jnp.where(spot < first, 1.0, 0.0)
    live = (ahead + sums)[GROUP - 1, 0].astype(jnp.int32)
    choice_ref[0] = sum((live > BLOCK * size).astype(jnp.int32) for size in SIZES[:-1])
    wait_bytes(near, send_sem.at[1])


def three_rows(group):
    return jnp.concatenate(list(pieces(group)) + [jnp.zeros_like(group)], 0).astype(BF16)


def joined(rows):
    return rows[0:8] + rows[8:16] + rows[16:24]


def force_kernel(blocks, count_ref, feature_ref, moment_ref, all_ref, rank_ref, out_ref,
                 part_ref, hot, near_ref, along_ref, target_ref, force_ref,
                 first, second, summed, send_sem, recv_sem):
    greet()
    tiles = blocks * BLOCK // LANES
    spot = lax.broadcasted_iota(jnp.int32, (LANES, LANES), 0).astype(F32)
    packed = [jnp.zeros((8, LANES), F32)] * tiles
    for g in range(GROUP):
        hot[g] = jnp.where(spot == rank_ref[0, g:g + 1, :], 1.0, 0.0).astype(BF16)
        chosen = joined(mm_t(three_rows(all_ref[g]), hot[g]))
        tile = rank_ref[1, g:g + 1, :]
        packed = [old + jnp.where(tile == at, chosen, 0.0) for at, old in enumerate(packed)]
    row_id = lax.broadcasted_iota(jnp.int32, (8, LANES), 0)
    for at in range(tiles):
        cols = pl.ds(at * LANES, LANES)
        target = jnp.where((row_id == 3) | (row_id == 7), 0.0, packed[at])
        target_ref[:, cols] = target
        near_ref[:, cols], along_ref[:, cols] = target_features(target)
    sub = lax.broadcasted_iota(jnp.int32, (8, BLOCK), 0)

    def block(index, carry):
        cols = pl.ds(pl.multiple_of(index * BLOCK, BLOCK), BLOCK)
        r2 = mm(feature_ref[...], near_ref[:, cols])
        dot = mm(feature_ref[...], along_ref[:, cols])
        inv = lax.rsqrt(r2)
        inv2 = inv * inv
        w = inv * inv2
        u = (w * inv2) * dot
        sums = []
        for value in (w, u):
            high = value.astype(BF16)
            low = (value - high.astype(F32)).astype(BF16)
            sums.append(joined(mm(moment_ref[...], high) + mm(moment_ref[...], low)))
        target = target_ref[:, cols]
        by_w, by_u = [total - target * total[3:4, :] for total in sums]
        force_ref[:, cols] = by_w - 3.0 * jnp.where(sub >= 4, pltpu.roll(by_u, 4, 0), 0.0)
        return carry

    lax.fori_loop(0, blocks, block, 0)
    for g in range(GROUP):
        tile = rank_ref[1, g:g + 1, :]
        chosen = jnp.zeros((8, LANES), F32)
        for at in range(tiles):
            chosen = jnp.where(tile == at, force_ref[:, at * LANES:(at + 1) * LANES], chosen)
        part_ref[g] = joined(mm(three_rows(chosen), hot[g]))
    row, col, core, zy, rc = place()
    await_greetings()
    for step in range(1, GROUP):
        peer, device = rc_peer(step)
        pltpu.make_async_remote_copy(
            src_ref=part_ref.at[peer], dst_ref=first.at[step - 1],
            send_sem=send_sem.at[0], recv_sem=recv_sem.at[0],
            device_id=device, device_id_type=MESH).start()
    total = part_ref[rc]
    wait_bytes(first, recv_sem.at[0])
    for step in range(1, GROUP):
        total = total + first[step - 1]
    summed[...] = total
    for step in range(1, GROUP):
        peer, device = zy_peer(step)
        pltpu.make_async_remote_copy(
            src_ref=summed, dst_ref=second.at[step - 1],
            send_sem=send_sem.at[1], recv_sem=recv_sem.at[1],
            device_id=device, device_id_type=MESH).start()
    wait_bytes(second, recv_sem.at[1])
    for step in range(1, GROUP):
        total = total + second[step - 1]
    mine = pltpu.roll(total, lax.rem(LANES - zy * ACT, LANES), 1)
    lane = lax.broadcasted_iota(jnp.int32, (8, LANES), 1)
    out_ref[...] = jnp.where(lane < count_ref[0], mine, 0.0)
    wait_bytes(first, send_sem.at[0])
    wait_bytes(second, send_sem.at[1])


def finish_kernel(force_ref, accel_ref, jerk_ref):
    accel_ref[...] = force_ref[0:3, 0:ACT]
    jerk_ref[...] = force_ref[4:7, 0:ACT]


def local(position, velocity, accel_old, jerk_old, mass, elapsed, active_index, active_count):
    vmem = pl.BlockSpec(memory_space=pltpu.VMEM)
    smem = pl.BlockSpec(memory_space=pltpu.SMEM)
    hbm = pl.BlockSpec(memory_space=pltpu.HBM)
    tiles = (GROUP, 8, LANES)
    features, moments, everyone, rank, choice = pl.pallas_call(
        gather_kernel,
        out_shape=(
            jax.ShapeDtypeStruct((STARS, LANES), BF16),
            jax.ShapeDtypeStruct((32, STARS), BF16),
            jax.ShapeDtypeStruct(tiles, F32),
            jax.ShapeDtypeStruct((2, GROUP, LANES), F32),
            jax.ShapeDtypeStruct((1,), jnp.int32),
        ),
        in_specs=[smem, smem] + [hbm] * 6,
        out_specs=(vmem,) * 4 + (smem,),
        scratch_shapes=[pltpu.VMEM((3, STARS), F32)] * 4 + [pltpu.VMEM((TILES, LANES), F32)] * 2 + [
            pltpu.VMEM((8, STARS), F32),
            pltpu.VMEM((8, LANES), F32),
            pltpu.VMEM((GROUP - 1, 8, LANES), F32),
            pltpu.SemaphoreType.DMA((6,)),
            pltpu.SemaphoreType.DMA((2,)),
            pltpu.SemaphoreType.DMA((2,)),
        ],
        compiler_params=pltpu.CompilerParams(
            collective_id=0, has_side_effects=True, vmem_limit_bytes=56 * 2**20),
        name="gather_targets",
    )(active_index, active_count, position, velocity, accel_old, jerk_old,
      mass.reshape(TILES, LANES), elapsed.reshape(TILES, LANES))

    def forces(at):
        return pl.pallas_call(
            functools.partial(force_kernel, SIZES[at]),
            out_shape=jax.ShapeDtypeStruct((8, LANES), F32),
            in_specs=[smem] + [vmem] * 4,
            out_specs=vmem,
            scratch_shapes=[
                pltpu.VMEM(tiles, F32),
                pltpu.VMEM((GROUP, LANES, LANES), BF16),
                pltpu.VMEM((LANES, SIZES[at] * BLOCK), BF16),
                pltpu.VMEM((LANES, SIZES[at] * BLOCK), BF16),
                pltpu.VMEM((8, SIZES[at] * BLOCK), F32),
                pltpu.VMEM((8, SIZES[at] * BLOCK), F32),
                pltpu.VMEM((GROUP - 1, 8, LANES), F32),
                pltpu.VMEM((GROUP - 1, 8, LANES), F32),
                pltpu.VMEM((8, LANES), F32),
                pltpu.SemaphoreType.DMA((2,)),
                pltpu.SemaphoreType.DMA((2,)),
            ],
            compiler_params=pltpu.CompilerParams(
                collective_id=1 + at, has_side_effects=True, vmem_limit_bytes=24 * 2**20),
            name="forces_%d" % SIZES[at],
        )

    branches = [forces(at) for at in range(len(SIZES))]
    mine = lax.switch(choice[0], branches, active_count, features, moments, everyone, rank)
    return pl.pallas_call(
        finish_kernel,
        out_shape=(jax.ShapeDtypeStruct((3, ACT), F32), jax.ShapeDtypeStruct((3, ACT), F32)),
        in_specs=[vmem],
        out_specs=(vmem, vmem),
        name="finish",
    )(mine)


def solution(mesh):
    split = P(None, ("row", "col"))
    flat = P(("row", "col"))
    return jax.shard_map(
        local,
        mesh=mesh,
        in_specs=(split, split, split, split, flat, flat, flat, flat),
        out_specs=(split, split),
        check_vma=False,
    )
```

```python
import functools

import jax
import jax.numpy as jnp
from jax import lax
from jax.experimental import pallas as pl
from jax.experimental.pallas import tpu as pltpu
from jax.sharding import PartitionSpec as P

SOFTENING = 0.0025
MESH = pl.DeviceIdType.MESH
F32, BF16 = jnp.float32, jnp.bfloat16
LANES = 128
GROUP = 16
ACT = 8
STARS = 4096
TILES = STARS // LANES
BLOCK = 256
SIZES = (3, 4, 8)


def place():
    row = lax.axis_index("row")
    col = lax.axis_index("col")
    z, y_lo, core = lax.div(col, 4), lax.rem(lax.div(col, 2), 2), lax.rem(col, 2)
    return row, z, y_lo, core, z * 2 + core, row * 2 + y_lo


def zc_peer(step):
    row, z, y_lo, core, zc, xy = place()
    peer = lax.rem(zc + step, GROUP)
    return peer, (row, lax.div(peer, 2) * 4 + y_lo * 2 + lax.rem(peer, 2))


def xy_peer(step):
    row, z, y_lo, core, zc, xy = place()
    peer = lax.rem(xy + step, GROUP)
    return peer, (lax.div(peer, 2), z * 4 + lax.rem(peer, 2) * 2 + core)


def ring(size, step):
    return min(step % size, -step % size)


ZC_STEPS = sorted(range(1, GROUP), key=lambda step: -ring(8, step // 2))
XY_STEPS = sorted(range(1, GROUP), key=lambda step: -ring(4, step // 4) - ring(4, step))


def greet():
    barrier = pltpu.get_barrier_semaphore()
    for peer, steps in ((zc_peer, ZC_STEPS), (xy_peer, XY_STEPS)):
        for step in steps:
            pl.semaphore_signal(barrier, inc=1, device_id=peer(step)[1], device_id_type=MESH)


def await_greetings():
    pl.semaphore_wait(pltpu.get_barrier_semaphore(), 2 * (GROUP - 1))


def wait_bytes(ref, sem):
    pltpu.make_async_copy(ref, ref, sem).wait()


def mm(a, b):
    return jnp.dot(a, b, preferred_element_type=F32)


def mm_t(a, b):
    return lax.dot_general(a, b, (((1,), (1,)), ((), ())), preferred_element_type=F32)


def pieces(value):
    first = value.astype(BF16).astype(F32)
    rest = value - first
    second = rest.astype(BF16).astype(F32)
    return first, second, rest - second


def coordinates(group):
    coarse = jnp.floor(group * 16.0 + 0.5) * 0.0625
    return coarse, pieces(group - coarse)


def scalars(group, coarse, shift):
    sub = lax.broadcasted_iota(jnp.int32, group.shape, 0)
    upper = sub < 3

    def pair(exact, whole):
        exact = jnp.sum(jnp.where(upper, exact, 0.0), axis=0, keepdims=True)
        whole = jnp.sum(jnp.where(upper, whole, 0.0), axis=0, keepdims=True)
        high = exact.astype(BF16).astype(F32)
        return (high, exact - high) + pieces(whole)

    fine = group - coarse
    vel, vel_coarse = pltpu.roll(group, 4, 0), pltpu.roll(coarse, 4, 0)
    square = pair(coarse * coarse, fine * (group + coarse) + jnp.where(sub == 0, shift, 0.0))
    cross = pair(coarse * vel_coarse, fine * vel + coarse * (vel - vel_coarse))
    return square, cross


def stack(rows, shape):
    sub = lax.broadcasted_iota(jnp.int32, shape, 0)
    total = jnp.zeros(shape, F32)
    for at, row in enumerate(rows):
        total = jnp.where(sub == at, row, total)
    return total


def source_features(group):
    coarse, (one, two, three) = coordinates(group)
    square, cross = scalars(group, coarse, 0.0)
    exact = stack(square[0:2] + (1.0, 1.0) + cross[0:2] + (1.0, 1.0), group.shape)
    rest = stack(square[2:5] + (1.0,) + cross[2:5] + (1.0,), group.shape)
    more = stack((1.0, 1.0, 0.0, 0.0, 1.0, 1.0, 0.0, 0.0), group.shape)
    none = jnp.zeros_like(group)
    return [exact, coarse, rest, more, coarse, coarse, coarse, one, two, three, one, one, two, two, none, none]


def target_features(group):
    coarse, (one, two, three) = coordinates(group)
    square, cross = scalars(group, coarse, SOFTENING)
    sub = lax.broadcasted_iota(jnp.int32, group.shape, 0)
    none = jnp.zeros_like(group)

    def tail(scalar, at):
        pad, rest = (0.0,) * at, (0.0,) * (4 - at)
        exact = stack(pad + (1.0, 1.0) + scalar[0:2] + rest, group.shape)
        fine = stack(pad + (1.0, 1.0, 1.0) + scalar[2:3] + rest, group.shape)
        more = stack(pad + scalar[3:5] + (0.0, 0.0) + rest, group.shape)
        return exact, fine, more

    def weights(change, scalar, at):
        exact, fine, more = tail(scalar, at)
        c, o, t, h = change(coarse), change(one), change(two), change(three)
        rows = [exact, c, fine, more, o, t, h, c, c, c, o, t, o, t, none, none]
        return jnp.concatenate(rows, 0).astype(BF16)

    near = weights(lambda v: jnp.where(sub < 3, -2.0 * v, 0.0), square, 0)
    along = weights(lambda v: -pltpu.roll(v, 4, 0), cross, 4)
    return near, along


def prepare_tile(tile, stars, mass_ref, feature_ref, moment_ref):
    cols = pl.ds(pl.multiple_of(tile * LANES, LANES), LANES)
    group = stars[:, cols]
    rows = jnp.concatenate(source_features(group), 0)
    feature_ref[cols, :] = rows.T.astype(BF16)
    sub = lax.broadcasted_iota(jnp.int32, group.shape, 0)
    moment = mass_ref[pl.ds(tile, 1), :] * jnp.where(sub == 3, 1.0, group)
    one, two, three = pieces(moment)
    moment_ref[:, cols] = jnp.concatenate([one, two, three, jnp.zeros_like(one)], 0).astype(BF16)


def gather_kernel(index_ref, count_ref, pos_hbm, vel_hbm, acc_hbm, jerk_hbm, mass_hbm, elapsed_hbm,
                  feature_ref, moment_ref, all_ref, rank_ref, choice_ref,
                  pos_ref, vel_ref, acc_ref, jerk_ref, mass_ref, elapsed_ref,
                  stars, mine, near, load_sem, send_sem, recv_sem):
    loads = [
        pltpu.make_async_copy(src, dst, load_sem.at[at])
        for at, (src, dst) in enumerate((
            (pos_hbm, pos_ref), (vel_hbm, vel_ref), (acc_hbm, acc_ref), (jerk_hbm, jerk_ref),
            (mass_hbm, mass_ref), (elapsed_hbm, elapsed_ref)))
    ]
    for load in loads:
        load.start()
    row, z, y_lo, core, zc, xy = place()
    greet()
    for load in loads:
        load.wait()
    stars[...] = jnp.zeros_like(stars)
    for tile in range(TILES):
        cols = pl.ds(tile * LANES, LANES)
        dt = elapsed_ref[tile:tile + 1, :]
        vel, acc, jerk = vel_ref[:, cols], acc_ref[:, cols], jerk_ref[:, cols]
        stars[0:3, cols] = pos_ref[:, cols] + dt * (vel + dt * (0.5 * acc + dt * (jerk * (1.0 / 6.0))))
        stars[4:7, cols] = vel + dt * (acc + dt * (0.5 * jerk))
    lane = lax.broadcasted_iota(jnp.int32, (8, LANES), 1)
    sub = lax.broadcasted_iota(jnp.int32, (8, LANES), 0)
    total = jnp.zeros((8, LANES), F32)
    for slot in range(ACT):
        away = lane - index_ref[slot]
        picked = jnp.zeros((8, LANES), F32)
        for tile in range(TILES):
            picked = jnp.where(away == -tile * LANES, stars[:, pl.ds(tile * LANES, LANES)], picked)
        value = jnp.sum(picked, axis=1, keepdims=True)
        value = jnp.where(sub == 3, jnp.where(slot < count_ref[0], 1.0, 0.0), value)
        total = jnp.where(lane == zc * ACT + slot, value, total)
    mine[...] = total
    await_greetings()
    for step in ZC_STEPS:
        peer, device = zc_peer(step)
        pltpu.make_async_remote_copy(
            src_ref=mine, dst_ref=near.at[step - 1],
            send_sem=send_sem.at[0], recv_sem=recv_sem.at[0],
            device_id=device, device_id_type=MESH).start()

    def prepare(tile, carry):
        prepare_tile(tile, stars, mass_ref, feature_ref, moment_ref)
        return carry

    lax.fori_loop(0, TILES // 2, prepare, 0, unroll=2)
    wait_bytes(near, recv_sem.at[0])
    for step in range(1, GROUP):
        total = total + near[step - 1]
    all_ref[pl.ds(xy, 1)] = total[None]
    for step in XY_STEPS:
        peer, device = xy_peer(step)
        pltpu.make_async_remote_copy(
            src_ref=all_ref.at[xy], dst_ref=all_ref.at[xy],
            send_sem=send_sem.at[1], recv_sem=recv_sem.at[1],
            device_id=device, device_id_type=MESH).start()
    lax.fori_loop(TILES // 2, TILES, prepare, 0, unroll=2)
    wait_bytes(near, send_sem.at[0])
    wait_bytes(near, recv_sem.at[1])
    alive = jnp.concatenate([all_ref[g, 3:4, :] for g in range(GROUP)], 0)
    before = lax.broadcasted_iota(jnp.int32, (LANES, LANES), 0)
    after = lax.broadcasted_iota(jnp.int32, (LANES, LANES), 1)
    inside = mm(alive.astype(BF16), jnp.where(before < after, 1.0, 0.0).astype(BF16))
    sums = mm(alive.astype(BF16), jnp.ones((LANES, LANES), BF16))
    earlier = jnp.where((after < before) & (after < GROUP), 1.0, 0.0)[0:GROUP, 0:GROUP]
    ahead = mm(earlier.astype(BF16), sums.astype(BF16))
    first = ahead - LANES * jnp.floor(ahead * (1.0 / LANES))
    lead = inside + first
    rank_ref[0] = jnp.where(alive > 0.0, lead - LANES * jnp.floor(lead * (1.0 / LANES)), -1.0)
    spot = lax.broadcasted_iota(jnp.int32, (GROUP, LANES), 1).astype(F32)
    rank_ref[1] = jnp.floor(ahead * (1.0 / LANES)) + jnp.where(spot < first, 1.0, 0.0)
    live = (ahead + sums)[GROUP - 1, 0].astype(jnp.int32)
    choice_ref[0] = sum((live > BLOCK * size).astype(jnp.int32) for size in SIZES[:-1])
    wait_bytes(near, send_sem.at[1])


def three_rows(group):
    return jnp.concatenate(list(pieces(group)) + [jnp.zeros_like(group)], 0).astype(BF16)


def joined(rows):
    return rows[0:8] + rows[8:16] + rows[16:24]


def force_kernel(blocks, count_ref, feature_ref, moment_ref, all_ref, rank_ref, out_ref,
                 part_ref, hot, near_ref, along_ref, target_ref, force_ref,
                 first, second, summed, send_sem, recv_sem):
    greet()
    tiles = blocks * BLOCK // LANES
    spot = lax.broadcasted_iota(jnp.int32, (LANES, LANES), 0).astype(F32)
    packed = [jnp.zeros((8, LANES), F32)] * tiles
    for g in range(GROUP):
        hot[g] = jnp.where(spot == rank_ref[0, g:g + 1, :], 1.0, 0.0).astype(BF16)
        chosen = joined(mm_t(three_rows(all_ref[g]), hot[g]))
        tile = rank_ref[1, g:g + 1, :]
        packed = [old + jnp.where(tile == at, chosen, 0.0) for at, old in enumerate(packed)]
    row_id = lax.broadcasted_iota(jnp.int32, (8, LANES), 0)
    for at in range(tiles):
        cols = pl.ds(at * LANES, LANES)
        target = jnp.where((row_id == 3) | (row_id == 7), 0.0, packed[at])
        target_ref[:, cols] = target
        near_ref[:, cols], along_ref[:, cols] = target_features(target)
    sub = lax.broadcasted_iota(jnp.int32, (8, BLOCK), 0)

    def block(index, carry):
        cols = pl.ds(pl.multiple_of(index * BLOCK, BLOCK), BLOCK)
        r2 = mm(feature_ref[...], near_ref[:, cols])
        dot = mm(feature_ref[...], along_ref[:, cols])
        inv = lax.rsqrt(r2)
        inv2 = inv * inv
        w = inv * inv2
        u = (w * inv2) * dot
        sums = []
        for value in (w, u):
            high = value.astype(BF16)
            low = (value - high.astype(F32)).astype(BF16)
            sums.append(joined(mm(moment_ref[...], high) + mm(moment_ref[...], low)))
        target = target_ref[:, cols]
        by_w, by_u = [total - target * total[3:4, :] for total in sums]
        force_ref[:, cols] = by_w - 3.0 * jnp.where(sub >= 4, pltpu.roll(by_u, 4, 0), 0.0)
        return carry

    lax.fori_loop(0, blocks, block, 0)
    for g in range(GROUP):
        tile = rank_ref[1, g:g + 1, :]
        chosen = jnp.zeros((8, LANES), F32)
        for at in range(tiles):
            chosen = jnp.where(tile == at, force_ref[:, at * LANES:(at + 1) * LANES], chosen)
        part_ref[g] = joined(mm(three_rows(chosen), hot[g]))
    row, z, y_lo, core, zc, xy = place()
    await_greetings()
    for step in XY_STEPS:
        peer, device = xy_peer(step)
        pltpu.make_async_remote_copy(
            src_ref=part_ref.at[peer], dst_ref=first.at[step - 1],
            send_sem=send_sem.at[0], recv_sem=recv_sem.at[0],
            device_id=device, device_id_type=MESH).start()
    total = part_ref[xy]
    wait_bytes(first, recv_sem.at[0])
    for step in range(1, GROUP):
        total = total + first[step - 1]
    summed[...] = total
    for step in ZC_STEPS:
        peer, device = zc_peer(step)
        pltpu.make_async_remote_copy(
            src_ref=summed, dst_ref=second.at[step - 1],
            send_sem=send_sem.at[1], recv_sem=recv_sem.at[1],
            device_id=device, device_id_type=MESH).start()
    wait_bytes(second, recv_sem.at[1])
    for step in range(1, GROUP):
        total = total + second[step - 1]
    mine = pltpu.roll(total, lax.rem(LANES - zc * ACT, LANES), 1)
    lane = lax.broadcasted_iota(jnp.int32, (8, LANES), 1)
    out_ref[...] = jnp.where(lane < count_ref[0], mine, 0.0)
    wait_bytes(first, send_sem.at[0])
    wait_bytes(second, send_sem.at[1])


def finish_kernel(force_ref, accel_ref, jerk_ref):
    accel_ref[...] = force_ref[0:3, 0:ACT]
    jerk_ref[...] = force_ref[4:7, 0:ACT]


def local(position, velocity, accel_old, jerk_old, mass, elapsed, active_index, active_count):
    vmem = pl.BlockSpec(memory_space=pltpu.VMEM)
    smem = pl.BlockSpec(memory_space=pltpu.SMEM)
    hbm = pl.BlockSpec(memory_space=pltpu.HBM)
    tiles = (GROUP, 8, LANES)
    features, moments, everyone, rank, choice = pl.pallas_call(
        gather_kernel,
        out_shape=(
            jax.ShapeDtypeStruct((STARS, LANES), BF16),
            jax.ShapeDtypeStruct((32, STARS), BF16),
            jax.ShapeDtypeStruct(tiles, F32),
            jax.ShapeDtypeStruct((2, GROUP, LANES), F32),
            jax.ShapeDtypeStruct((1,), jnp.int32),
        ),
        in_specs=[smem, smem] + [hbm] * 6,
        out_specs=(vmem,) * 4 + (smem,),
        scratch_shapes=[pltpu.VMEM((3, STARS), F32)] * 4 + [pltpu.VMEM((TILES, LANES), F32)] * 2 + [
            pltpu.VMEM((8, STARS), F32),
            pltpu.VMEM((8, LANES), F32),
            pltpu.VMEM((GROUP - 1, 8, LANES), F32),
            pltpu.SemaphoreType.DMA((6,)),
            pltpu.SemaphoreType.DMA((2,)),
            pltpu.SemaphoreType.DMA((2,)),
        ],
        compiler_params=pltpu.CompilerParams(
            collective_id=0, has_side_effects=True, vmem_limit_bytes=56 * 2**20),
        name="gather_targets",
    )(active_index, active_count, position, velocity, accel_old, jerk_old,
      mass.reshape(TILES, LANES), elapsed.reshape(TILES, LANES))

    def forces(at):
        return pl.pallas_call(
            functools.partial(force_kernel, SIZES[at]),
            out_shape=jax.ShapeDtypeStruct((8, LANES), F32),
            in_specs=[smem] + [vmem] * 4,
            out_specs=vmem,
            scratch_shapes=[
                pltpu.VMEM(tiles, F32),
                pltpu.VMEM((GROUP, LANES, LANES), BF16),
                pltpu.VMEM((LANES, SIZES[at] * BLOCK), BF16),
                pltpu.VMEM((LANES, SIZES[at] * BLOCK), BF16),
                pltpu.VMEM((8, SIZES[at] * BLOCK), F32),
                pltpu.VMEM((8, SIZES[at] * BLOCK), F32),
                pltpu.VMEM((GROUP - 1, 8, LANES), F32),
                pltpu.VMEM((GROUP - 1, 8, LANES), F32),
                pltpu.VMEM((8, LANES), F32),
                pltpu.SemaphoreType.DMA((2,)),
                pltpu.SemaphoreType.DMA((2,)),
            ],
            compiler_params=pltpu.CompilerParams(
                collective_id=1 + at, has_side_effects=True, vmem_limit_bytes=24 * 2**20),
            name="forces_%d" % SIZES[at],
        )

    branches = [forces(at) for at in range(len(SIZES))]
    mine = lax.switch(choice[0], branches, active_count, features, moments, everyone, rank)
    return pl.pallas_call(
        finish_kernel,
        out_shape=(jax.ShapeDtypeStruct((3, ACT), F32), jax.ShapeDtypeStruct((3, ACT), F32)),
        in_specs=[vmem],
        out_specs=(vmem, vmem),
        name="finish",
    )(mine)


def solution(mesh):
    split = P(None, ("row", "col"))
    flat = P(("row", "col"))
    return jax.shard_map(
        local,
        mesh=mesh,
        in_specs=(split, split, split, split, flat, flat, flat, flat),
        out_specs=(split, split),
        check_vma=False,
    )
```

```python
import functools

import jax
import jax.numpy as jnp
from jax import lax
from jax.experimental import pallas as pl
from jax.experimental.pallas import tpu as pltpu
from jax.sharding import PartitionSpec as P

SOFTENING = 0.0025
MESH = pl.DeviceIdType.MESH
F32, BF16 = jnp.float32, jnp.bfloat16
LANES = 128
GROUP = 16
ACT = 8
STARS = 4096
TILES = STARS // LANES
BLOCK = 256
SIZES = ((3, 2), (4, 2), (8, 8))


def place():
    row = lax.axis_index("row")
    col = lax.axis_index("col")
    z, y_lo, core = lax.div(col, 4), lax.rem(lax.div(col, 2), 2), lax.rem(col, 2)
    return row, z, y_lo, core, z * 2 + core, row * 2 + y_lo


def zc_peer(step):
    row, z, y_lo, core, zc, xy = place()
    peer = lax.rem(zc + step, GROUP)
    return peer, (row, lax.div(peer, 2) * 4 + y_lo * 2 + lax.rem(peer, 2))


def xy_peer(offset):
    row, z, y_lo, core, zc, xy = place()
    x = lax.rem(lax.div(row, 2) + offset[0], 4)
    y = lax.rem(lax.rem(row, 2) * 2 + y_lo + offset[1], 4)
    return x * 4 + y, (x * 2 + lax.div(y, 2), z * 4 + lax.rem(y, 2) * 2 + core)


def ring(size, step):
    return min(step % size, -step % size)


ZC_STEPS = sorted(range(1, GROUP), key=lambda step: -ring(8, step // 2))
XY_STEPS = sorted(((i // 4, i % 4) for i in range(1, GROUP)), key=lambda at: -ring(4, at[0]) - ring(4, at[1]))
FAR = 9
LAST_FAR = XY_STEPS[FAR - 1]


def distances(tile, centre):
    x, y = ((tile >> 2) - (centre >> 2)) & 3, ((tile & 3) - (centre & 3)) & 3
    return jnp.minimum(x, 4 - x) + jnp.minimum(y, 4 - y), x * 4 + y


def greet():
    barrier = pltpu.get_barrier_semaphore()
    for peer, steps in ((zc_peer, ZC_STEPS), (xy_peer, XY_STEPS)):
        for step in steps:
            pl.semaphore_signal(barrier, inc=1, device_id=peer(step)[1], device_id_type=MESH)


def await_greetings():
    pl.semaphore_wait(pltpu.get_barrier_semaphore(), 2 * (GROUP - 1))


def wait_bytes(ref, sem):
    pltpu.make_async_copy(ref, ref, sem).wait()


def mm(a, b):
    return jnp.dot(a, b, preferred_element_type=F32)


def mm_t(a, b):
    return lax.dot_general(a, b, (((1,), (1,)), ((), ())), preferred_element_type=F32)


def pieces(value):
    first = value.astype(BF16).astype(F32)
    rest = value - first
    second = rest.astype(BF16).astype(F32)
    return first, second, rest - second


def coordinates(group):
    coarse = jnp.floor(group * 16.0 + 0.5) * 0.0625
    return coarse, pieces(group - coarse)


def scalars(group, coarse, shift):
    sub = lax.broadcasted_iota(jnp.int32, group.shape, 0)
    upper = sub < 3

    def pair(exact, whole):
        exact = jnp.sum(jnp.where(upper, exact, 0.0), axis=0, keepdims=True)
        whole = jnp.sum(jnp.where(upper, whole, 0.0), axis=0, keepdims=True)
        high = exact.astype(BF16).astype(F32)
        return (high, exact - high) + pieces(whole)

    fine = group - coarse
    vel, vel_coarse = pltpu.roll(group, 4, 0), pltpu.roll(coarse, 4, 0)
    square = pair(coarse * coarse, fine * (group + coarse) + jnp.where(sub == 0, shift, 0.0))
    cross = pair(coarse * vel_coarse, fine * vel + coarse * (vel - vel_coarse))
    return square, cross


def stack(rows, shape):
    sub = lax.broadcasted_iota(jnp.int32, shape, 0)
    total = jnp.zeros(shape, F32)
    for at, row in enumerate(rows):
        total = jnp.where(sub == at, row, total)
    return total


def source_features(group):
    coarse, (one, two, three) = coordinates(group)
    square, cross = scalars(group, coarse, 0.0)
    exact = stack(square[0:2] + (1.0, 1.0) + cross[0:2] + (1.0, 1.0), group.shape)
    rest = stack(square[2:5] + (1.0,) + cross[2:5] + (1.0,), group.shape)
    more = stack((1.0, 1.0, 0.0, 0.0, 1.0, 1.0, 0.0, 0.0), group.shape)
    none = jnp.zeros_like(group)
    return [exact, coarse, rest, more, coarse, coarse, coarse, one, two, three, one, one, two, two, none, none]


def target_features(group):
    coarse, (one, two, three) = coordinates(group)
    square, cross = scalars(group, coarse, SOFTENING)
    sub = lax.broadcasted_iota(jnp.int32, group.shape, 0)
    none = jnp.zeros_like(group)

    def tail(scalar, at):
        pad, rest = (0.0,) * at, (0.0,) * (4 - at)
        exact = stack(pad + (1.0, 1.0) + scalar[0:2] + rest, group.shape)
        fine = stack(pad + (1.0, 1.0, 1.0) + scalar[2:3] + rest, group.shape)
        more = stack(pad + scalar[3:5] + (0.0, 0.0) + rest, group.shape)
        return exact, fine, more

    def weights(change, scalar, at):
        exact, fine, more = tail(scalar, at)
        c, o, t, h = change(coarse), change(one), change(two), change(three)
        rows = [exact, c, fine, more, o, t, h, c, c, c, o, t, o, t, none, none]
        return jnp.concatenate(rows, 0).astype(BF16)

    near = weights(lambda v: jnp.where(sub < 3, -2.0 * v, 0.0), square, 0)
    along = weights(lambda v: -pltpu.roll(v, 4, 0), cross, 4)
    return near, along


def prepare_tile(tile, stars, mass_ref, feature_ref, moment_ref):
    cols = pl.ds(pl.multiple_of(tile * LANES, LANES), LANES)
    group = stars[:, cols]
    rows = jnp.concatenate(source_features(group), 0)
    feature_ref[cols, :] = rows.T.astype(BF16)
    sub = lax.broadcasted_iota(jnp.int32, group.shape, 0)
    moment = mass_ref[pl.ds(tile, 1), :] * jnp.where(sub == 3, 1.0, group)
    one, two, three = pieces(moment)
    moment_ref[:, cols] = jnp.concatenate([one, two, three, jnp.zeros_like(one)], 0).astype(BF16)


def gather_kernel(index_ref, count_ref, pos_hbm, vel_hbm, acc_hbm, jerk_hbm, mass_hbm, elapsed_hbm,
                  feature_ref, moment_ref, all_ref, rank_ref, choice_ref,
                  pos_ref, vel_ref, acc_ref, jerk_ref, mass_ref, elapsed_ref,
                  stars, mine, near, load_sem, send_sem, recv_sem):
    loads = [
        pltpu.make_async_copy(src, dst, load_sem.at[at])
        for at, (src, dst) in enumerate((
            (pos_hbm, pos_ref), (vel_hbm, vel_ref), (acc_hbm, acc_ref), (jerk_hbm, jerk_ref),
            (mass_hbm, mass_ref), (elapsed_hbm, elapsed_ref)))
    ]
    for load in loads:
        load.start()
    row, z, y_lo, core, zc, xy = place()
    greet()
    for load in loads:
        load.wait()
    stars[...] = jnp.zeros_like(stars)
    for tile in range(TILES):
        cols = pl.ds(tile * LANES, LANES)
        dt = elapsed_ref[tile:tile + 1, :]
        vel, acc, jerk = vel_ref[:, cols], acc_ref[:, cols], jerk_ref[:, cols]
        stars[0:3, cols] = pos_ref[:, cols] + dt * (vel + dt * (0.5 * acc + dt * (jerk * (1.0 / 6.0))))
        stars[4:7, cols] = vel + dt * (acc + dt * (0.5 * jerk))
    lane = lax.broadcasted_iota(jnp.int32, (8, LANES), 1)
    sub = lax.broadcasted_iota(jnp.int32, (8, LANES), 0)
    total = jnp.zeros((8, LANES), F32)
    for slot in range(ACT):
        away = lane - index_ref[slot]
        picked = jnp.zeros((8, LANES), F32)
        for tile in range(TILES):
            picked = jnp.where(away == -tile * LANES, stars[:, pl.ds(tile * LANES, LANES)], picked)
        value = jnp.sum(picked, axis=1, keepdims=True)
        value = jnp.where(sub == 3, jnp.where(slot < count_ref[0], 1.0, 0.0), value)
        total = jnp.where(lane == zc * ACT + slot, value, total)
    mine[...] = total
    await_greetings()
    for step in ZC_STEPS:
        peer, device = zc_peer(step)
        pltpu.make_async_remote_copy(
            src_ref=mine, dst_ref=near.at[step - 1],
            send_sem=send_sem.at[0], recv_sem=recv_sem.at[0],
            device_id=device, device_id_type=MESH).start()

    def prepare(tile, carry):
        prepare_tile(tile, stars, mass_ref, feature_ref, moment_ref)
        return carry

    lax.fori_loop(0, TILES // 2, prepare, 0, unroll=2)
    wait_bytes(near, recv_sem.at[0])
    for step in range(1, GROUP):
        total = total + near[step - 1]
    all_ref[pl.ds(xy, 1)] = total[None]
    for step in XY_STEPS:
        peer, device = xy_peer(step)
        pltpu.make_async_remote_copy(
            src_ref=all_ref.at[xy], dst_ref=all_ref.at[xy],
            send_sem=send_sem.at[1], recv_sem=recv_sem.at[1],
            device_id=device, device_id_type=MESH).start()
    lax.fori_loop(TILES // 2, TILES, prepare, 0, unroll=2)
    wait_bytes(near, send_sem.at[0])
    wait_bytes(near, recv_sem.at[1])
    alive = jnp.concatenate([all_ref[g, 3:4, :] for g in range(GROUP)], 0)
    before = lax.broadcasted_iota(jnp.int32, (LANES, LANES), 0)
    after = lax.broadcasted_iota(jnp.int32, (LANES, LANES), 1)
    inside = mm(alive.astype(BF16), jnp.where(before < after, 1.0, 0.0).astype(BF16))
    sums = mm(alive.astype(BF16), jnp.ones((LANES, LANES), BF16))
    tile = lax.broadcasted_iota(jnp.int32, (GROUP, GROUP), 0)
    other = lax.broadcasted_iota(jnp.int32, (GROUP, GROUP), 1)
    (hops, step), (other_hops, other_step) = distances(tile, xy), distances(other, xy)
    earlier = other_step - GROUP * other_hops < step - GROUP * hops
    ahead = mm(jnp.where(earlier, 1.0, 0.0).astype(BF16), sums.astype(BF16))
    hops, step = distances(other, tile)
    last_hops, last_step = ring(4, LAST_FAR[0]) + ring(4, LAST_FAR[1]), LAST_FAR[0] * 4 + LAST_FAR[1]
    far = step - GROUP * hops <= last_step - GROUP * last_hops
    far = mm(jnp.where(far, 1.0, 0.0).astype(BF16), sums.astype(BF16))
    first = ahead - LANES * jnp.floor(ahead * (1.0 / LANES))
    lead = inside + first
    rank_ref[0] = jnp.where(alive > 0.0, lead - LANES * jnp.floor(lead * (1.0 / LANES)), -1.0)
    spot = lax.broadcasted_iota(jnp.int32, (GROUP, LANES), 1).astype(F32)
    rank_ref[1] = jnp.floor(ahead * (1.0 / LANES)) + jnp.where(spot < first, 1.0, 0.0)
    live = jnp.max(ahead + sums, axis=0, keepdims=True)
    far = jnp.max(far, axis=0, keepdims=True)
    choice = jnp.full((1, LANES), len(SIZES) - 1.0, F32)
    for at in reversed(range(len(SIZES) - 1)):
        blocks, early = SIZES[at]
        choice = jnp.where((live <= blocks * BLOCK) & (far <= early * BLOCK), float(at), choice)
    choice_ref[0] = choice[0, 0].astype(jnp.int32)
    wait_bytes(near, send_sem.at[1])


def three_rows(group):
    return jnp.concatenate(list(pieces(group)) + [jnp.zeros_like(group)], 0).astype(BF16)


def joined(rows):
    return rows[0:8] + rows[8:16] + rows[16:24]


def force_kernel(blocks, early, count_ref, feature_ref, moment_ref, all_ref, rank_ref, out_ref,
                 part_ref, hot, near_ref, along_ref, target_ref, force_ref,
                 first, second, summed, send_sem, recv_sem):
    greet()
    tiles = blocks * BLOCK // LANES
    spot = lax.broadcasted_iota(jnp.int32, (LANES, LANES), 0).astype(F32)
    packed = [jnp.zeros((8, LANES), F32)] * tiles
    for g in range(GROUP):
        hot[g] = jnp.where(spot == rank_ref[0, g:g + 1, :], 1.0, 0.0).astype(BF16)
        chosen = joined(mm_t(three_rows(all_ref[g]), hot[g]))
        tile = rank_ref[1, g:g + 1, :]
        packed = [old + jnp.where(tile == at, chosen, 0.0) for at, old in enumerate(packed)]
    row_id = lax.broadcasted_iota(jnp.int32, (8, LANES), 0)
    for at in range(tiles):
        cols = pl.ds(at * LANES, LANES)
        target = jnp.where((row_id == 3) | (row_id == 7), 0.0, packed[at])
        target_ref[:, cols] = target
        near_ref[:, cols], along_ref[:, cols] = target_features(target)
    sub = lax.broadcasted_iota(jnp.int32, (8, BLOCK), 0)

    def block(index, carry):
        cols = pl.ds(pl.multiple_of(index * BLOCK, BLOCK), BLOCK)
        r2 = mm(feature_ref[...], near_ref[:, cols])
        dot = mm(feature_ref[...], along_ref[:, cols])
        inv = lax.rsqrt(r2)
        inv2 = inv * inv
        w = inv * inv2
        u = (w * inv2) * dot
        sums = []
        for value in (w, u):
            high = value.astype(BF16)
            low = (value - high.astype(F32)).astype(BF16)
            sums.append(joined(mm(moment_ref[...], high) + mm(moment_ref[...], low)))
        target = target_ref[:, cols]
        by_w, by_u = [total - target * total[3:4, :] for total in sums]
        force_ref[:, cols] = by_w - 3.0 * jnp.where(sub >= 4, pltpu.roll(by_u, 4, 0), 0.0)
        return carry

    def unpack(peer, done):
        tile = rank_ref[1, pl.ds(peer, 1), :]
        chosen = jnp.zeros((8, LANES), F32)
        for at in range(done * BLOCK // LANES):
            chosen = jnp.where(tile == at, force_ref[:, at * LANES:(at + 1) * LANES], chosen)
        part_ref[peer] = joined(mm(three_rows(chosen), hot[peer]))

    def send(at, peer, device):
        pltpu.make_async_remote_copy(
            src_ref=part_ref.at[peer], dst_ref=first.at[at],
            send_sem=send_sem.at[0], recv_sem=recv_sem.at[0],
            device_id=device, device_id_type=MESH).start()

    row, z, y_lo, core, zc, xy = place()
    peers = [xy_peer(step) for step in XY_STEPS]

    def send_far():
        for peer, device in peers[:FAR]:
            unpack(peer, early)
        await_greetings()
        for at in range(FAR):
            send(at, *peers[at])

    def step(index, carry):
        pl.when(index == early)(send_far)
        return block(index, carry)

    lax.fori_loop(0, blocks, step, 0)
    if early == blocks:
        send_far()
    for peer, device in peers[FAR:]:
        unpack(peer, blocks)
    for at in range(FAR, GROUP - 1):
        send(at, *peers[at])
    unpack(xy, blocks)
    total = part_ref[xy]
    wait_bytes(first, recv_sem.at[0])
    for step in range(1, GROUP):
        total = total + first[step - 1]
    summed[...] = total
    for step in ZC_STEPS:
        peer, device = zc_peer(step)
        pltpu.make_async_remote_copy(
            src_ref=summed, dst_ref=second.at[step - 1],
            send_sem=send_sem.at[1], recv_sem=recv_sem.at[1],
            device_id=device, device_id_type=MESH).start()
    wait_bytes(second, recv_sem.at[1])
    for step in range(1, GROUP):
        total = total + second[step - 1]
    mine = pltpu.roll(total, lax.rem(LANES - zc * ACT, LANES), 1)
    lane = lax.broadcasted_iota(jnp.int32, (8, LANES), 1)
    out_ref[...] = jnp.where(lane < count_ref[0], mine, 0.0)
    wait_bytes(first, send_sem.at[0])
    wait_bytes(second, send_sem.at[1])


def finish_kernel(force_ref, accel_ref, jerk_ref):
    accel_ref[...] = force_ref[0:3, 0:ACT]
    jerk_ref[...] = force_ref[4:7, 0:ACT]


def local(position, velocity, accel_old, jerk_old, mass, elapsed, active_index, active_count):
    vmem = pl.BlockSpec(memory_space=pltpu.VMEM)
    smem = pl.BlockSpec(memory_space=pltpu.SMEM)
    hbm = pl.BlockSpec(memory_space=pltpu.HBM)
    tiles = (GROUP, 8, LANES)
    features, moments, everyone, rank, choice = pl.pallas_call(
        gather_kernel,
        out_shape=(
            jax.ShapeDtypeStruct((STARS, LANES), BF16),
            jax.ShapeDtypeStruct((32, STARS), BF16),
            jax.ShapeDtypeStruct(tiles, F32),
            jax.ShapeDtypeStruct((2, GROUP, LANES), F32),
            jax.ShapeDtypeStruct((1,), jnp.int32),
        ),
        in_specs=[smem, smem] + [hbm] * 6,
        out_specs=(vmem,) * 4 + (smem,),
        scratch_shapes=[pltpu.VMEM((3, STARS), F32)] * 4 + [pltpu.VMEM((TILES, LANES), F32)] * 2 + [
            pltpu.VMEM((8, STARS), F32),
            pltpu.VMEM((8, LANES), F32),
            pltpu.VMEM((GROUP - 1, 8, LANES), F32),
            pltpu.SemaphoreType.DMA((6,)),
            pltpu.SemaphoreType.DMA((2,)),
            pltpu.SemaphoreType.DMA((2,)),
        ],
        compiler_params=pltpu.CompilerParams(
            collective_id=0, has_side_effects=True, vmem_limit_bytes=56 * 2**20),
        name="gather_targets",
    )(active_index, active_count, position, velocity, accel_old, jerk_old,
      mass.reshape(TILES, LANES), elapsed.reshape(TILES, LANES))

    def forces(at):
        return pl.pallas_call(
            functools.partial(force_kernel, *SIZES[at]),
            out_shape=jax.ShapeDtypeStruct((8, LANES), F32),
            in_specs=[smem] + [vmem] * 4,
            out_specs=vmem,
            scratch_shapes=[
                pltpu.VMEM(tiles, F32),
                pltpu.VMEM((GROUP, LANES, LANES), BF16),
                pltpu.VMEM((LANES, SIZES[at][0] * BLOCK), BF16),
                pltpu.VMEM((LANES, SIZES[at][0] * BLOCK), BF16),
                pltpu.VMEM((8, SIZES[at][0] * BLOCK), F32),
                pltpu.VMEM((8, SIZES[at][0] * BLOCK), F32),
                pltpu.VMEM((GROUP - 1, 8, LANES), F32),
                pltpu.VMEM((GROUP - 1, 8, LANES), F32),
                pltpu.VMEM((8, LANES), F32),
                pltpu.SemaphoreType.DMA((2,)),
                pltpu.SemaphoreType.DMA((2,)),
            ],
            compiler_params=pltpu.CompilerParams(
                collective_id=1 + at, has_side_effects=True, vmem_limit_bytes=24 * 2**20),
            name="forces_%d" % SIZES[at][0],
        )

    branches = [forces(at) for at in range(len(SIZES))]
    mine = lax.switch(choice[0], branches, active_count, features, moments, everyone, rank)
    return pl.pallas_call(
        finish_kernel,
        out_shape=(jax.ShapeDtypeStruct((3, ACT), F32), jax.ShapeDtypeStruct((3, ACT), F32)),
        in_specs=[vmem],
        out_specs=(vmem, vmem),
        name="finish",
    )(mine)


def solution(mesh):
    split = P(None, ("row", "col"))
    flat = P(("row", "col"))
    return jax.shard_map(
        local,
        mesh=mesh,
        in_specs=(split, split, split, split, flat, flat, flat, flat),
        out_specs=(split, split),
        check_vma=False,
    )
```

```python
import jax
import jax.numpy as jnp
from jax import lax
from jax.experimental import pallas as pl
from jax.experimental.pallas import tpu as pltpu
from jax.sharding import PartitionSpec as P

SOFTENING = 0.0025
MESH = pl.DeviceIdType.MESH
F32, BF16 = jnp.float32, jnp.bfloat16
LANES = 128
GROUP = 16
ACT = 8
STARS = 4096
TILES = STARS // LANES
BLOCK = 256
MIDDLE = 512
ROOM = 896
SLOTS = GROUP * LANES


def ring(size, step):
    return min(step % size, -step % size)


def hops(step):
    return ring(4, step[0]) + ring(4, step[1])


ZC_STEPS = sorted(range(1, GROUP), key=lambda step: -ring(8, step // 2))
XY_STEPS = sorted(((i // 4, i % 4) for i in range(GROUP)), key=lambda step: (2, 3, 4, 1, 0).index(hops(step)))
START = sum(hops(step) == 2 for step in XY_STEPS)
EARLY = sum(hops(step) >= 2 for step in XY_STEPS)
NEAR_FIRST = sorted(range(GROUP - 1), key=lambda at: hops(XY_STEPS[at]))
FAR_FIRST = NEAR_FIRST[::-1]


def place():
    row = lax.axis_index("row")
    col = lax.axis_index("col")
    z, y_lo, core = col >> 2, (col >> 1) & 1, col & 1
    return row, z, y_lo, core, z * 2 + core, row * 2 + y_lo


def zc_peers():
    row, z, y_lo, core, zc, xy = place()
    peers = []
    for step in ZC_STEPS:
        peer = (zc + step) & (GROUP - 1)
        peers.append((peer, (row, (peer >> 1) * 4 + y_lo * 2 + (peer & 1))))
    return peers


def xy_peers():
    row, z, y_lo, core, zc, xy = place()
    rows = [((row >> 1) + step) & 3 for step in range(4)]
    columns = [((row & 1) * 2 + y_lo + step) & 3 for step in range(4)]
    peers = []
    for step in XY_STEPS:
        x, y = rows[step[0]], columns[step[1]]
        peers.append((x * 4 + y, (x * 2 + (y >> 1), z * 4 + (y & 1) * 2 + core)))
    return peers


def greet():
    barrier = pltpu.get_barrier_semaphore()
    for peer, device in zc_peers() + xy_peers()[:-1]:
        pl.semaphore_signal(barrier, inc=1, device_id=device, device_id_type=MESH)


def await_greetings():
    pl.semaphore_wait(pltpu.get_barrier_semaphore(), 2 * (GROUP - 1))


def wait_bytes(ref, sem):
    pltpu.make_async_copy(ref, ref, sem).wait()


def send(src, dst, sent, landed, device):
    pltpu.make_async_remote_copy(
        src_ref=src, dst_ref=dst, send_sem=sent, recv_sem=landed,
        device_id=device, device_id_type=MESH).start()


def mm(a, b):
    return jnp.dot(a, b, preferred_element_type=F32)


def mm_t(a, b):
    return lax.dot_general(a, b, (((1,), (1,)), ((), ())), preferred_element_type=F32)


def pieces(value):
    first = value.astype(BF16).astype(F32)
    rest = value - first
    second = rest.astype(BF16).astype(F32)
    return first, second, rest - second


def coordinates(group):
    coarse = jnp.floor(group * 16.0 + 0.5) * 0.0625
    return coarse, pieces(group - coarse)


def scalars(group, coarse, shift):
    sub = lax.broadcasted_iota(jnp.int32, group.shape, 0)
    upper = sub < 3

    def pair(exact, whole):
        exact = jnp.sum(jnp.where(upper, exact, 0.0), axis=0, keepdims=True)
        whole = jnp.sum(jnp.where(upper, whole, 0.0), axis=0, keepdims=True)
        high = exact.astype(BF16).astype(F32)
        return (high, exact - high) + pieces(whole)

    fine = group - coarse
    vel, vel_coarse = pltpu.roll(group, 4, 0), pltpu.roll(coarse, 4, 0)
    square = pair(coarse * coarse, fine * (group + coarse) + jnp.where(sub == 0, shift, 0.0))
    cross = pair(coarse * vel_coarse, fine * vel + coarse * (vel - vel_coarse))
    return square, cross


def stack(rows, shape):
    sub = lax.broadcasted_iota(jnp.int32, shape, 0)
    total = jnp.zeros(shape, F32)
    for at, row in enumerate(rows):
        total = jnp.where(sub == at, row, total)
    return total


def source_features(group):
    coarse, (one, two, three) = coordinates(group)
    square, cross = scalars(group, coarse, 0.0)
    exact = stack(square[0:2] + (1.0, 1.0) + cross[0:2] + (1.0, 1.0), group.shape)
    rest = stack(square[2:5] + (1.0,) + cross[2:5] + (1.0,), group.shape)
    more = stack((1.0, 1.0, 0.0, 0.0, 1.0, 1.0, 0.0, 0.0), group.shape)
    none = jnp.zeros_like(group)
    return [exact, coarse, rest, more, coarse, coarse, coarse, one, two, three, one, one, two, two, none, none]


def target_features(group):
    coarse, (one, two, three) = coordinates(group)
    square, cross = scalars(group, coarse, SOFTENING)
    sub = lax.broadcasted_iota(jnp.int32, group.shape, 0)
    none = jnp.zeros_like(group)

    def tail(scalar, at):
        pad, rest = (0.0,) * at, (0.0,) * (4 - at)
        exact = stack(pad + (1.0, 1.0) + scalar[0:2] + rest, group.shape)
        fine = stack(pad + (1.0, 1.0, 1.0) + scalar[2:3] + rest, group.shape)
        more = stack(pad + scalar[3:5] + (0.0, 0.0) + rest, group.shape)
        return exact, fine, more

    def weights(change, scalar, at):
        exact, fine, more = tail(scalar, at)
        c, o, t, h = change(coarse), change(one), change(two), change(three)
        rows = [exact, c, fine, more, o, t, h, c, c, c, o, t, o, t, none, none]
        return jnp.concatenate(rows, 0).astype(BF16)

    near = weights(lambda v: jnp.where(sub < 3, -2.0 * v, 0.0), square, 0)
    along = weights(lambda v: -pltpu.roll(v, 4, 0), cross, 4)
    return near, along


def prepare_tile(tile, stars, mass_ref, feature_ref, moment_ref):
    cols = pl.ds(pl.multiple_of(tile * LANES, LANES), LANES)
    group = stars[:, cols]
    rows = jnp.concatenate(source_features(group), 0)
    feature_ref[cols, :] = rows.T.astype(BF16)
    sub = lax.broadcasted_iota(jnp.int32, group.shape, 0)
    moment = mass_ref[pl.ds(tile, 1), :] * jnp.where(sub == 3, 1.0, group)
    one, two, three = pieces(moment)
    moment_ref[:, cols] = jnp.concatenate([one, two, three, jnp.zeros_like(one)], 0).astype(BF16)


def three_rows(group):
    return jnp.concatenate(list(pieces(group)) + [jnp.zeros_like(group)], 0).astype(BF16)


def joined(rows):
    return rows[0:8] + rows[8:16] + rows[16:24]


def places(alive, start):
    before = lax.broadcasted_iota(jnp.int32, (LANES, LANES), 0)
    after = lax.broadcasted_iota(jnp.int32, (LANES, LANES), 1)
    tile = lax.broadcasted_iota(jnp.int32, (GROUP, GROUP), 0)
    other = lax.broadcasted_iota(jnp.int32, (GROUP, GROUP), 1)
    alive_b = alive.astype(BF16)
    inside = mm(alive_b, jnp.where(before < after, 1.0, 0.0).astype(BF16))
    sums = mm(alive_b, jnp.ones((LANES, LANES), BF16))
    ahead = mm(jnp.where(other < tile, 1.0, 0.0).astype(BF16), sums.astype(BF16))
    if start:
        late = lax.broadcasted_iota(jnp.int32, (GROUP, LANES), 0) >= start
        ahead = ahead + jnp.where(late, jnp.maximum(BLOCK - ahead[start:start + 1, :], 0.0), 0.0)
    first = ahead - LANES * jnp.floor(ahead * (1.0 / LANES))
    lead = inside + first
    lane = jnp.where(alive > 0.0, lead - LANES * jnp.floor(lead * (1.0 / LANES)), -1.0)
    spot = lax.broadcasted_iota(jnp.int32, (GROUP, LANES), 1).astype(F32)
    return lane, jnp.floor(ahead * (1.0 / LANES)) + jnp.where(spot < first, 1.0, 0.0)


def pack(at, group, lane, tile, hot, packed):
    spot = lax.broadcasted_iota(jnp.int32, (LANES, LANES), 0).astype(F32)
    hot[at] = jnp.where(spot == lane[at:at + 1, :], 1.0, 0.0).astype(BF16)
    chosen = joined(mm_t(three_rows(group), hot[at]))
    return [old + jnp.where(tile[at:at + 1, :] == number, chosen, 0.0) for number, old in enumerate(packed)]


def unpack(at, tile, numbers, hot, force_ref):
    chosen = jnp.zeros((8, LANES), F32)
    for number in numbers:
        chosen = jnp.where(tile == number, force_ref[:, number * LANES:(number + 1) * LANES], chosen)
    return joined(mm(three_rows(chosen), hot[at]))


def weigh(number, packed, target_ref, near_ref, along_ref):
    sub = lax.broadcasted_iota(jnp.int32, (8, LANES), 0)
    cols = pl.ds(number * LANES, LANES)
    target = jnp.where((sub == 3) | (sub == 7), 0.0, packed)
    target_ref[:, cols] = target
    near_ref[:, cols], along_ref[:, cols] = target_features(target)


def pair_weights(r2, dot):
    inv = lax.rsqrt(r2)
    inv2 = inv * inv
    w = inv * inv2
    out = []
    for value in (w, (w * inv2) * dot):
        high = value.astype(BF16)
        out.append((high, (value - high.astype(F32)).astype(BF16)))
    return out


def force_of(by_w, by_u, target):
    sub = lax.broadcasted_iota(jnp.int32, target.shape, 0)
    by_w, by_u = by_w - target * by_w[3:4, :], by_u - target * by_u[3:4, :]
    return by_w - 3.0 * jnp.where(sub >= 4, pltpu.roll(by_u, 4, 0), 0.0)


def force_block(lead, feature_ref, moment_ref, near_ref, along_ref, target_ref, force_ref):
    cols = pl.ds(pl.multiple_of(lead, LANES), BLOCK)
    r2 = mm(feature_ref[...], near_ref[:, cols])
    dot = mm(feature_ref[...], along_ref[:, cols])
    sums = [joined(mm(moment_ref[...], high) + mm(moment_ref[...], low)) for high, low in pair_weights(r2, dot)]
    force_ref[:, cols] = force_of(*sums, target_ref[:, cols])


def force_half_block(lead, feature_ref, moment_ref, near_ref, along_ref, target_ref, force_ref):
    cols = pl.ds(lead, LANES)
    both = mm(feature_ref[...], jnp.concatenate([near_ref[:, cols], along_ref[:, cols]], 1))
    sums = []
    for high, low in pair_weights(both[:, :LANES], both[:, LANES:]):
        total = mm(moment_ref[...], jnp.concatenate([high, low], 1))
        sums.append(joined(total[:, :LANES] + total[:, LANES:]))
    force_ref[:, cols] = force_of(*sums, target_ref[:, cols])


def last_stage(total, summed, second, send_sem, recv_sem):
    summed[...] = total
    for at, (peer, device) in enumerate(zc_peers()):
        send(summed, second.at[at], send_sem, recv_sem, device)


def last_sum(total, count_ref, second, recv_sem):
    wait_bytes(second, recv_sem)
    for at in range(GROUP - 1):
        total = total + second[at]
    row, z, y_lo, core, zc, xy = place()
    mine = pltpu.roll(total, (LANES - zc * ACT) & (LANES - 1), 1)
    lane = lax.broadcasted_iota(jnp.int32, (8, LANES), 1)
    return jnp.where(lane < count_ref[0], mine, 0.0)


def overfull(all_ref):
    alive = jnp.concatenate([all_ref[g, 3:4, :] for g in range(GROUP)], 0).astype(BF16)
    sums = mm(alive, jnp.ones((LANES, LANES), BF16)).astype(BF16)
    centre = lax.broadcasted_iota(jnp.int32, (GROUP, GROUP), 0)
    tile = lax.broadcasted_iota(jnp.int32, (GROUP, GROUP), 1)
    x, y = ((tile >> 2) - (centre >> 2)) & 3, ((tile & 3) - (centre & 3)) & 3
    away = jnp.minimum(x, 4 - x) + jnp.minimum(y, 4 - y)
    begun, far, near = [
        mm(jnp.where(of, 1.0, 0.0).astype(BF16), sums) for of in (away == 2, away > 2, away < 2)]
    early = jnp.maximum(begun, float(BLOCK)) + far
    over = (early > MIDDLE + LANES) | (early + near > ROOM)
    return jnp.max(jnp.where(over, 1.0, 0.0), axis=0, keepdims=True)[0, 0].astype(jnp.int32)


def fast_kernel(index_ref, count_ref, pos_hbm, vel_hbm, acc_hbm, jerk_hbm, mass_hbm, elapsed_hbm,
                out_ref, stars, all_ref, choice_ref,
                pos_ref, vel_ref, acc_ref, jerk_ref, mass_ref, elapsed_ref,
                feature_ref, moment_ref, mine, landed, tile_ref, hot, near_ref, along_ref, target_ref,
                force_ref, part_ref, first, second, summed, load_sem, send_sem, recv_sem):
    loads = [
        pltpu.make_async_copy(src, dst, load_sem.at[at])
        for at, (src, dst) in enumerate((
            (pos_hbm, pos_ref), (vel_hbm, vel_ref), (acc_hbm, acc_ref), (jerk_hbm, jerk_ref),
            (mass_hbm, mass_ref), (elapsed_hbm, elapsed_ref)))
    ]
    for load in loads:
        load.start()
    greet()
    for load in loads:
        load.wait()
    row, z, y_lo, core, zc, xy = place()
    stars[...] = jnp.zeros_like(stars)
    for tile in range(TILES):
        cols = pl.ds(tile * LANES, LANES)
        dt = elapsed_ref[tile:tile + 1, :]
        vel, acc, jerk = vel_ref[:, cols], acc_ref[:, cols], jerk_ref[:, cols]
        stars[0:3, cols] = pos_ref[:, cols] + dt * (vel + dt * (0.5 * acc + dt * (jerk * (1.0 / 6.0))))
        stars[4:7, cols] = vel + dt * (acc + dt * (0.5 * jerk))
    lane = lax.broadcasted_iota(jnp.int32, (8, LANES), 1)
    sub = lax.broadcasted_iota(jnp.int32, (8, LANES), 0)
    total = jnp.zeros((8, LANES), F32)
    for slot in range(ACT):
        away = lane - index_ref[slot]
        picked = jnp.zeros((8, LANES), F32)
        for tile in range(TILES):
            picked = jnp.where(away == -tile * LANES, stars[:, pl.ds(tile * LANES, LANES)], picked)
        value = jnp.sum(picked, axis=1, keepdims=True)
        value = jnp.where(sub == 3, jnp.where(slot < count_ref[0], 1.0, 0.0), value)
        total = jnp.where(lane == zc * ACT + slot, value, total)
    mine[...] = total
    await_greetings()
    for at, (peer, device) in enumerate(zc_peers()):
        send(mine, landed.at[at], send_sem.at[0], recv_sem.at[0], device)

    def prepare(tile, carry):
        prepare_tile(tile, stars, mass_ref, feature_ref, moment_ref)
        return carry

    lax.fori_loop(0, TILES // 2, prepare, 0, unroll=2)
    wait_bytes(landed, recv_sem.at[0])
    for at in range(GROUP - 1):
        total = total + landed[at]
    all_ref[pl.ds(xy, 1)] = total[None]
    peers = xy_peers()
    for at in FAR_FIRST:
        far = 2 if START <= at < EARLY else 1
        send(all_ref.at[xy], all_ref.at[xy], send_sem.at[1], recv_sem.at[far], peers[at][1])
    lax.fori_loop(TILES // 2, TILES, prepare, 0, unroll=2)

    wait_bytes(landed.at[pl.ds(0, GROUP - 1 - EARLY + START)], recv_sem.at[1])
    none = jnp.zeros((1, LANES), F32)
    numbers = ROOM // LANES
    spots, tiles = places(jnp.concatenate(
        [all_ref[peer, 3:4, :] for peer, device in peers[:START]] + [none] * (GROUP - START), 0), START)
    packed = [jnp.zeros((8, LANES), F32)] * numbers
    for at in range(START):
        packed = pack(at, all_ref[peers[at][0]], spots, tiles, hot, packed)
    for number in range(2):
        weigh(number, packed[number], target_ref, near_ref, along_ref)
    for number in range(2, numbers):
        target_ref[:, number * LANES:(number + 1) * LANES] = packed[number]

    def pack_rest():
        wait_bytes(landed.at[pl.ds(0, EARLY - START)], recv_sem.at[2])
        spots, tiles = places(jnp.concatenate([all_ref[peer, 3:4, :] for peer, device in peers], 0), START)
        tile_ref[...] = tiles
        packed = [target_ref[:, number * LANES:(number + 1) * LANES] for number in range(numbers)]
        for at in range(START, GROUP):
            packed = pack(at, all_ref[peers[at][0]], spots, tiles, hot, packed)
        for number in range(2, numbers):
            weigh(number, packed[number], target_ref, near_ref, along_ref)

    refs = (feature_ref, moment_ref, near_ref, along_ref, target_ref, force_ref)

    def send_early():
        force_half_block(MIDDLE, *refs)
        for at in range(EARLY):
            part_ref[at] = unpack(at, tile_ref[at:at + 1, :], range((MIDDLE + LANES) // LANES), hot, force_ref)
        for at in FAR_FIRST:
            if at < EARLY:
                send(part_ref.at[at], first.at[at], send_sem.at[2], recv_sem.at[3], peers[at][1])

    def step(index, carry):
        pl.when(index == 1)(pack_rest)
        pl.when(index == 2)(send_early)
        force_block(index * BLOCK + (index >> 1) * LANES, *refs)
        return carry

    lax.fori_loop(0, 3, step, 0)
    for at in range(EARLY, GROUP):
        part_ref[at] = unpack(at, tile_ref[at:at + 1, :], range(2, numbers), hot, force_ref)
        if at < GROUP - 1:
            send(part_ref.at[at], first.at[at], send_sem.at[2], recv_sem.at[3], peers[at][1])
    total = part_ref[GROUP - 1]
    wait_bytes(first, recv_sem.at[3])
    for at in range(GROUP - 1):
        total = total + first[at]
    last_stage(total, summed, second, send_sem.at[3], recv_sem.at[4])
    choice_ref[0] = overfull(all_ref)
    out_ref[...] = last_sum(total, count_ref, second, recv_sem.at[4])
    for at in range(4):
        wait_bytes(landed, send_sem.at[at])


def general_kernel(count_ref, mass_ref, stars, all_ref, out_ref,
                   feature_ref, moment_ref, tile_ref, hot, near_ref, along_ref, target_ref,
                   force_ref, part_ref, first, second, summed, send_sem, recv_sem):
    greet()

    def prepare(tile, carry):
        prepare_tile(tile, stars, mass_ref, feature_ref, moment_ref)
        return carry

    lax.fori_loop(0, TILES, prepare, 0)
    numbers = SLOTS // LANES
    spots, tiles = places(jnp.concatenate([all_ref[g, 3:4, :] for g in range(GROUP)], 0), 0)
    tile_ref[...] = tiles
    packed = [jnp.zeros((8, LANES), F32)] * numbers
    for at in range(GROUP):
        packed = pack(at, all_ref[at], spots, tiles, hot, packed)
    for number in range(numbers):
        weigh(number, packed[number], target_ref, near_ref, along_ref)

    def step(index, carry):
        force_block(index * BLOCK, feature_ref, moment_ref, near_ref, along_ref, target_ref, force_ref)
        return carry

    lax.fori_loop(0, SLOTS // BLOCK, step, 0)
    for at in range(GROUP):
        part_ref[at] = unpack(at, tile_ref[at:at + 1, :], range(numbers), hot, force_ref)
    await_greetings()
    peers = xy_peers()
    for at in FAR_FIRST:
        peer, device = peers[at]
        send(part_ref.at[peer], first.at[at], send_sem.at[0], recv_sem.at[0], device)
    total = part_ref[peers[-1][0]]
    wait_bytes(first, recv_sem.at[0])
    for at in range(GROUP - 1):
        total = total + first[at]
    last_stage(total, summed, second, send_sem.at[1], recv_sem.at[1])
    out_ref[...] = last_sum(total, count_ref, second, recv_sem.at[1])
    for at in range(2):
        wait_bytes(first, send_sem.at[at])


def finish_kernel(force_ref, accel_ref, jerk_ref):
    accel_ref[...] = force_ref[0:3, 0:ACT]
    jerk_ref[...] = force_ref[4:7, 0:ACT]


def force_scratch(room):
    return [
        pltpu.VMEM((GROUP, LANES), F32),
        pltpu.VMEM((GROUP, LANES, LANES), BF16),
        pltpu.VMEM((LANES, room), BF16),
        pltpu.VMEM((LANES, room), BF16),
        pltpu.VMEM((8, room), F32),
        pltpu.VMEM((8, room), F32),
        pltpu.VMEM((GROUP, 8, LANES), F32),
        pltpu.VMEM((GROUP - 1, 8, LANES), F32),
        pltpu.VMEM((GROUP - 1, 8, LANES), F32),
        pltpu.VMEM((8, LANES), F32),
    ]


def local(position, velocity, accel_old, jerk_old, mass, elapsed, active_index, active_count):
    vmem = pl.BlockSpec(memory_space=pltpu.VMEM)
    smem = pl.BlockSpec(memory_space=pltpu.SMEM)
    hbm = pl.BlockSpec(memory_space=pltpu.HBM)
    star_scratch = [pltpu.VMEM((STARS, LANES), BF16), pltpu.VMEM((32, STARS), BF16)]
    mass = mass.reshape(TILES, LANES)
    mine, stars, everyone, choice = pl.pallas_call(
        fast_kernel,
        out_shape=(
            jax.ShapeDtypeStruct((8, LANES), F32),
            jax.ShapeDtypeStruct((8, STARS), F32),
            jax.ShapeDtypeStruct((GROUP, 8, LANES), F32),
            jax.ShapeDtypeStruct((1,), jnp.int32),
        ),
        in_specs=[smem, smem] + [hbm] * 6,
        out_specs=(vmem,) * 3 + (smem,),
        scratch_shapes=[pltpu.VMEM((3, STARS), F32)] * 4 + [pltpu.VMEM((TILES, LANES), F32)] * 2
        + star_scratch + [
            pltpu.VMEM((8, LANES), F32),
            pltpu.VMEM((GROUP - 1, 8, LANES), F32),
        ] + force_scratch(ROOM) + [
            pltpu.SemaphoreType.DMA((6,)),
            pltpu.SemaphoreType.DMA((4,)),
            pltpu.SemaphoreType.DMA((5,)),
        ],
        compiler_params=pltpu.CompilerParams(
            collective_id=0, has_side_effects=True, vmem_limit_bytes=56 * 2**20),
        name="fast",
    )(active_index, active_count, position, velocity, accel_old, jerk_old, mass, elapsed.reshape(TILES, LANES))

    def general():
        return pl.pallas_call(
            general_kernel,
            out_shape=jax.ShapeDtypeStruct((8, LANES), F32),
            in_specs=[smem] + [vmem] * 3,
            out_specs=vmem,
            scratch_shapes=star_scratch + force_scratch(SLOTS) + [
                pltpu.SemaphoreType.DMA((2,)),
                pltpu.SemaphoreType.DMA((2,)),
            ],
            compiler_params=pltpu.CompilerParams(
                collective_id=1, has_side_effects=True, vmem_limit_bytes=32 * 2**20),
            name="general",
        )(active_count, mass, stars, everyone)

    mine = lax.cond(choice[0] > 0, general, lambda: mine)
    return pl.pallas_call(
        finish_kernel,
        out_shape=(jax.ShapeDtypeStruct((3, ACT), F32), jax.ShapeDtypeStruct((3, ACT), F32)),
        in_specs=[vmem],
        out_specs=(vmem, vmem),
        name="finish",
    )(mine)


def solution(mesh):
    split = P(None, ("row", "col"))
    flat = P(("row", "col"))
    return jax.shard_map(
        local,
        mesh=mesh,
        in_specs=(split, split, split, split, flat, flat, flat, flat),
        out_specs=(split, split),
        check_vma=False,
    )
```

```python
import functools

import jax
import jax.numpy as jnp
from jax import lax
from jax.experimental import pallas as pl
from jax.experimental.pallas import tpu as pltpu
from jax.sharding import PartitionSpec as P

SOFTENING = 0.0025
MESH = pl.DeviceIdType.MESH
F32, BF16 = jnp.float32, jnp.bfloat16
LANES = 128
GROUP = 16
ACT = 8
STARS = 4096
TILES = STARS // LANES
BLOCK = 256
SIZES = ((3, 2), (4, 2), (8, 8))


def ring(size, step):
    return min(step % size, -step % size)


ZC_STEPS = sorted(range(1, GROUP), key=lambda step: -ring(8, step // 2))
XY_STEPS = sorted(((i // 4, i % 4) for i in range(1, GROUP)), key=lambda at: -ring(4, at[0]) - ring(4, at[1]))
FAR = 9
LAST_FAR = XY_STEPS[FAR - 1]


def place():
    row = lax.axis_index("row")
    col = lax.axis_index("col")
    z, y_lo, core = col >> 2, (col >> 1) & 1, col & 1
    return row, z, y_lo, core, z * 2 + core, row * 2 + y_lo


def zc_peers():
    row, z, y_lo, core, zc, xy = place()
    peers = []
    for step in ZC_STEPS:
        peer = (zc + step) & (GROUP - 1)
        peers.append((peer, (row, (peer >> 1) * 4 + y_lo * 2 + (peer & 1))))
    return peers


def xy_peers():
    row, z, y_lo, core, zc, xy = place()
    rows = [((row >> 1) + step) & 3 for step in range(4)]
    columns = [((row & 1) * 2 + y_lo + step) & 3 for step in range(4)]
    peers = []
    for step in XY_STEPS:
        x, y = rows[step[0]], columns[step[1]]
        peers.append((x * 4 + y, (x * 2 + (y >> 1), z * 4 + (y & 1) * 2 + core)))
    return peers


def distances(tile, centre):
    x, y = ((tile >> 2) - (centre >> 2)) & 3, ((tile & 3) - (centre & 3)) & 3
    return jnp.minimum(x, 4 - x) + jnp.minimum(y, 4 - y), x * 4 + y


def greet():
    barrier = pltpu.get_barrier_semaphore()
    for peer, device in zc_peers() + xy_peers():
        pl.semaphore_signal(barrier, inc=1, device_id=device, device_id_type=MESH)


def await_greetings():
    pl.semaphore_wait(pltpu.get_barrier_semaphore(), 2 * (GROUP - 1))


def wait_bytes(ref, sem):
    pltpu.make_async_copy(ref, ref, sem).wait()


def mm(a, b):
    return jnp.dot(a, b, preferred_element_type=F32)


def mm_t(a, b):
    return lax.dot_general(a, b, (((1,), (1,)), ((), ())), preferred_element_type=F32)


def pieces(value):
    first = value.astype(BF16).astype(F32)
    rest = value - first
    second = rest.astype(BF16).astype(F32)
    return first, second, rest - second


def coordinates(group):
    coarse = jnp.floor(group * 16.0 + 0.5) * 0.0625
    return coarse, pieces(group - coarse)


def scalars(group, coarse, shift):
    sub = lax.broadcasted_iota(jnp.int32, group.shape, 0)
    upper = sub < 3

    def pair(exact, whole):
        exact = jnp.sum(jnp.where(upper, exact, 0.0), axis=0, keepdims=True)
        whole = jnp.sum(jnp.where(upper, whole, 0.0), axis=0, keepdims=True)
        high = exact.astype(BF16).astype(F32)
        return (high, exact - high) + pieces(whole)

    fine = group - coarse
    vel, vel_coarse = pltpu.roll(group, 4, 0), pltpu.roll(coarse, 4, 0)
    square = pair(coarse * coarse, fine * (group + coarse) + jnp.where(sub == 0, shift, 0.0))
    cross = pair(coarse * vel_coarse, fine * vel + coarse * (vel - vel_coarse))
    return square, cross


def stack(rows, shape):
    sub = lax.broadcasted_iota(jnp.int32, shape, 0)
    total = jnp.zeros(shape, F32)
    for at, row in enumerate(rows):
        total = jnp.where(sub == at, row, total)
    return total


def source_features(group):
    coarse, (one, two, three) = coordinates(group)
    square, cross = scalars(group, coarse, 0.0)
    exact = stack(square[0:2] + (1.0, 1.0) + cross[0:2] + (1.0, 1.0), group.shape)
    rest = stack(square[2:5] + (1.0,) + cross[2:5] + (1.0,), group.shape)
    more = stack((1.0, 1.0, 0.0, 0.0, 1.0, 1.0, 0.0, 0.0), group.shape)
    none = jnp.zeros_like(group)
    return [exact, coarse, rest, more, coarse, coarse, coarse, one, two, three, one, one, two, two, none, none]


def target_features(group):
    coarse, (one, two, three) = coordinates(group)
    square, cross = scalars(group, coarse, SOFTENING)
    sub = lax.broadcasted_iota(jnp.int32, group.shape, 0)
    none = jnp.zeros_like(group)

    def tail(scalar, at):
        pad, rest = (0.0,) * at, (0.0,) * (4 - at)
        exact = stack(pad + (1.0, 1.0) + scalar[0:2] + rest, group.shape)
        fine = stack(pad + (1.0, 1.0, 1.0) + scalar[2:3] + rest, group.shape)
        more = stack(pad + scalar[3:5] + (0.0, 0.0) + rest, group.shape)
        return exact, fine, more

    def weights(change, scalar, at):
        exact, fine, more = tail(scalar, at)
        c, o, t, h = change(coarse), change(one), change(two), change(three)
        rows = [exact, c, fine, more, o, t, h, c, c, c, o, t, o, t, none, none]
        return jnp.concatenate(rows, 0).astype(BF16)

    near = weights(lambda v: jnp.where(sub < 3, -2.0 * v, 0.0), square, 0)
    along = weights(lambda v: -pltpu.roll(v, 4, 0), cross, 4)
    return near, along


def prepare_tile(tile, stars, mass_ref, feature_ref, moment_ref):
    cols = pl.ds(pl.multiple_of(tile * LANES, LANES), LANES)
    group = stars[:, cols]
    rows = jnp.concatenate(source_features(group), 0)
    feature_ref[cols, :] = rows.T.astype(BF16)
    sub = lax.broadcasted_iota(jnp.int32, group.shape, 0)
    moment = mass_ref[pl.ds(tile, 1), :] * jnp.where(sub == 3, 1.0, group)
    one, two, three = pieces(moment)
    moment_ref[:, cols] = jnp.concatenate([one, two, three, jnp.zeros_like(one)], 0).astype(BF16)


def gather_kernel(index_ref, count_ref, pos_hbm, vel_hbm, acc_hbm, jerk_hbm, mass_hbm, elapsed_hbm,
                  feature_ref, moment_ref, all_ref, rank_ref, choice_ref,
                  pos_ref, vel_ref, acc_ref, jerk_ref, mass_ref, elapsed_ref,
                  stars, mine, near, load_sem, send_sem, recv_sem):
    loads = [
        pltpu.make_async_copy(src, dst, load_sem.at[at])
        for at, (src, dst) in enumerate((
            (pos_hbm, pos_ref), (vel_hbm, vel_ref), (acc_hbm, acc_ref), (jerk_hbm, jerk_ref),
            (mass_hbm, mass_ref), (elapsed_hbm, elapsed_ref)))
    ]
    for load in loads:
        load.start()
    row, z, y_lo, core, zc, xy = place()
    greet()
    for load in loads:
        load.wait()
    stars[...] = jnp.zeros_like(stars)
    for tile in range(TILES):
        cols = pl.ds(tile * LANES, LANES)
        dt = elapsed_ref[tile:tile + 1, :]
        vel, acc, jerk = vel_ref[:, cols], acc_ref[:, cols], jerk_ref[:, cols]
        stars[0:3, cols] = pos_ref[:, cols] + dt * (vel + dt * (0.5 * acc + dt * (jerk * (1.0 / 6.0))))
        stars[4:7, cols] = vel + dt * (acc + dt * (0.5 * jerk))
    lane = lax.broadcasted_iota(jnp.int32, (8, LANES), 1)
    sub = lax.broadcasted_iota(jnp.int32, (8, LANES), 0)
    total = jnp.zeros((8, LANES), F32)
    for slot in range(ACT):
        away = lane - index_ref[slot]
        picked = jnp.zeros((8, LANES), F32)
        for tile in range(TILES):
            picked = jnp.where(away == -tile * LANES, stars[:, pl.ds(tile * LANES, LANES)], picked)
        value = jnp.sum(picked, axis=1, keepdims=True)
        value = jnp.where(sub == 3, jnp.where(slot < count_ref[0], 1.0, 0.0), value)
        total = jnp.where(lane == zc * ACT + slot, value, total)
    mine[...] = total
    await_greetings()
    for at, (peer, device) in enumerate(zc_peers()):
        pltpu.make_async_remote_copy(
            src_ref=mine, dst_ref=near.at[at],
            send_sem=send_sem.at[0], recv_sem=recv_sem.at[0],
            device_id=device, device_id_type=MESH).start()

    def prepare(tile, carry):
        prepare_tile(tile, stars, mass_ref, feature_ref, moment_ref)
        return carry

    lax.fori_loop(0, TILES // 2, prepare, 0, unroll=2)
    wait_bytes(near, recv_sem.at[0])
    for step in range(1, GROUP):
        total = total + near[step - 1]
    all_ref[pl.ds(xy, 1)] = total[None]
    for peer, device in xy_peers():
        pltpu.make_async_remote_copy(
            src_ref=all_ref.at[xy], dst_ref=all_ref.at[xy],
            send_sem=send_sem.at[1], recv_sem=recv_sem.at[1],
            device_id=device, device_id_type=MESH).start()
    lax.fori_loop(TILES // 2, TILES, prepare, 0, unroll=2)
    wait_bytes(near, send_sem.at[0])
    wait_bytes(near, recv_sem.at[1])
    alive = jnp.concatenate([all_ref[g, 3:4, :] for g in range(GROUP)], 0)
    before = lax.broadcasted_iota(jnp.int32, (LANES, LANES), 0)
    after = lax.broadcasted_iota(jnp.int32, (LANES, LANES), 1)
    inside = mm(alive.astype(BF16), jnp.where(before < after, 1.0, 0.0).astype(BF16))
    sums = mm(alive.astype(BF16), jnp.ones((LANES, LANES), BF16))
    tile = lax.broadcasted_iota(jnp.int32, (GROUP, GROUP), 0)
    other = lax.broadcasted_iota(jnp.int32, (GROUP, GROUP), 1)
    (hops, step), (other_hops, other_step) = distances(tile, xy), distances(other, xy)
    earlier = other_step - GROUP * other_hops < step - GROUP * hops
    ahead = mm(jnp.where(earlier, 1.0, 0.0).astype(BF16), sums.astype(BF16))
    hops, step = distances(other, tile)
    last_hops, last_step = ring(4, LAST_FAR[0]) + ring(4, LAST_FAR[1]), LAST_FAR[0] * 4 + LAST_FAR[1]
    far = step - GROUP * hops <= last_step - GROUP * last_hops
    far = mm(jnp.where(far, 1.0, 0.0).astype(BF16), sums.astype(BF16))
    first = ahead - LANES * jnp.floor(ahead * (1.0 / LANES))
    lead = inside + first
    rank_ref[0] = jnp.where(alive > 0.0, lead - LANES * jnp.floor(lead * (1.0 / LANES)), -1.0)
    spot = lax.broadcasted_iota(jnp.int32, (GROUP, LANES), 1).astype(F32)
    rank_ref[1] = jnp.floor(ahead * (1.0 / LANES)) + jnp.where(spot < first, 1.0, 0.0)
    live = jnp.max(ahead + sums, axis=0, keepdims=True)
    far = jnp.max(far, axis=0, keepdims=True)
    choice = jnp.full((1, LANES), len(SIZES) - 1.0, F32)
    for at in reversed(range(len(SIZES) - 1)):
        blocks, early = SIZES[at]
        choice = jnp.where((live <= blocks * BLOCK) & (far <= early * BLOCK), float(at), choice)
    choice_ref[0] = choice[0, 0].astype(jnp.int32)
    wait_bytes(near, send_sem.at[1])


def three_rows(group):
    return jnp.concatenate(list(pieces(group)) + [jnp.zeros_like(group)], 0).astype(BF16)


def joined(rows):
    return rows[0:8] + rows[8:16] + rows[16:24]


def force_kernel(blocks, early, count_ref, feature_ref, moment_ref, all_ref, rank_ref, out_ref,
                 part_ref, hot, near_ref, along_ref, target_ref, force_ref,
                 first, second, summed, send_sem, recv_sem):
    greet()
    tiles = blocks * BLOCK // LANES
    spot = lax.broadcasted_iota(jnp.int32, (LANES, LANES), 0).astype(F32)
    packed = [jnp.zeros((8, LANES), F32)] * tiles
    for g in range(GROUP):
        hot[g] = jnp.where(spot == rank_ref[0, g:g + 1, :], 1.0, 0.0).astype(BF16)
        chosen = joined(mm_t(three_rows(all_ref[g]), hot[g]))
        tile = rank_ref[1, g:g + 1, :]
        packed = [old + jnp.where(tile == at, chosen, 0.0) for at, old in enumerate(packed)]
    row_id = lax.broadcasted_iota(jnp.int32, (8, LANES), 0)
    for at in range(tiles):
        cols = pl.ds(at * LANES, LANES)
        target_ref[:, cols] = jnp.where((row_id == 3) | (row_id == 7), 0.0, packed[at])

    def weigh(cols):
        near_ref[:, cols], along_ref[:, cols] = target_features(target_ref[:, cols])

    weigh(pl.ds(0, BLOCK))
    sub = lax.broadcasted_iota(jnp.int32, (8, BLOCK), 0)

    def block(index, carry):
        cols = pl.ds(pl.multiple_of(index * BLOCK, BLOCK), BLOCK)
        r2 = mm(feature_ref[...], near_ref[:, cols])
        dot = mm(feature_ref[...], along_ref[:, cols])
        inv = lax.rsqrt(r2)
        inv2 = inv * inv
        w = inv * inv2
        u = (w * inv2) * dot
        sums = []
        for value in (w, u):
            high = value.astype(BF16)
            low = (value - high.astype(F32)).astype(BF16)
            sums.append(joined(mm(moment_ref[...], high) + mm(moment_ref[...], low)))
        target = target_ref[:, cols]
        by_w, by_u = [total - target * total[3:4, :] for total in sums]
        force_ref[:, cols] = by_w - 3.0 * jnp.where(sub >= 4, pltpu.roll(by_u, 4, 0), 0.0)
        weigh(pl.ds(pl.multiple_of(lax.rem(index + 1, blocks) * BLOCK, BLOCK), BLOCK))
        return carry

    def unpack(peer, done):
        tile = rank_ref[1, pl.ds(peer, 1), :]
        chosen = jnp.zeros((8, LANES), F32)
        for at in range(done * BLOCK // LANES):
            chosen = jnp.where(tile == at, force_ref[:, at * LANES:(at + 1) * LANES], chosen)
        part_ref[peer] = joined(mm(three_rows(chosen), hot[peer]))

    def send(at, peer, device):
        pltpu.make_async_remote_copy(
            src_ref=part_ref.at[peer], dst_ref=first.at[at],
            send_sem=send_sem.at[0], recv_sem=recv_sem.at[0],
            device_id=device, device_id_type=MESH).start()

    row, z, y_lo, core, zc, xy = place()
    peers = xy_peers()

    def send_far():
        for peer, device in peers[:FAR]:
            unpack(peer, early)
        await_greetings()
        for at in range(FAR):
            send(at, *peers[at])

    def step(index, carry):
        pl.when(index == early)(send_far)
        return block(index, carry)

    lax.fori_loop(0, blocks, step, 0)
    if early == blocks:
        send_far()
    for peer, device in peers[FAR:]:
        unpack(peer, blocks)
    for at in range(FAR, GROUP - 1):
        send(at, *peers[at])
    unpack(xy, blocks)
    total = part_ref[xy]
    wait_bytes(first, recv_sem.at[0])
    for step in range(1, GROUP):
        total = total + first[step - 1]
    summed[...] = total
    for at, (peer, device) in enumerate(zc_peers()):
        pltpu.make_async_remote_copy(
            src_ref=summed, dst_ref=second.at[at],
            send_sem=send_sem.at[1], recv_sem=recv_sem.at[1],
            device_id=device, device_id_type=MESH).start()
    wait_bytes(second, recv_sem.at[1])
    for step in range(1, GROUP):
        total = total + second[step - 1]
    mine = pltpu.roll(total, lax.rem(LANES - zc * ACT, LANES), 1)
    lane = lax.broadcasted_iota(jnp.int32, (8, LANES), 1)
    out_ref[...] = jnp.where(lane < count_ref[0], mine, 0.0)
    wait_bytes(first, send_sem.at[0])
    wait_bytes(second, send_sem.at[1])


def finish_kernel(force_ref, accel_ref, jerk_ref):
    accel_ref[...] = force_ref[0:3, 0:ACT]
    jerk_ref[...] = force_ref[4:7, 0:ACT]


def local(position, velocity, accel_old, jerk_old, mass, elapsed, active_index, active_count):
    vmem = pl.BlockSpec(memory_space=pltpu.VMEM)
    smem = pl.BlockSpec(memory_space=pltpu.SMEM)
    hbm = pl.BlockSpec(memory_space=pltpu.HBM)
    tiles = (GROUP, 8, LANES)
    features, moments, everyone, rank, choice = pl.pallas_call(
        gather_kernel,
        out_shape=(
            jax.ShapeDtypeStruct((STARS, LANES), BF16),
            jax.ShapeDtypeStruct((32, STARS), BF16),
            jax.ShapeDtypeStruct(tiles, F32),
            jax.ShapeDtypeStruct((2, GROUP, LANES), F32),
            jax.ShapeDtypeStruct((1,), jnp.int32),
        ),
        in_specs=[smem, smem] + [hbm] * 6,
        out_specs=(vmem,) * 4 + (smem,),
        scratch_shapes=[pltpu.VMEM((3, STARS), F32)] * 4 + [pltpu.VMEM((TILES, LANES), F32)] * 2 + [
            pltpu.VMEM((8, STARS), F32),
            pltpu.VMEM((8, LANES), F32),
            pltpu.VMEM((GROUP - 1, 8, LANES), F32),
            pltpu.SemaphoreType.DMA((6,)),
            pltpu.SemaphoreType.DMA((2,)),
            pltpu.SemaphoreType.DMA((2,)),
        ],
        compiler_params=pltpu.CompilerParams(
            collective_id=0, has_side_effects=True, vmem_limit_bytes=56 * 2**20),
        name="gather_targets",
    )(active_index, active_count, position, velocity, accel_old, jerk_old,
      mass.reshape(TILES, LANES), elapsed.reshape(TILES, LANES))

    def forces(at):
        return pl.pallas_call(
            functools.partial(force_kernel, *SIZES[at]),
            out_shape=jax.ShapeDtypeStruct((8, LANES), F32),
            in_specs=[smem] + [vmem] * 4,
            out_specs=vmem,
            scratch_shapes=[
                pltpu.VMEM(tiles, F32),
                pltpu.VMEM((GROUP, LANES, LANES), BF16),
                pltpu.VMEM((LANES, SIZES[at][0] * BLOCK), BF16),
                pltpu.VMEM((LANES, SIZES[at][0] * BLOCK), BF16),
                pltpu.VMEM((8, SIZES[at][0] * BLOCK), F32),
                pltpu.VMEM((8, SIZES[at][0] * BLOCK), F32),
                pltpu.VMEM((GROUP - 1, 8, LANES), F32),
                pltpu.VMEM((GROUP - 1, 8, LANES), F32),
                pltpu.VMEM((8, LANES), F32),
                pltpu.SemaphoreType.DMA((2,)),
                pltpu.SemaphoreType.DMA((2,)),
            ],
            compiler_params=pltpu.CompilerParams(
                collective_id=1 + at, has_side_effects=True, vmem_limit_bytes=24 * 2**20),
            name="forces_%d" % SIZES[at][0],
        )

    branches = [forces(at) for at in range(len(SIZES))]
    mine = lax.switch(choice[0], branches, active_count, features, moments, everyone, rank)
    return pl.pallas_call(
        finish_kernel,
        out_shape=(jax.ShapeDtypeStruct((3, ACT), F32), jax.ShapeDtypeStruct((3, ACT), F32)),
        in_specs=[vmem],
        out_specs=(vmem, vmem),
        name="finish",
    )(mine)


def solution(mesh):
    split = P(None, ("row", "col"))
    flat = P(("row", "col"))
    return jax.shard_map(
        local,
        mesh=mesh,
        in_specs=(split, split, split, split, flat, flat, flat, flat),
        out_specs=(split, split),
        check_vma=False,
    )
```

```python
import functools

import jax
import jax.numpy as jnp
from jax import lax
from jax.experimental import pallas as pl
from jax.experimental.pallas import tpu as pltpu
from jax.sharding import PartitionSpec as P

SOFTENING = 0.0025
MESH = pl.DeviceIdType.MESH
F32, BF16 = jnp.float32, jnp.bfloat16
LANES = 128
GROUP = 16
ACT = 8
STARS = 4096
TILES = STARS // LANES
BLOCK = 256
SIZES = ((3, 2), (4, 2), (8, 8))


def ring(size, step):
    return min(step % size, -step % size)


ZC_STEPS = sorted(range(1, GROUP), key=lambda step: -ring(8, step // 2))
XY_STEPS = sorted(((i // 4, i % 4) for i in range(1, GROUP)), key=lambda at: -ring(4, at[0]) - ring(4, at[1]))
FAR = 9
LAST_FAR = XY_STEPS[FAR - 1]


def place():
    row = lax.axis_index("row")
    col = lax.axis_index("col")
    z, y_lo, core = col >> 2, (col >> 1) & 1, col & 1
    return row, z, y_lo, core, z * 2 + core, row * 2 + y_lo


def zc_peers():
    row, z, y_lo, core, zc, xy = place()
    peers = []
    for step in ZC_STEPS:
        peer = (zc + step) & (GROUP - 1)
        peers.append((peer, (row, (peer >> 1) * 4 + y_lo * 2 + (peer & 1))))
    return peers


def xy_peers():
    row, z, y_lo, core, zc, xy = place()
    rows = [((row >> 1) + step) & 3 for step in range(4)]
    columns = [((row & 1) * 2 + y_lo + step) & 3 for step in range(4)]
    peers = []
    for step in XY_STEPS:
        x, y = rows[step[0]], columns[step[1]]
        peers.append((x * 4 + y, (x * 2 + (y >> 1), z * 4 + (y & 1) * 2 + core)))
    return peers


def distances(tile, centre):
    x, y = ((tile >> 2) - (centre >> 2)) & 3, ((tile & 3) - (centre & 3)) & 3
    return jnp.minimum(x, 4 - x) + jnp.minimum(y, 4 - y), x * 4 + y


def greet():
    barrier = pltpu.get_barrier_semaphore()
    for peer, device in zc_peers() + xy_peers():
        pl.semaphore_signal(barrier, inc=1, device_id=device, device_id_type=MESH)


def await_greetings():
    pl.semaphore_wait(pltpu.get_barrier_semaphore(), 2 * (GROUP - 1))


def wait_bytes(ref, sem):
    pltpu.make_async_copy(ref, ref, sem).wait()


def mm(a, b):
    return jnp.dot(a, b, preferred_element_type=F32)


def mm_t(a, b):
    return lax.dot_general(a, b, (((1,), (1,)), ((), ())), preferred_element_type=F32)


def pieces(value):
    first = value.astype(BF16).astype(F32)
    rest = value - first
    second = rest.astype(BF16).astype(F32)
    return first, second, rest - second


def coordinates(group):
    coarse = jnp.floor(group * 16.0 + 0.5) * 0.0625
    return coarse, pieces(group - coarse)


def scalars(group, coarse, shift):
    sub = lax.broadcasted_iota(jnp.int32, group.shape, 0)
    upper = sub < 3

    def pair(exact, whole):
        exact = jnp.sum(jnp.where(upper, exact, 0.0), axis=0, keepdims=True)
        whole = jnp.sum(jnp.where(upper, whole, 0.0), axis=0, keepdims=True)
        high = exact.astype(BF16).astype(F32)
        return (high, exact - high) + pieces(whole)

    fine = group - coarse
    vel, vel_coarse = pltpu.roll(group, 4, 0), pltpu.roll(coarse, 4, 0)
    square = pair(coarse * coarse, fine * (group + coarse) + jnp.where(sub == 0, shift, 0.0))
    cross = pair(coarse * vel_coarse, fine * vel + coarse * (vel - vel_coarse))
    return square, cross


def stack(rows, shape):
    sub = lax.broadcasted_iota(jnp.int32, shape, 0)
    total = jnp.zeros(shape, F32)
    for at, row in enumerate(rows):
        total = jnp.where(sub == at, row, total)
    return total


def source_features(group):
    coarse, (one, two, three) = coordinates(group)
    square, cross = scalars(group, coarse, 0.0)
    exact = stack(square[0:2] + (1.0, 1.0) + cross[0:2] + (1.0, 1.0), group.shape)
    rest = stack(square[2:5] + (1.0,) + cross[2:5] + (1.0,), group.shape)
    more = stack((1.0, 1.0, 0.0, 0.0, 1.0, 1.0, 0.0, 0.0), group.shape)
    none = jnp.zeros_like(group)
    return [exact, coarse, rest, more, coarse, coarse, coarse, one, two, three, one, one, two, two, none, none]


def target_features(group):
    coarse, (one, two, three) = coordinates(group)
    square, cross = scalars(group, coarse, SOFTENING)
    sub = lax.broadcasted_iota(jnp.int32, group.shape, 0)
    none = jnp.zeros_like(group)

    def tail(scalar, at):
        pad, rest = (0.0,) * at, (0.0,) * (4 - at)
        exact = stack(pad + (1.0, 1.0) + scalar[0:2] + rest, group.shape)
        fine = stack(pad + (1.0, 1.0, 1.0) + scalar[2:3] + rest, group.shape)
        more = stack(pad + scalar[3:5] + (0.0, 0.0) + rest, group.shape)
        return exact, fine, more

    def weights(change, scalar, at):
        exact, fine, more = tail(scalar, at)
        c, o, t, h = change(coarse), change(one), change(two), change(three)
        rows = [exact, c, fine, more, o, t, h, c, c, c, o, t, o, t, none, none]
        return jnp.concatenate(rows, 0).astype(BF16)

    near = weights(lambda v: jnp.where(sub < 3, -2.0 * v, 0.0), square, 0)
    along = weights(lambda v: -pltpu.roll(v, 4, 0), cross, 4)
    return near, along


def prepare_tile(tile, stars, mass_ref, feature_ref, moment_ref):
    cols = pl.ds(pl.multiple_of(tile * LANES, LANES), LANES)
    group = stars[:, cols]
    rows = jnp.concatenate(source_features(group), 0)
    feature_ref[cols, :] = rows.T.astype(BF16)
    sub = lax.broadcasted_iota(jnp.int32, group.shape, 0)
    moment = mass_ref[pl.ds(tile, 1), :] * jnp.where(sub == 3, 1.0, group)
    one, two, three = pieces(moment)
    moment_ref[:, cols] = jnp.concatenate([one, two, three, jnp.zeros_like(one)], 0).astype(BF16)


def gather_kernel(index_ref, count_ref, pos_hbm, vel_hbm, acc_hbm, jerk_hbm, mass_hbm, elapsed_hbm,
                  feature_ref, moment_ref, all_ref, rank_ref, choice_ref,
                  pos_ref, vel_ref, acc_ref, jerk_ref, mass_ref, elapsed_ref,
                  stars, mine, near, load_sem, send_sem, recv_sem):
    loads = [
        pltpu.make_async_copy(src, dst, load_sem.at[at])
        for at, (src, dst) in enumerate((
            (pos_hbm, pos_ref), (vel_hbm, vel_ref), (acc_hbm, acc_ref), (jerk_hbm, jerk_ref),
            (mass_hbm, mass_ref), (elapsed_hbm, elapsed_ref)))
    ]
    for load in loads:
        load.start()
    row, z, y_lo, core, zc, xy = place()
    greet()
    for load in loads:
        load.wait()
    stars[...] = jnp.zeros_like(stars)
    for tile in range(TILES):
        cols = pl.ds(tile * LANES, LANES)
        dt = elapsed_ref[tile:tile + 1, :]
        vel, acc, jerk = vel_ref[:, cols], acc_ref[:, cols], jerk_ref[:, cols]
        stars[0:3, cols] = pos_ref[:, cols] + dt * (vel + dt * (0.5 * acc + dt * (jerk * (1.0 / 6.0))))
        stars[4:7, cols] = vel + dt * (acc + dt * (0.5 * jerk))
    lane = lax.broadcasted_iota(jnp.int32, (8, LANES), 1)
    sub = lax.broadcasted_iota(jnp.int32, (8, LANES), 0)
    total = jnp.zeros((8, LANES), F32)
    for slot in range(ACT):
        away = lane - index_ref[slot]
        picked = jnp.zeros((8, LANES), F32)
        for tile in range(TILES):
            picked = jnp.where(away == -tile * LANES, stars[:, pl.ds(tile * LANES, LANES)], picked)
        value = jnp.sum(picked, axis=1, keepdims=True)
        value = jnp.where(sub == 3, jnp.where(slot < count_ref[0], 1.0, 0.0), value)
        total = jnp.where(lane == zc * ACT + slot, value, total)
    mine[...] = total
    await_greetings()
    for at, (peer, device) in enumerate(zc_peers()):
        pltpu.make_async_remote_copy(
            src_ref=mine, dst_ref=near.at[at],
            send_sem=send_sem.at[0], recv_sem=recv_sem.at[0],
            device_id=device, device_id_type=MESH).start()

    def prepare(tile, carry):
        prepare_tile(tile, stars, mass_ref, feature_ref, moment_ref)
        return carry

    lax.fori_loop(0, TILES // 2, prepare, 0, unroll=2)
    wait_bytes(near, recv_sem.at[0])
    for step in range(1, GROUP):
        total = total + near[step - 1]
    all_ref[pl.ds(xy, 1)] = total[None]
    for peer, device in xy_peers():
        pltpu.make_async_remote_copy(
            src_ref=all_ref.at[xy], dst_ref=all_ref.at[xy],
            send_sem=send_sem.at[1], recv_sem=recv_sem.at[1],
            device_id=device, device_id_type=MESH).start()
    lax.fori_loop(TILES // 2, TILES, prepare, 0, unroll=2)
    wait_bytes(near, send_sem.at[0])
    wait_bytes(near, recv_sem.at[1])
    alive = jnp.concatenate([all_ref[g, 3:4, :] for g in range(GROUP)], 0)
    before = lax.broadcasted_iota(jnp.int32, (LANES, LANES), 0)
    after = lax.broadcasted_iota(jnp.int32, (LANES, LANES), 1)
    inside = mm(alive.astype(BF16), jnp.where(before < after, 1.0, 0.0).astype(BF16))
    sums = mm(alive.astype(BF16), jnp.ones((LANES, LANES), BF16))
    tile = lax.broadcasted_iota(jnp.int32, (GROUP, GROUP), 0)
    other = lax.broadcasted_iota(jnp.int32, (GROUP, GROUP), 1)
    (hops, step), (other_hops, other_step) = distances(tile, xy), distances(other, xy)
    earlier = other_step - GROUP * other_hops < step - GROUP * hops
    ahead = mm(jnp.where(earlier, 1.0, 0.0).astype(BF16), sums.astype(BF16))
    hops, step = distances(other, tile)
    last_hops, last_step = ring(4, LAST_FAR[0]) + ring(4, LAST_FAR[1]), LAST_FAR[0] * 4 + LAST_FAR[1]
    far = step - GROUP * hops <= last_step - GROUP * last_hops
    far = mm(jnp.where(far, 1.0, 0.0).astype(BF16), sums.astype(BF16))
    first = ahead - LANES * jnp.floor(ahead * (1.0 / LANES))
    lead = inside + first
    rank_ref[0] = jnp.where(alive > 0.0, lead - LANES * jnp.floor(lead * (1.0 / LANES)), -1.0)
    spot = lax.broadcasted_iota(jnp.int32, (GROUP, LANES), 1).astype(F32)
    rank_ref[1] = jnp.floor(ahead * (1.0 / LANES)) + jnp.where(spot < first, 1.0, 0.0)
    live = jnp.max(ahead + sums, axis=0, keepdims=True) - jnp.min(sums, axis=0, keepdims=True)
    far = jnp.max(far, axis=0, keepdims=True)
    choice = jnp.full((1, LANES), len(SIZES) - 1.0, F32)
    for at in reversed(range(len(SIZES) - 1)):
        blocks, early = SIZES[at]
        choice = jnp.where((live <= blocks * BLOCK) & (far <= early * BLOCK), float(at), choice)
    choice_ref[0] = choice[0, 0].astype(jnp.int32)
    wait_bytes(near, send_sem.at[1])


def three_rows(group):
    return jnp.concatenate(list(pieces(group)) + [jnp.zeros_like(group)], 0).astype(BF16)


def joined(rows):
    return rows[0:8] + rows[8:16] + rows[16:24]


def pair_weights(r2, dot):
    inv = lax.rsqrt(r2)
    inv2 = inv * inv
    w = inv * inv2
    out = []
    for value in (w, (w * inv2) * dot):
        high = value.astype(BF16)
        out.append((high, (value - high.astype(F32)).astype(BF16)))
    return out


def force_of(by_w, by_u, target):
    sub = lax.broadcasted_iota(jnp.int32, target.shape, 0)
    by_w, by_u = by_w - target * by_w[3:4, :], by_u - target * by_u[3:4, :]
    return by_w - 3.0 * jnp.where(sub >= 4, pltpu.roll(by_u, 4, 0), 0.0)


def force_kernel(blocks, early, count_ref, feature_ref, moment_ref, all_ref, rank_ref, out_ref,
                 part_ref, hot, near_ref, along_ref, target_ref, force_ref,
                 first, second, summed, send_sem, recv_sem):
    greet()
    tiles = blocks * BLOCK // LANES
    spot = lax.broadcasted_iota(jnp.int32, (LANES, LANES), 0).astype(F32)
    packed = [jnp.zeros((8, LANES), F32)] * tiles
    for g in range(GROUP):
        hot[g] = jnp.where(spot == rank_ref[0, g:g + 1, :], 1.0, 0.0).astype(BF16)
        chosen = joined(mm_t(three_rows(all_ref[g]), hot[g]))
        tile = rank_ref[1, g:g + 1, :]
        packed = [old + jnp.where(tile == at, chosen, 0.0) for at, old in enumerate(packed)]
    row_id = lax.broadcasted_iota(jnp.int32, (8, LANES), 0)
    for at in range(tiles):
        cols = pl.ds(at * LANES, LANES)
        target_ref[:, cols] = jnp.where((row_id == 3) | (row_id == 7), 0.0, packed[at])

    def weigh(cols):
        near_ref[:, cols], along_ref[:, cols] = target_features(target_ref[:, cols])

    weigh(pl.ds(0, BLOCK))

    def block(index, carry):
        cols = pl.ds(pl.multiple_of(index * BLOCK, BLOCK), BLOCK)
        r2 = mm(feature_ref[...], near_ref[:, cols])
        dot = mm(feature_ref[...], along_ref[:, cols])
        sums = [joined(mm(moment_ref[...], high) + mm(moment_ref[...], low)) for high, low in pair_weights(r2, dot)]
        force_ref[:, cols] = force_of(*sums, target_ref[:, cols])
        weigh(pl.ds(pl.multiple_of(lax.rem(index + 1, blocks) * BLOCK, BLOCK), BLOCK))
        return carry

    def unpack(peer, done):
        tile = rank_ref[1, pl.ds(peer, 1), :]
        chosen = jnp.zeros((8, LANES), F32)
        for at in range(done * BLOCK // LANES):
            chosen = jnp.where(tile == at, force_ref[:, at * LANES:(at + 1) * LANES], chosen)
        part_ref[peer] = joined(mm(three_rows(chosen), hot[peer]))

    def send(at, peer, device):
        pltpu.make_async_remote_copy(
            src_ref=part_ref.at[peer], dst_ref=first.at[at],
            send_sem=send_sem.at[0], recv_sem=recv_sem.at[0],
            device_id=device, device_id_type=MESH).start()

    row, z, y_lo, core, zc, xy = place()
    peers = xy_peers()

    def send_far():
        for peer, device in peers[:FAR]:
            unpack(peer, early)
        await_greetings()
        for at in range(FAR):
            send(at, *peers[at])

    def step(index, carry):
        pl.when(index == early)(send_far)
        return block(index, carry)

    lax.fori_loop(0, blocks, step, 0)
    if early == blocks:
        send_far()
    for at in range(FAR, GROUP - 1):
        unpack(peers[at][0], blocks)
        send(at, *peers[at])
    target = jnp.where((row_id == 3) | (row_id == 7), 0.0, all_ref[xy])
    both = mm(feature_ref[...], jnp.concatenate(target_features(target), 1))
    sums = []
    for high, low in pair_weights(both[:, :LANES], both[:, LANES:]):
        halves = mm(moment_ref[...], jnp.concatenate([high, low], 1))
        sums.append(joined(halves[:, :LANES] + halves[:, LANES:]))
    total = force_of(*sums, target)
    wait_bytes(first, recv_sem.at[0])
    for step in range(1, GROUP):
        total = total + first[step - 1]
    summed[...] = total
    for at, (peer, device) in enumerate(zc_peers()):
        pltpu.make_async_remote_copy(
            src_ref=summed, dst_ref=second.at[at],
            send_sem=send_sem.at[1], recv_sem=recv_sem.at[1],
            device_id=device, device_id_type=MESH).start()
    wait_bytes(second, recv_sem.at[1])
    for step in range(1, GROUP):
        total = total + second[step - 1]
    mine = pltpu.roll(total, lax.rem(LANES - zc * ACT, LANES), 1)
    lane = lax.broadcasted_iota(jnp.int32, (8, LANES), 1)
    out_ref[...] = jnp.where(lane < count_ref[0], mine, 0.0)
    wait_bytes(first, send_sem.at[0])
    wait_bytes(second, send_sem.at[1])


def finish_kernel(force_ref, accel_ref, jerk_ref):
    accel_ref[...] = force_ref[0:3, 0:ACT]
    jerk_ref[...] = force_ref[4:7, 0:ACT]


def local(position, velocity, accel_old, jerk_old, mass, elapsed, active_index, active_count):
    vmem = pl.BlockSpec(memory_space=pltpu.VMEM)
    smem = pl.BlockSpec(memory_space=pltpu.SMEM)
    hbm = pl.BlockSpec(memory_space=pltpu.HBM)
    tiles = (GROUP, 8, LANES)
    features, moments, everyone, rank, choice = pl.pallas_call(
        gather_kernel,
        out_shape=(
            jax.ShapeDtypeStruct((STARS, LANES), BF16),
            jax.ShapeDtypeStruct((32, STARS), BF16),
            jax.ShapeDtypeStruct(tiles, F32),
            jax.ShapeDtypeStruct((2, GROUP, LANES), F32),
            jax.ShapeDtypeStruct((1,), jnp.int32),
        ),
        in_specs=[smem, smem] + [hbm] * 6,
        out_specs=(vmem,) * 4 + (smem,),
        scratch_shapes=[pltpu.VMEM((3, STARS), F32)] * 4 + [pltpu.VMEM((TILES, LANES), F32)] * 2 + [
            pltpu.VMEM((8, STARS), F32),
            pltpu.VMEM((8, LANES), F32),
            pltpu.VMEM((GROUP - 1, 8, LANES), F32),
            pltpu.SemaphoreType.DMA((6,)),
            pltpu.SemaphoreType.DMA((2,)),
            pltpu.SemaphoreType.DMA((2,)),
        ],
        compiler_params=pltpu.CompilerParams(
            collective_id=0, has_side_effects=True, vmem_limit_bytes=56 * 2**20),
        name="gather_targets",
    )(active_index, active_count, position, velocity, accel_old, jerk_old,
      mass.reshape(TILES, LANES), elapsed.reshape(TILES, LANES))

    def forces(at):
        return pl.pallas_call(
            functools.partial(force_kernel, *SIZES[at]),
            out_shape=jax.ShapeDtypeStruct((8, LANES), F32),
            in_specs=[smem] + [vmem] * 4,
            out_specs=vmem,
            scratch_shapes=[
                pltpu.VMEM(tiles, F32),
                pltpu.VMEM((GROUP, LANES, LANES), BF16),
                pltpu.VMEM((LANES, SIZES[at][0] * BLOCK), BF16),
                pltpu.VMEM((LANES, SIZES[at][0] * BLOCK), BF16),
                pltpu.VMEM((8, SIZES[at][0] * BLOCK), F32),
                pltpu.VMEM((8, SIZES[at][0] * BLOCK), F32),
                pltpu.VMEM((GROUP - 1, 8, LANES), F32),
                pltpu.VMEM((GROUP - 1, 8, LANES), F32),
                pltpu.VMEM((8, LANES), F32),
                pltpu.SemaphoreType.DMA((2,)),
                pltpu.SemaphoreType.DMA((2,)),
            ],
            compiler_params=pltpu.CompilerParams(
                collective_id=1 + at, has_side_effects=True, vmem_limit_bytes=24 * 2**20),
            name="forces_%d" % SIZES[at][0],
        )

    branches = [forces(at) for at in range(len(SIZES))]
    mine = lax.switch(choice[0], branches, active_count, features, moments, everyone, rank)
    return pl.pallas_call(
        finish_kernel,
        out_shape=(jax.ShapeDtypeStruct((3, ACT), F32), jax.ShapeDtypeStruct((3, ACT), F32)),
        in_specs=[vmem],
        out_specs=(vmem, vmem),
        name="finish",
    )(mine)


def solution(mesh):
    split = P(None, ("row", "col"))
    flat = P(("row", "col"))
    return jax.shard_map(
        local,
        mesh=mesh,
        in_specs=(split, split, split, split, flat, flat, flat, flat),
        out_specs=(split, split),
        check_vma=False,
    )
```

```python
import functools

import jax
import jax.numpy as jnp
from jax import lax
from jax.experimental import pallas as pl
from jax.experimental.pallas import tpu as pltpu
from jax.sharding import PartitionSpec as P

SOFTENING = 0.0025
MESH = pl.DeviceIdType.MESH
F32, BF16 = jnp.float32, jnp.bfloat16
LANES = 128
GROUP = 16
ACT = 8
STARS = 4096
TILES = STARS // LANES
BLOCK = 256
SIZES = ((3, 2, False), (3, 2, True), (4, 2, False), (8, 8, False))


def ring(size, step):
    return min(step % size, -step % size)


ZC_STEPS = sorted(range(1, GROUP), key=lambda step: -ring(8, step // 2))
XY_STEPS = sorted(((i // 4, i % 4) for i in range(1, GROUP)), key=lambda at: -ring(4, at[0]) - ring(4, at[1]))
FAR = 9
LAST_FAR = XY_STEPS[FAR - 1]


def place():
    row = lax.axis_index("row")
    col = lax.axis_index("col")
    z, y_lo, core = col >> 2, (col >> 1) & 1, col & 1
    return row, z, y_lo, core, z * 2 + core, row * 2 + y_lo


def zc_peers():
    row, z, y_lo, core, zc, xy = place()
    peers = []
    for step in ZC_STEPS:
        peer = (zc + step) & (GROUP - 1)
        peers.append((peer, (row, (peer >> 1) * 4 + y_lo * 2 + (peer & 1))))
    return peers


def xy_peers():
    row, z, y_lo, core, zc, xy = place()
    rows = [((row >> 1) + step) & 3 for step in range(4)]
    columns = [((row & 1) * 2 + y_lo + step) & 3 for step in range(4)]
    peers = []
    for step in XY_STEPS:
        x, y = rows[step[0]], columns[step[1]]
        peers.append((x * 4 + y, (x * 2 + (y >> 1), z * 4 + (y & 1) * 2 + core)))
    return peers


def distances(tile, centre):
    x, y = ((tile >> 2) - (centre >> 2)) & 3, ((tile & 3) - (centre & 3)) & 3
    return jnp.minimum(x, 4 - x) + jnp.minimum(y, 4 - y), x * 4 + y


def greet():
    barrier = pltpu.get_barrier_semaphore()
    for peer, device in zc_peers() + xy_peers():
        pl.semaphore_signal(barrier, inc=1, device_id=device, device_id_type=MESH)


def await_greetings():
    pl.semaphore_wait(pltpu.get_barrier_semaphore(), 2 * (GROUP - 1))


def wait_bytes(ref, sem):
    pltpu.make_async_copy(ref, ref, sem).wait()


def mm(a, b):
    return jnp.dot(a, b, preferred_element_type=F32)


def mm_t(a, b):
    return lax.dot_general(a, b, (((1,), (1,)), ((), ())), preferred_element_type=F32)


def pieces(value):
    first = value.astype(BF16).astype(F32)
    rest = value - first
    second = rest.astype(BF16).astype(F32)
    return first, second, rest - second


def coordinates(group):
    coarse = jnp.floor(group * 16.0 + 0.5) * 0.0625
    return coarse, pieces(group - coarse)


def scalars(group, coarse, shift):
    sub = lax.broadcasted_iota(jnp.int32, group.shape, 0)
    upper = sub < 3

    def pair(exact, whole):
        exact = jnp.sum(jnp.where(upper, exact, 0.0), axis=0, keepdims=True)
        whole = jnp.sum(jnp.where(upper, whole, 0.0), axis=0, keepdims=True)
        high = exact.astype(BF16).astype(F32)
        return (high, exact - high) + pieces(whole)

    fine = group - coarse
    vel, vel_coarse = pltpu.roll(group, 4, 0), pltpu.roll(coarse, 4, 0)
    square = pair(coarse * coarse, fine * (group + coarse) + jnp.where(sub == 0, shift, 0.0))
    cross = pair(coarse * vel_coarse, fine * vel + coarse * (vel - vel_coarse))
    return square, cross


def stack(rows, shape):
    sub = lax.broadcasted_iota(jnp.int32, shape, 0)
    total = jnp.zeros(shape, F32)
    for at, row in enumerate(rows):
        total = jnp.where(sub == at, row, total)
    return total


def source_features(group):
    coarse, (one, two, three) = coordinates(group)
    square, cross = scalars(group, coarse, 0.0)
    exact = stack(square[0:2] + (1.0, 1.0) + cross[0:2] + (1.0, 1.0), group.shape)
    rest = stack(square[2:5] + (1.0,) + cross[2:5] + (1.0,), group.shape)
    more = stack((1.0, 1.0, 0.0, 0.0, 1.0, 1.0, 0.0, 0.0), group.shape)
    none = jnp.zeros_like(group)
    return [exact, coarse, rest, more, coarse, coarse, coarse, one, two, three, one, one, two, two, none, none]


def target_features(group):
    coarse, (one, two, three) = coordinates(group)
    square, cross = scalars(group, coarse, SOFTENING)
    sub = lax.broadcasted_iota(jnp.int32, group.shape, 0)
    none = jnp.zeros_like(group)

    def tail(scalar, at):
        pad, rest = (0.0,) * at, (0.0,) * (4 - at)
        exact = stack(pad + (1.0, 1.0) + scalar[0:2] + rest, group.shape)
        fine = stack(pad + (1.0, 1.0, 1.0) + scalar[2:3] + rest, group.shape)
        more = stack(pad + scalar[3:5] + (0.0, 0.0) + rest, group.shape)
        return exact, fine, more

    def weights(change, scalar, at):
        exact, fine, more = tail(scalar, at)
        c, o, t, h = change(coarse), change(one), change(two), change(three)
        rows = [exact, c, fine, more, o, t, h, c, c, c, o, t, o, t, none, none]
        return jnp.concatenate(rows, 0).astype(BF16)

    near = weights(lambda v: jnp.where(sub < 3, -2.0 * v, 0.0), square, 0)
    along = weights(lambda v: -pltpu.roll(v, 4, 0), cross, 4)
    return near, along


def prepare_tile(tile, stars, mass_ref, feature_ref, moment_ref):
    cols = pl.ds(pl.multiple_of(tile * LANES, LANES), LANES)
    group = stars[:, cols]
    rows = jnp.concatenate(source_features(group), 0)
    feature_ref[cols, :] = rows.T.astype(BF16)
    sub = lax.broadcasted_iota(jnp.int32, group.shape, 0)
    moment = mass_ref[pl.ds(tile, 1), :] * jnp.where(sub == 3, 1.0, group)
    one, two, three = pieces(moment)
    moment_ref[:, cols] = jnp.concatenate([one, two, three, jnp.zeros_like(one)], 0).astype(BF16)


def gather_kernel(index_ref, count_ref, pos_hbm, vel_hbm, acc_hbm, jerk_hbm, mass_hbm, elapsed_hbm,
                  feature_ref, moment_ref, all_ref, rank_ref, choice_ref,
                  pos_ref, vel_ref, acc_ref, jerk_ref, mass_ref, elapsed_ref,
                  stars, mine, near, load_sem, send_sem, recv_sem):
    loads = [
        pltpu.make_async_copy(src, dst, load_sem.at[at])
        for at, (src, dst) in enumerate((
            (pos_hbm, pos_ref), (vel_hbm, vel_ref), (acc_hbm, acc_ref), (jerk_hbm, jerk_ref),
            (mass_hbm, mass_ref), (elapsed_hbm, elapsed_ref)))
    ]
    for load in loads:
        load.start()
    row, z, y_lo, core, zc, xy = place()
    greet()
    for load in loads:
        load.wait()
    stars[...] = jnp.zeros_like(stars)
    for tile in range(TILES):
        cols = pl.ds(tile * LANES, LANES)
        dt = elapsed_ref[tile:tile + 1, :]
        vel, acc, jerk = vel_ref[:, cols], acc_ref[:, cols], jerk_ref[:, cols]
        stars[0:3, cols] = pos_ref[:, cols] + dt * (vel + dt * (0.5 * acc + dt * (jerk * (1.0 / 6.0))))
        stars[4:7, cols] = vel + dt * (acc + dt * (0.5 * jerk))
    lane = lax.broadcasted_iota(jnp.int32, (8, LANES), 1)
    sub = lax.broadcasted_iota(jnp.int32, (8, LANES), 0)
    total = jnp.zeros((8, LANES), F32)
    for slot in range(ACT):
        away = lane - index_ref[slot]
        picked = jnp.zeros((8, LANES), F32)
        for tile in range(TILES):
            picked = jnp.where(away == -tile * LANES, stars[:, pl.ds(tile * LANES, LANES)], picked)
        value = jnp.sum(picked, axis=1, keepdims=True)
        value = jnp.where(sub == 3, jnp.where(slot < count_ref[0], 1.0, 0.0), value)
        total = jnp.where(lane == zc * ACT + slot, value, total)
    mine[...] = total
    await_greetings()
    for at, (peer, device) in enumerate(zc_peers()):
        pltpu.make_async_remote_copy(
            src_ref=mine, dst_ref=near.at[at],
            send_sem=send_sem.at[0], recv_sem=recv_sem.at[0],
            device_id=device, device_id_type=MESH).start()

    def prepare(tile, carry):
        prepare_tile(tile, stars, mass_ref, feature_ref, moment_ref)
        return carry

    lax.fori_loop(0, TILES // 2, prepare, 0, unroll=2)
    wait_bytes(near, recv_sem.at[0])
    for step in range(1, GROUP):
        total = total + near[step - 1]
    all_ref[pl.ds(xy, 1)] = total[None]
    for peer, device in xy_peers():
        pltpu.make_async_remote_copy(
            src_ref=all_ref.at[xy], dst_ref=all_ref.at[xy],
            send_sem=send_sem.at[1], recv_sem=recv_sem.at[1],
            device_id=device, device_id_type=MESH).start()
    lax.fori_loop(TILES // 2, TILES, prepare, 0, unroll=2)
    wait_bytes(near, send_sem.at[0])
    wait_bytes(near, recv_sem.at[1])
    alive = jnp.concatenate([all_ref[g, 3:4, :] for g in range(GROUP)], 0)
    before = lax.broadcasted_iota(jnp.int32, (LANES, LANES), 0)
    after = lax.broadcasted_iota(jnp.int32, (LANES, LANES), 1)
    inside = mm(alive.astype(BF16), jnp.where(before < after, 1.0, 0.0).astype(BF16))
    sums = mm(alive.astype(BF16), jnp.ones((LANES, LANES), BF16))
    tile = lax.broadcasted_iota(jnp.int32, (GROUP, GROUP), 0)
    other = lax.broadcasted_iota(jnp.int32, (GROUP, GROUP), 1)
    (hops, step), (other_hops, other_step) = distances(tile, xy), distances(other, xy)
    earlier = other_step - GROUP * other_hops < step - GROUP * hops
    ahead = mm(jnp.where(earlier, 1.0, 0.0).astype(BF16), sums.astype(BF16))
    hops, step = distances(other, tile)
    last_hops, last_step = ring(4, LAST_FAR[0]) + ring(4, LAST_FAR[1]), LAST_FAR[0] * 4 + LAST_FAR[1]
    far = step - GROUP * hops <= last_step - GROUP * last_hops
    far = mm(jnp.where(far, 1.0, 0.0).astype(BF16), sums.astype(BF16))
    first = ahead - LANES * jnp.floor(ahead * (1.0 / LANES))
    lead = inside + first
    rank_ref[0] = jnp.where(alive > 0.0, lead - LANES * jnp.floor(lead * (1.0 / LANES)), -1.0)
    spot = lax.broadcasted_iota(jnp.int32, (GROUP, LANES), 1).astype(F32)
    rank_ref[1] = jnp.floor(ahead * (1.0 / LANES)) + jnp.where(spot < first, 1.0, 0.0)
    live = jnp.max(ahead + sums, axis=0, keepdims=True)
    others = live - jnp.min(sums, axis=0, keepdims=True)
    far = jnp.max(far, axis=0, keepdims=True)
    choice = jnp.full((1, LANES), len(SIZES) - 1.0, F32)
    for at in reversed(range(len(SIZES) - 1)):
        blocks, early, apart = SIZES[at]
        need = others if apart else live
        choice = jnp.where((need <= blocks * BLOCK) & (far <= early * BLOCK), float(at), choice)
    choice_ref[0] = choice[0, 0].astype(jnp.int32)
    wait_bytes(near, send_sem.at[1])


def three_rows(group):
    return jnp.concatenate(list(pieces(group)) + [jnp.zeros_like(group)], 0).astype(BF16)


def joined(rows):
    return rows[0:8] + rows[8:16] + rows[16:24]


def pair_weights(r2, dot):
    inv = lax.rsqrt(r2)
    inv2 = inv * inv
    w = inv * inv2
    out = []
    for value in (w, (w * inv2) * dot):
        high = value.astype(BF16)
        out.append((high, (value - high.astype(F32)).astype(BF16)))
    return out


def force_of(by_w, by_u, target):
    sub = lax.broadcasted_iota(jnp.int32, target.shape, 0)
    by_w, by_u = by_w - target * by_w[3:4, :], by_u - target * by_u[3:4, :]
    return by_w - 3.0 * jnp.where(sub >= 4, pltpu.roll(by_u, 4, 0), 0.0)


def force_apart(group, feature_ref, moment_ref):
    sub = lax.broadcasted_iota(jnp.int32, group.shape, 0)
    target = jnp.where((sub == 3) | (sub == 7), 0.0, group)
    both = mm(feature_ref[...], jnp.concatenate(target_features(target), 1))
    sums = []
    for high, low in pair_weights(both[:, :LANES], both[:, LANES:]):
        halves = mm(moment_ref[...], jnp.concatenate([high, low], 1))
        sums.append(joined(halves[:, :LANES] + halves[:, LANES:]))
    return force_of(*sums, target)


def force_kernel(blocks, early, apart, count_ref, feature_ref, moment_ref, all_ref, rank_ref, out_ref,
                 part_ref, hot, near_ref, along_ref, target_ref, force_ref,
                 first, second, summed, send_sem, recv_sem):
    greet()
    tiles = blocks * BLOCK // LANES
    spot = lax.broadcasted_iota(jnp.int32, (LANES, LANES), 0).astype(F32)
    packed = [jnp.zeros((8, LANES), F32)] * tiles
    for g in range(GROUP):
        hot[g] = jnp.where(spot == rank_ref[0, g:g + 1, :], 1.0, 0.0).astype(BF16)
        chosen = joined(mm_t(three_rows(all_ref[g]), hot[g]))
        tile = rank_ref[1, g:g + 1, :]
        packed = [old + jnp.where(tile == at, chosen, 0.0) for at, old in enumerate(packed)]
    row_id = lax.broadcasted_iota(jnp.int32, (8, LANES), 0)
    for at in range(tiles):
        cols = pl.ds(at * LANES, LANES)
        target_ref[:, cols] = jnp.where((row_id == 3) | (row_id == 7), 0.0, packed[at])

    def weigh(cols):
        near_ref[:, cols], along_ref[:, cols] = target_features(target_ref[:, cols])

    weigh(pl.ds(0, BLOCK))

    def block(index, carry):
        cols = pl.ds(pl.multiple_of(index * BLOCK, BLOCK), BLOCK)
        r2 = mm(feature_ref[...], near_ref[:, cols])
        dot = mm(feature_ref[...], along_ref[:, cols])
        sums = [joined(mm(moment_ref[...], high) + mm(moment_ref[...], low)) for high, low in pair_weights(r2, dot)]
        force_ref[:, cols] = force_of(*sums, target_ref[:, cols])
        weigh(pl.ds(pl.multiple_of(lax.rem(index + 1, blocks) * BLOCK, BLOCK), BLOCK))
        return carry

    def unpack(peer, done):
        tile = rank_ref[1, pl.ds(peer, 1), :]
        chosen = jnp.zeros((8, LANES), F32)
        for at in range(done * BLOCK // LANES):
            chosen = jnp.where(tile == at, force_ref[:, at * LANES:(at + 1) * LANES], chosen)
        part_ref[peer] = joined(mm(three_rows(chosen), hot[peer]))

    def send(at, peer, device):
        pltpu.make_async_remote_copy(
            src_ref=part_ref.at[peer], dst_ref=first.at[at],
            send_sem=send_sem.at[0], recv_sem=recv_sem.at[0],
            device_id=device, device_id_type=MESH).start()

    row, z, y_lo, core, zc, xy = place()
    peers = xy_peers()

    def send_far():
        for peer, device in peers[:FAR]:
            unpack(peer, early)
        await_greetings()
        for at in range(FAR):
            send(at, *peers[at])

    def step(index, carry):
        pl.when(index == early)(send_far)
        return block(index, carry)

    lax.fori_loop(0, blocks, step, 0)
    if early == blocks:
        send_far()
    for at in range(FAR, GROUP - 1):
        unpack(peers[at][0], blocks)
        send(at, *peers[at])
    if apart:
        total = force_apart(all_ref[xy], feature_ref, moment_ref)
    else:
        unpack(xy, blocks)
        total = part_ref[xy]
    wait_bytes(first, recv_sem.at[0])
    for step in range(1, GROUP):
        total = total + first[step - 1]
    summed[...] = total
    for at, (peer, device) in enumerate(zc_peers()):
        pltpu.make_async_remote_copy(
            src_ref=summed, dst_ref=second.at[at],
            send_sem=send_sem.at[1], recv_sem=recv_sem.at[1],
            device_id=device, device_id_type=MESH).start()
    wait_bytes(second, recv_sem.at[1])
    for step in range(1, GROUP):
        total = total + second[step - 1]
    mine = pltpu.roll(total, lax.rem(LANES - zc * ACT, LANES), 1)
    lane = lax.broadcasted_iota(jnp.int32, (8, LANES), 1)
    out_ref[...] = jnp.where(lane < count_ref[0], mine, 0.0)
    wait_bytes(first, send_sem.at[0])
    wait_bytes(second, send_sem.at[1])


def finish_kernel(force_ref, accel_ref, jerk_ref):
    accel_ref[...] = force_ref[0:3, 0:ACT]
    jerk_ref[...] = force_ref[4:7, 0:ACT]


def local(position, velocity, accel_old, jerk_old, mass, elapsed, active_index, active_count):
    vmem = pl.BlockSpec(memory_space=pltpu.VMEM)
    smem = pl.BlockSpec(memory_space=pltpu.SMEM)
    hbm = pl.BlockSpec(memory_space=pltpu.HBM)
    tiles = (GROUP, 8, LANES)
    features, moments, everyone, rank, choice = pl.pallas_call(
        gather_kernel,
        out_shape=(
            jax.ShapeDtypeStruct((STARS, LANES), BF16),
            jax.ShapeDtypeStruct((32, STARS), BF16),
            jax.ShapeDtypeStruct(tiles, F32),
            jax.ShapeDtypeStruct((2, GROUP, LANES), F32),
            jax.ShapeDtypeStruct((1,), jnp.int32),
        ),
        in_specs=[smem, smem] + [hbm] * 6,
        out_specs=(vmem,) * 4 + (smem,),
        scratch_shapes=[pltpu.VMEM((3, STARS), F32)] * 4 + [pltpu.VMEM((TILES, LANES), F32)] * 2 + [
            pltpu.VMEM((8, STARS), F32),
            pltpu.VMEM((8, LANES), F32),
            pltpu.VMEM((GROUP - 1, 8, LANES), F32),
            pltpu.SemaphoreType.DMA((6,)),
            pltpu.SemaphoreType.DMA((2,)),
            pltpu.SemaphoreType.DMA((2,)),
        ],
        compiler_params=pltpu.CompilerParams(
            collective_id=0, has_side_effects=True, vmem_limit_bytes=56 * 2**20),
        name="gather_targets",
    )(active_index, active_count, position, velocity, accel_old, jerk_old,
      mass.reshape(TILES, LANES), elapsed.reshape(TILES, LANES))

    def forces(at):
        return pl.pallas_call(
            functools.partial(force_kernel, *SIZES[at]),
            out_shape=jax.ShapeDtypeStruct((8, LANES), F32),
            in_specs=[smem] + [vmem] * 4,
            out_specs=vmem,
            scratch_shapes=[
                pltpu.VMEM(tiles, F32),
                pltpu.VMEM((GROUP, LANES, LANES), BF16),
                pltpu.VMEM((LANES, SIZES[at][0] * BLOCK), BF16),
                pltpu.VMEM((LANES, SIZES[at][0] * BLOCK), BF16),
                pltpu.VMEM((8, SIZES[at][0] * BLOCK), F32),
                pltpu.VMEM((8, SIZES[at][0] * BLOCK), F32),
                pltpu.VMEM((GROUP - 1, 8, LANES), F32),
                pltpu.VMEM((GROUP - 1, 8, LANES), F32),
                pltpu.VMEM((8, LANES), F32),
                pltpu.SemaphoreType.DMA((2,)),
                pltpu.SemaphoreType.DMA((2,)),
            ],
            compiler_params=pltpu.CompilerParams(
                collective_id=1 + at, has_side_effects=True, vmem_limit_bytes=24 * 2**20),
            name="forces_%d%s" % (SIZES[at][0], "_apart" if SIZES[at][2] else ""),
        )

    branches = [forces(at) for at in range(len(SIZES))]
    mine = lax.switch(choice[0], branches, active_count, features, moments, everyone, rank)
    return pl.pallas_call(
        finish_kernel,
        out_shape=(jax.ShapeDtypeStruct((3, ACT), F32), jax.ShapeDtypeStruct((3, ACT), F32)),
        in_specs=[vmem],
        out_specs=(vmem, vmem),
        name="finish",
    )(mine)


def solution(mesh):
    split = P(None, ("row", "col"))
    flat = P(("row", "col"))
    return jax.shard_map(
        local,
        mesh=mesh,
        in_specs=(split, split, split, split, flat, flat, flat, flat),
        out_specs=(split, split),
        check_vma=False,
    )
```

```python
import functools

import jax
import jax.numpy as jnp
from jax import lax
from jax.experimental import pallas as pl
from jax.experimental.pallas import tpu as pltpu
from jax.sharding import PartitionSpec as P

SOFTENING = 0.0025
MESH = pl.DeviceIdType.MESH
F32, BF16 = jnp.float32, jnp.bfloat16
LANES = 128
GROUP = 16
ACT = 8
STARS = 4096
TILES = STARS // LANES
BLOCK = 256
SIZES = ((3, 2, False), (3, 2, True), (4, 2, False), (8, 8, False))


def ring(size, step):
    return min(step % size, -step % size)


ZC_STEPS = sorted(range(1, GROUP), key=lambda step: -ring(8, step // 2))
XY_STEPS = sorted(((i // 4, i % 4) for i in range(1, GROUP)), key=lambda at: -ring(4, at[0]) - ring(4, at[1]))
FAR = 9
LAST_FAR = XY_STEPS[FAR - 1]


def place():
    row = lax.axis_index("row")
    col = lax.axis_index("col")
    z, y_lo, core = col >> 2, (col >> 1) & 1, col & 1
    return row, z, y_lo, core, z * 2 + core, row * 2 + y_lo


def zc_peers():
    row, z, y_lo, core, zc, xy = place()
    peers = []
    for step in ZC_STEPS:
        peer = (zc + step) & (GROUP - 1)
        peers.append((peer, (row, (peer >> 1) * 4 + y_lo * 2 + (peer & 1))))
    return peers


def xy_peers():
    row, z, y_lo, core, zc, xy = place()
    rows = [((row >> 1) + step) & 3 for step in range(4)]
    columns = [((row & 1) * 2 + y_lo + step) & 3 for step in range(4)]
    peers = []
    for step in XY_STEPS:
        x, y = rows[step[0]], columns[step[1]]
        peers.append((x * 4 + y, (x * 2 + (y >> 1), z * 4 + (y & 1) * 2 + core)))
    return peers


def distances(tile, centre):
    x, y = ((tile >> 2) - (centre >> 2)) & 3, ((tile & 3) - (centre & 3)) & 3
    return jnp.minimum(x, 4 - x) + jnp.minimum(y, 4 - y), x * 4 + y


def greet():
    barrier = pltpu.get_barrier_semaphore()
    for peer, device in zc_peers() + xy_peers():
        pl.semaphore_signal(barrier, inc=1, device_id=device, device_id_type=MESH)


def await_greetings():
    pl.semaphore_wait(pltpu.get_barrier_semaphore(), 2 * (GROUP - 1))


def wait_bytes(ref, sem):
    pltpu.make_async_copy(ref, ref, sem).wait()


def mm(a, b):
    return jnp.dot(a, b, preferred_element_type=F32)


def mm_t(a, b):
    return lax.dot_general(a, b, (((1,), (1,)), ((), ())), preferred_element_type=F32)


def pieces(value):
    first = value.astype(BF16).astype(F32)
    rest = value - first
    second = rest.astype(BF16).astype(F32)
    return first, second, rest - second


def coordinates(group):
    coarse = jnp.floor(group * 16.0 + 0.5) * 0.0625
    return coarse, pieces(group - coarse)


def scalars(group, coarse, shift):
    sub = lax.broadcasted_iota(jnp.int32, group.shape, 0)
    upper = sub < 3

    def pair(exact, whole):
        exact = jnp.sum(jnp.where(upper, exact, 0.0), axis=0, keepdims=True)
        whole = jnp.sum(jnp.where(upper, whole, 0.0), axis=0, keepdims=True)
        high = exact.astype(BF16).astype(F32)
        return (high, exact - high) + pieces(whole)

    fine = group - coarse
    vel, vel_coarse = pltpu.roll(group, 4, 0), pltpu.roll(coarse, 4, 0)
    square = pair(coarse * coarse, fine * (group + coarse) + jnp.where(sub == 0, shift, 0.0))
    cross = pair(coarse * vel_coarse, fine * vel + coarse * (vel - vel_coarse))
    return square, cross


def stack(rows, shape):
    sub = lax.broadcasted_iota(jnp.int32, shape, 0)
    total = jnp.zeros(shape, F32)
    for at, row in enumerate(rows):
        total = jnp.where(sub == at, row, total)
    return total


def source_features(group):
    coarse, (one, two, three) = coordinates(group)
    square, cross = scalars(group, coarse, 0.0)
    exact = stack(square[0:2] + (1.0, 1.0) + cross[0:2] + (1.0, 1.0), group.shape)
    rest = stack(square[2:5] + (1.0,) + cross[2:5] + (1.0,), group.shape)
    more = stack((1.0, 1.0, 0.0, 0.0, 1.0, 1.0, 0.0, 0.0), group.shape)
    none = jnp.zeros_like(group)
    return [exact, coarse, rest, more, coarse, coarse, coarse, one, two, three, one, one, two, two, none, none]


def target_features(group):
    coarse, (one, two, three) = coordinates(group)
    square, cross = scalars(group, coarse, SOFTENING)
    sub = lax.broadcasted_iota(jnp.int32, group.shape, 0)
    none = jnp.zeros_like(group)

    def tail(scalar, at):
        pad, rest = (0.0,) * at, (0.0,) * (4 - at)
        exact = stack(pad + (1.0, 1.0) + scalar[0:2] + rest, group.shape)
        fine = stack(pad + (1.0, 1.0, 1.0) + scalar[2:3] + rest, group.shape)
        more = stack(pad + scalar[3:5] + (0.0, 0.0) + rest, group.shape)
        return exact, fine, more

    def weights(change, scalar, at):
        exact, fine, more = tail(scalar, at)
        c, o, t, h = change(coarse), change(one), change(two), change(three)
        rows = [exact, c, fine, more, o, t, h, c, c, c, o, t, o, t, none, none]
        return jnp.concatenate(rows, 0).astype(BF16)

    near = weights(lambda v: jnp.where(sub < 3, -2.0 * v, 0.0), square, 0)
    along = weights(lambda v: -pltpu.roll(v, 4, 0), cross, 4)
    return near, along


def prepare_tile(tile, stars, mass_ref, feature_ref, moment_ref):
    cols = pl.ds(pl.multiple_of(tile * LANES, LANES), LANES)
    group = stars[:, cols]
    rows = jnp.concatenate(source_features(group), 0)
    feature_ref[cols, :] = rows.T.astype(BF16)
    sub = lax.broadcasted_iota(jnp.int32, group.shape, 0)
    moment = mass_ref[pl.ds(tile, 1), :] * jnp.where(sub == 3, 1.0, group)
    one, two, three = pieces(moment)
    moment_ref[:, cols] = jnp.concatenate([one, two, three, jnp.zeros_like(one)], 0).astype(BF16)


def gather_kernel(index_ref, count_ref, pos_hbm, vel_hbm, acc_hbm, jerk_hbm, mass_hbm, elapsed_hbm,
                  feature_ref, moment_ref, all_ref, rank_ref, choice_ref,
                  pos_ref, vel_ref, acc_ref, jerk_ref, mass_ref, elapsed_ref,
                  stars, mine, near, load_sem, send_sem, recv_sem):
    loads = [
        pltpu.make_async_copy(src, dst, load_sem.at[at])
        for at, (src, dst) in enumerate((
            (pos_hbm, pos_ref), (vel_hbm, vel_ref), (acc_hbm, acc_ref), (jerk_hbm, jerk_ref),
            (mass_hbm, mass_ref), (elapsed_hbm, elapsed_ref)))
    ]
    for load in loads:
        load.start()
    row, z, y_lo, core, zc, xy = place()
    greet()
    for load in loads:
        load.wait()
    stars[...] = jnp.zeros_like(stars)
    for tile in range(TILES):
        cols = pl.ds(tile * LANES, LANES)
        dt = elapsed_ref[tile:tile + 1, :]
        vel, acc, jerk = vel_ref[:, cols], acc_ref[:, cols], jerk_ref[:, cols]
        stars[0:3, cols] = pos_ref[:, cols] + dt * (vel + dt * (0.5 * acc + dt * (jerk * (1.0 / 6.0))))
        stars[4:7, cols] = vel + dt * (acc + dt * (0.5 * jerk))
    lane = lax.broadcasted_iota(jnp.int32, (8, LANES), 1)
    sub = lax.broadcasted_iota(jnp.int32, (8, LANES), 0)
    total = jnp.zeros((8, LANES), F32)
    for slot in range(ACT):
        away = lane - index_ref[slot]
        picked = jnp.zeros((8, LANES), F32)
        for tile in range(TILES):
            picked = jnp.where(away == -tile * LANES, stars[:, pl.ds(tile * LANES, LANES)], picked)
        value = jnp.sum(picked, axis=1, keepdims=True)
        value = jnp.where(sub == 3, jnp.where(slot < count_ref[0], 1.0, 0.0), value)
        total = jnp.where(lane == zc * ACT + slot, value, total)
    mine[...] = total
    await_greetings()
    for at, (peer, device) in enumerate(zc_peers()):
        pltpu.make_async_remote_copy(
            src_ref=mine, dst_ref=near.at[at],
            send_sem=send_sem.at[0], recv_sem=recv_sem.at[0],
            device_id=device, device_id_type=MESH).start()

    def prepare(tile, carry):
        prepare_tile(tile, stars, mass_ref, feature_ref, moment_ref)
        return carry

    lax.fori_loop(0, TILES // 2, prepare, 0, unroll=2)
    wait_bytes(near, recv_sem.at[0])
    for step in range(1, GROUP):
        total = total + near[step - 1]
    all_ref[pl.ds(xy, 1)] = total[None]
    for peer, device in xy_peers():
        pltpu.make_async_remote_copy(
            src_ref=all_ref.at[xy], dst_ref=all_ref.at[xy],
            send_sem=send_sem.at[1], recv_sem=recv_sem.at[1],
            device_id=device, device_id_type=MESH).start()
    lax.fori_loop(TILES // 2, TILES, prepare, 0, unroll=2)
    wait_bytes(near, send_sem.at[0])
    wait_bytes(near, recv_sem.at[1])
    alive = jnp.concatenate([all_ref[g, 3:4, :] for g in range(GROUP)], 0)
    before = lax.broadcasted_iota(jnp.int32, (LANES, LANES), 0)
    after = lax.broadcasted_iota(jnp.int32, (LANES, LANES), 1)
    inside = mm(alive.astype(BF16), jnp.where(before < after, 1.0, 0.0).astype(BF16))
    sums = mm(alive.astype(BF16), jnp.ones((LANES, LANES), BF16))
    tile = lax.broadcasted_iota(jnp.int32, (GROUP, GROUP), 0)
    other = lax.broadcasted_iota(jnp.int32, (GROUP, GROUP), 1)
    (hops, step), (other_hops, other_step) = distances(tile, xy), distances(other, xy)
    earlier = other_step - GROUP * other_hops < step - GROUP * hops
    ahead = mm(jnp.where(earlier, 1.0, 0.0).astype(BF16), sums.astype(BF16))
    hops, step = distances(other, tile)
    last_hops, last_step = ring(4, LAST_FAR[0]) + ring(4, LAST_FAR[1]), LAST_FAR[0] * 4 + LAST_FAR[1]
    far = step - GROUP * hops <= last_step - GROUP * last_hops
    far = mm(jnp.where(far, 1.0, 0.0).astype(BF16), sums.astype(BF16))
    first = ahead - LANES * jnp.floor(ahead * (1.0 / LANES))
    lead = inside + first
    rank_ref[0] = jnp.where(alive > 0.0, lead - LANES * jnp.floor(lead * (1.0 / LANES)), -1.0)
    spot = lax.broadcasted_iota(jnp.int32, (GROUP, LANES), 1).astype(F32)
    rank_ref[1] = jnp.floor(ahead * (1.0 / LANES)) + jnp.where(spot < first, 1.0, 0.0)
    live = jnp.max(ahead + sums, axis=0, keepdims=True)
    others = live - jnp.min(sums, axis=0, keepdims=True)
    far = jnp.max(far, axis=0, keepdims=True)
    choice = jnp.full((1, LANES), len(SIZES) - 1.0, F32)
    for at in reversed(range(len(SIZES) - 1)):
        blocks, early, apart = SIZES[at]
        need = others if apart else live
        choice = jnp.where((need <= blocks * BLOCK) & (far <= early * BLOCK), float(at), choice)
    choice_ref[0] = choice[0, 0].astype(jnp.int32)
    wait_bytes(near, send_sem.at[1])


def three_rows(group):
    return jnp.concatenate(list(pieces(group)) + [jnp.zeros_like(group)], 0).astype(BF16)


def halved(rows):
    return rows[0:8] + rows[8:16]


def joined(rows):
    return halved(rows) + rows[16:24]


def pair_weights(r2, dot):
    inv = lax.rsqrt(r2)
    inv2 = inv * inv
    w = inv * inv2
    out = []
    for value in (w, (w * inv2) * dot):
        high = value.astype(BF16)
        out.append((high, (value - high.astype(F32)).astype(BF16)))
    return out


def force_of(by_w, by_u, target):
    sub = lax.broadcasted_iota(jnp.int32, target.shape, 0)
    by_w, by_u = by_w - target * by_w[3:4, :], by_u - target * by_u[3:4, :]
    return by_w - 3.0 * jnp.where(sub >= 4, pltpu.roll(by_u, 4, 0), 0.0)


def force_apart(group, feature_ref, moment_ref):
    sub = lax.broadcasted_iota(jnp.int32, group.shape, 0)
    target = jnp.where((sub == 3) | (sub == 7), 0.0, group)
    both = mm(feature_ref[...], jnp.concatenate(target_features(target), 1))
    sums = []
    for high, low in pair_weights(both[:, :LANES], both[:, LANES:]):
        halves = mm(moment_ref[...], jnp.concatenate([high, low], 1))
        sums.append(joined(halves[:, :LANES] + halves[:, LANES:]))
    return force_of(*sums, target)


def force_kernel(blocks, early, apart, count_ref, feature_ref, moment_ref, all_ref, rank_ref, out_ref,
                 part_ref, hot, near_ref, along_ref, target_ref, force_ref,
                 first, second, summed, send_sem, recv_sem):
    greet()
    tiles = blocks * BLOCK // LANES
    spot = lax.broadcasted_iota(jnp.int32, (LANES, LANES), 0).astype(F32)
    packed = [jnp.zeros((8, LANES), F32)] * tiles
    for g in range(GROUP):
        hot[g] = jnp.where(spot == rank_ref[0, g:g + 1, :], 1.0, 0.0).astype(BF16)
        chosen = joined(mm_t(three_rows(all_ref[g]), hot[g]))
        tile = rank_ref[1, g:g + 1, :]
        packed = [old + jnp.where(tile == at, chosen, 0.0) for at, old in enumerate(packed)]
    row_id = lax.broadcasted_iota(jnp.int32, (8, LANES), 0)
    for at in range(tiles):
        cols = pl.ds(at * LANES, LANES)
        target_ref[:, cols] = jnp.where((row_id == 3) | (row_id == 7), 0.0, packed[at])

    def weigh(cols):
        near_ref[:, cols], along_ref[:, cols] = target_features(target_ref[:, cols])

    weigh(pl.ds(0, BLOCK))

    def block(index, carry):
        cols = pl.ds(pl.multiple_of(index * BLOCK, BLOCK), BLOCK)
        r2 = mm(feature_ref[...], near_ref[:, cols])
        dot = mm(feature_ref[...], along_ref[:, cols])
        sums = [halved(mm(moment_ref[0:16, :], low)) + joined(mm(moment_ref[...], high))
                for high, low in pair_weights(r2, dot)]
        force_ref[:, cols] = force_of(*sums, target_ref[:, cols])
        weigh(pl.ds(pl.multiple_of(lax.rem(index + 1, blocks) * BLOCK, BLOCK), BLOCK))
        return carry

    def unpack(peer, done):
        tile = rank_ref[1, pl.ds(peer, 1), :]
        chosen = jnp.zeros((8, LANES), F32)
        for at in range(done * BLOCK // LANES):
            chosen = jnp.where(tile == at, force_ref[:, at * LANES:(at + 1) * LANES], chosen)
        part_ref[peer] = joined(mm(three_rows(chosen), hot[peer]))

    def send(at, peer, device):
        pltpu.make_async_remote_copy(
            src_ref=part_ref.at[peer], dst_ref=first.at[at],
            send_sem=send_sem.at[0], recv_sem=recv_sem.at[0],
            device_id=device, device_id_type=MESH).start()

    row, z, y_lo, core, zc, xy = place()
    peers = xy_peers()

    def send_far():
        for peer, device in peers[:FAR]:
            unpack(peer, early)
        await_greetings()
        for at in range(FAR):
            send(at, *peers[at])

    def step(index, carry):
        pl.when(index == early)(send_far)
        return block(index, carry)

    lax.fori_loop(0, blocks, step, 0)
    if early == blocks:
        send_far()
    for at in range(FAR, GROUP - 1):
        unpack(peers[at][0], blocks)
        send(at, *peers[at])
    if apart:
        total = force_apart(all_ref[xy], feature_ref, moment_ref)
    else:
        unpack(xy, blocks)
        total = part_ref[xy]
    wait_bytes(first, recv_sem.at[0])
    for step in range(1, GROUP):
        total = total + first[step - 1]
    summed[...] = total
    for at, (peer, device) in enumerate(zc_peers()):
        pltpu.make_async_remote_copy(
            src_ref=summed, dst_ref=second.at[at],
            send_sem=send_sem.at[1], recv_sem=recv_sem.at[1],
            device_id=device, device_id_type=MESH).start()
    wait_bytes(second, recv_sem.at[1])
    for step in range(1, GROUP):
        total = total + second[step - 1]
    mine = pltpu.roll(total, lax.rem(LANES - zc * ACT, LANES), 1)
    lane = lax.broadcasted_iota(jnp.int32, (8, LANES), 1)
    out_ref[...] = jnp.where(lane < count_ref[0], mine, 0.0)
    wait_bytes(first, send_sem.at[0])
    wait_bytes(second, send_sem.at[1])


def finish_kernel(force_ref, accel_ref, jerk_ref):
    accel_ref[...] = force_ref[0:3, 0:ACT]
    jerk_ref[...] = force_ref[4:7, 0:ACT]


def local(position, velocity, accel_old, jerk_old, mass, elapsed, active_index, active_count):
    vmem = pl.BlockSpec(memory_space=pltpu.VMEM)
    smem = pl.BlockSpec(memory_space=pltpu.SMEM)
    hbm = pl.BlockSpec(memory_space=pltpu.HBM)
    tiles = (GROUP, 8, LANES)
    features, moments, everyone, rank, choice = pl.pallas_call(
        gather_kernel,
        out_shape=(
            jax.ShapeDtypeStruct((STARS, LANES), BF16),
            jax.ShapeDtypeStruct((32, STARS), BF16),
            jax.ShapeDtypeStruct(tiles, F32),
            jax.ShapeDtypeStruct((2, GROUP, LANES), F32),
            jax.ShapeDtypeStruct((1,), jnp.int32),
        ),
        in_specs=[smem, smem] + [hbm] * 6,
        out_specs=(vmem,) * 4 + (smem,),
        scratch_shapes=[pltpu.VMEM((3, STARS), F32)] * 4 + [pltpu.VMEM((TILES, LANES), F32)] * 2 + [
            pltpu.VMEM((8, STARS), F32),
            pltpu.VMEM((8, LANES), F32),
            pltpu.VMEM((GROUP - 1, 8, LANES), F32),
            pltpu.SemaphoreType.DMA((6,)),
            pltpu.SemaphoreType.DMA((2,)),
            pltpu.SemaphoreType.DMA((2,)),
        ],
        compiler_params=pltpu.CompilerParams(
            collective_id=0, has_side_effects=True, vmem_limit_bytes=56 * 2**20),
        name="gather_targets",
    )(active_index, active_count, position, velocity, accel_old, jerk_old,
      mass.reshape(TILES, LANES), elapsed.reshape(TILES, LANES))

    def forces(at):
        return pl.pallas_call(
            functools.partial(force_kernel, *SIZES[at]),
            out_shape=jax.ShapeDtypeStruct((8, LANES), F32),
            in_specs=[smem] + [vmem] * 4,
            out_specs=vmem,
            scratch_shapes=[
                pltpu.VMEM(tiles, F32),
                pltpu.VMEM((GROUP, LANES, LANES), BF16),
                pltpu.VMEM((LANES, SIZES[at][0] * BLOCK), BF16),
                pltpu.VMEM((LANES, SIZES[at][0] * BLOCK), BF16),
                pltpu.VMEM((8, SIZES[at][0] * BLOCK), F32),
                pltpu.VMEM((8, SIZES[at][0] * BLOCK), F32),
                pltpu.VMEM((GROUP - 1, 8, LANES), F32),
                pltpu.VMEM((GROUP - 1, 8, LANES), F32),
                pltpu.VMEM((8, LANES), F32),
                pltpu.SemaphoreType.DMA((2,)),
                pltpu.SemaphoreType.DMA((2,)),
            ],
            compiler_params=pltpu.CompilerParams(
                collective_id=1 + at, has_side_effects=True, vmem_limit_bytes=24 * 2**20),
            name="forces_%d%s" % (SIZES[at][0], "_apart" if SIZES[at][2] else ""),
        )

    branches = [forces(at) for at in range(len(SIZES))]
    mine = lax.switch(choice[0], branches, active_count, features, moments, everyone, rank)
    return pl.pallas_call(
        finish_kernel,
        out_shape=(jax.ShapeDtypeStruct((3, ACT), F32), jax.ShapeDtypeStruct((3, ACT), F32)),
        in_specs=[vmem],
        out_specs=(vmem, vmem),
        name="finish",
    )(mine)


def solution(mesh):
    split = P(None, ("row", "col"))
    flat = P(("row", "col"))
    return jax.shard_map(
        local,
        mesh=mesh,
        in_specs=(split, split, split, split, flat, flat, flat, flat),
        out_specs=(split, split),
        check_vma=False,
    )
```

```python
import functools

import jax
import jax.numpy as jnp
from jax import lax
from jax.experimental import pallas as pl
from jax.experimental.pallas import tpu as pltpu
from jax.sharding import PartitionSpec as P

SOFTENING = 0.0025
MESH = pl.DeviceIdType.MESH
F32, BF16 = jnp.float32, jnp.bfloat16
LANES = 128
GROUP = 16
ACT = 8
STARS = 4096
TILES = STARS // LANES
BLOCK = 256
SIZES = ((3, 2, False), (3, 2, True), (4, 2, False), (8, 8, False))


def ring(size, step):
    return min(step % size, -step % size)


ZC_STEPS = sorted(range(1, GROUP), key=lambda step: -ring(8, step // 2))
XY_STEPS = sorted(((i // 4, i % 4) for i in range(1, GROUP)), key=lambda at: -ring(4, at[0]) - ring(4, at[1]))
FAR = 9
LAST_FAR = XY_STEPS[FAR - 1]


def place():
    row = lax.axis_index("row")
    col = lax.axis_index("col")
    z, y_lo, core = col >> 2, (col >> 1) & 1, col & 1
    return row, z, y_lo, core, z * 2 + core, row * 2 + y_lo


def zc_peers():
    row, z, y_lo, core, zc, xy = place()
    peers = []
    for step in ZC_STEPS:
        peer = (zc + step) & (GROUP - 1)
        peers.append((peer, (row, (peer >> 1) * 4 + y_lo * 2 + (peer & 1))))
    return peers


def xy_peers():
    row, z, y_lo, core, zc, xy = place()
    rows = [((row >> 1) + step) & 3 for step in range(4)]
    columns = [((row & 1) * 2 + y_lo + step) & 3 for step in range(4)]
    peers = []
    for step in XY_STEPS:
        x, y = rows[step[0]], columns[step[1]]
        peers.append((x * 4 + y, (x * 2 + (y >> 1), z * 4 + (y & 1) * 2 + core)))
    return peers


def distances(tile, centre):
    x, y = ((tile >> 2) - (centre >> 2)) & 3, ((tile & 3) - (centre & 3)) & 3
    return jnp.minimum(x, 4 - x) + jnp.minimum(y, 4 - y), x * 4 + y


def greet():
    barrier = pltpu.get_barrier_semaphore()
    for peer, device in zc_peers() + xy_peers():
        pl.semaphore_signal(barrier, inc=1, device_id=device, device_id_type=MESH)


def await_greetings():
    pl.semaphore_wait(pltpu.get_barrier_semaphore(), 2 * (GROUP - 1))


def wait_bytes(ref, sem):
    pltpu.make_async_copy(ref, ref, sem).wait()


def mm(a, b):
    return jnp.dot(a, b, preferred_element_type=F32)


def mm_t(a, b):
    return lax.dot_general(a, b, (((1,), (1,)), ((), ())), preferred_element_type=F32)


def pieces(value):
    first = value.astype(BF16).astype(F32)
    rest = value - first
    second = rest.astype(BF16).astype(F32)
    return first, second, rest - second


def coordinates(group):
    coarse = jnp.floor(group * 16.0 + 0.5) * 0.0625
    return coarse, pieces(group - coarse)


def scalars(group, coarse, shift):
    sub = lax.broadcasted_iota(jnp.int32, group.shape, 0)
    upper = sub < 3

    def pair(exact, whole):
        exact = jnp.sum(jnp.where(upper, exact, 0.0), axis=0, keepdims=True)
        whole = jnp.sum(jnp.where(upper, whole, 0.0), axis=0, keepdims=True)
        high = exact.astype(BF16).astype(F32)
        return (high, exact - high) + pieces(whole)

    fine = group - coarse
    vel, vel_coarse = pltpu.roll(group, 4, 0), pltpu.roll(coarse, 4, 0)
    square = pair(coarse * coarse, fine * (group + coarse) + jnp.where(sub == 0, shift, 0.0))
    cross = pair(coarse * vel_coarse, fine * vel + coarse * (vel - vel_coarse))
    return square, cross


def stack(rows, shape):
    sub = lax.broadcasted_iota(jnp.int32, shape, 0)
    total = jnp.zeros(shape, F32)
    for at, row in enumerate(rows):
        total = jnp.where(sub == at, row, total)
    return total


def source_features(group):
    coarse, (one, two, three) = coordinates(group)
    square, cross = scalars(group, coarse, 0.0)
    exact = stack(square[0:2] + (1.0, 1.0) + cross[0:2] + (1.0, 1.0), group.shape)
    rest = stack(square[2:5] + (1.0,) + cross[2:5] + (1.0,), group.shape)
    more = stack((1.0, 1.0, 0.0, 0.0, 1.0, 1.0, 0.0, 0.0), group.shape)
    none = jnp.zeros_like(group)
    return [exact, coarse, rest, more, coarse, coarse, coarse, one, two, three, one, one, two, two, none, none]


def target_features(group):
    coarse, (one, two, three) = coordinates(group)
    square, cross = scalars(group, coarse, SOFTENING)
    sub = lax.broadcasted_iota(jnp.int32, group.shape, 0)
    none = jnp.zeros_like(group)

    def tail(scalar, at):
        pad, rest = (0.0,) * at, (0.0,) * (4 - at)
        exact = stack(pad + (1.0, 1.0) + scalar[0:2] + rest, group.shape)
        fine = stack(pad + (1.0, 1.0, 1.0) + scalar[2:3] + rest, group.shape)
        more = stack(pad + scalar[3:5] + (0.0, 0.0) + rest, group.shape)
        return exact, fine, more

    def weights(change, scalar, at):
        exact, fine, more = tail(scalar, at)
        c, o, t, h = change(coarse), change(one), change(two), change(three)
        rows = [exact, c, fine, more, o, t, h, c, c, c, o, t, o, t, none, none]
        return jnp.concatenate(rows, 0).astype(BF16)

    near = weights(lambda v: jnp.where(sub < 3, -2.0 * v, 0.0), square, 0)
    along = weights(lambda v: -pltpu.roll(v, 4, 0), cross, 4)
    return near, along


def prepare_tile(tile, stars, mass_ref, feature_ref, moment_ref):
    cols = pl.ds(pl.multiple_of(tile * LANES, LANES), LANES)
    group = stars[:, cols]
    rows = jnp.concatenate(source_features(group), 0)
    feature_ref[cols, :] = rows.T.astype(BF16)
    sub = lax.broadcasted_iota(jnp.int32, group.shape, 0)
    moment = mass_ref[pl.ds(tile, 1), :] * jnp.where(sub == 3, 1.0, group)
    one, two, three = pieces(moment)
    moment_ref[:, cols] = jnp.concatenate([one, two, three, jnp.zeros_like(one)], 0).astype(BF16)


def gather_kernel(index_ref, count_ref, pos_hbm, vel_hbm, acc_hbm, jerk_hbm, mass_hbm, elapsed_hbm,
                  feature_ref, moment_ref, all_ref, rank_ref, choice_ref,
                  pos_ref, vel_ref, acc_ref, jerk_ref, mass_ref, elapsed_ref,
                  stars, mine, near, load_sem, send_sem, recv_sem):
    loads = [
        pltpu.make_async_copy(src, dst, load_sem.at[at])
        for at, (src, dst) in enumerate((
            (pos_hbm, pos_ref), (vel_hbm, vel_ref), (acc_hbm, acc_ref), (jerk_hbm, jerk_ref),
            (mass_hbm, mass_ref), (elapsed_hbm, elapsed_ref)))
    ]
    for load in loads:
        load.start()
    row, z, y_lo, core, zc, xy = place()
    greet()
    for load in loads:
        load.wait()
    stars[...] = jnp.zeros_like(stars)
    for tile in range(TILES):
        cols = pl.ds(tile * LANES, LANES)
        dt = elapsed_ref[tile:tile + 1, :]
        vel, acc, jerk = vel_ref[:, cols], acc_ref[:, cols], jerk_ref[:, cols]
        stars[0:3, cols] = pos_ref[:, cols] + dt * (vel + dt * (0.5 * acc + dt * (jerk * (1.0 / 6.0))))
        stars[4:7, cols] = vel + dt * (acc + dt * (0.5 * jerk))
    lane = lax.broadcasted_iota(jnp.int32, (8, LANES), 1)
    sub = lax.broadcasted_iota(jnp.int32, (8, LANES), 0)
    total = jnp.zeros((8, LANES), F32)
    for slot in range(ACT):
        away = lane - index_ref[slot]
        picked = jnp.zeros((8, LANES), F32)
        for tile in range(TILES):
            picked = jnp.where(away == -tile * LANES, stars[:, pl.ds(tile * LANES, LANES)], picked)
        value = jnp.sum(picked, axis=1, keepdims=True)
        value = jnp.where(sub == 3, jnp.where(slot < count_ref[0], 1.0, 0.0), value)
        total = jnp.where(lane == zc * ACT + slot, value, total)
    mine[...] = total
    await_greetings()
    for at, (peer, device) in enumerate(zc_peers()):
        pltpu.make_async_remote_copy(
            src_ref=mine, dst_ref=near.at[at],
            send_sem=send_sem.at[0], recv_sem=recv_sem.at[0],
            device_id=device, device_id_type=MESH).start()

    def prepare(tile, carry):
        prepare_tile(tile, stars, mass_ref, feature_ref, moment_ref)
        return carry

    lax.fori_loop(0, TILES // 2, prepare, 0, unroll=2)
    wait_bytes(near, recv_sem.at[0])
    for step in range(1, GROUP):
        total = total + near[step - 1]
    all_ref[pl.ds(xy, 1)] = total[None]
    for peer, device in xy_peers():
        pltpu.make_async_remote_copy(
            src_ref=all_ref.at[xy], dst_ref=all_ref.at[xy],
            send_sem=send_sem.at[1], recv_sem=recv_sem.at[1],
            device_id=device, device_id_type=MESH).start()
    lax.fori_loop(TILES // 2, TILES, prepare, 0, unroll=2)
    wait_bytes(near, send_sem.at[0])
    wait_bytes(near, recv_sem.at[1])
    alive = jnp.concatenate([all_ref[g, 3:4, :] for g in range(GROUP)], 0)
    before = lax.broadcasted_iota(jnp.int32, (LANES, LANES), 0)
    after = lax.broadcasted_iota(jnp.int32, (LANES, LANES), 1)
    inside = mm(alive.astype(BF16), jnp.where(before < after, 1.0, 0.0).astype(BF16))
    sums = mm(alive.astype(BF16), jnp.ones((LANES, LANES), BF16))
    tile = lax.broadcasted_iota(jnp.int32, (GROUP, GROUP), 0)
    other = lax.broadcasted_iota(jnp.int32, (GROUP, GROUP), 1)
    (hops, step), (other_hops, other_step) = distances(tile, xy), distances(other, xy)
    earlier = other_step - GROUP * other_hops < step - GROUP * hops
    ahead = mm(jnp.where(earlier, 1.0, 0.0).astype(BF16), sums.astype(BF16))
    hops, step = distances(other, tile)
    last_hops, last_step = ring(4, LAST_FAR[0]) + ring(4, LAST_FAR[1]), LAST_FAR[0] * 4 + LAST_FAR[1]
    far = step - GROUP * hops <= last_step - GROUP * last_hops
    far = mm(jnp.where(far, 1.0, 0.0).astype(BF16), sums.astype(BF16))
    first = ahead - LANES * jnp.floor(ahead * (1.0 / LANES))
    lead = inside + first
    rank_ref[0] = jnp.where(alive > 0.0, lead - LANES * jnp.floor(lead * (1.0 / LANES)), -1.0)
    spot = lax.broadcasted_iota(jnp.int32, (GROUP, LANES), 1).astype(F32)
    rank_ref[1] = jnp.floor(ahead * (1.0 / LANES)) + jnp.where(spot < first, 1.0, 0.0)
    live = jnp.max(ahead + sums, axis=0, keepdims=True)
    others = live - jnp.min(sums, axis=0, keepdims=True)
    far = jnp.max(far, axis=0, keepdims=True)
    choice = jnp.full((1, LANES), len(SIZES) - 1.0, F32)
    for at in reversed(range(len(SIZES) - 1)):
        blocks, early, apart = SIZES[at]
        need = others if apart else live
        choice = jnp.where((need <= blocks * BLOCK) & (far <= early * BLOCK), float(at), choice)
    choice_ref[0] = choice[0, 0].astype(jnp.int32)
    wait_bytes(near, send_sem.at[1])


def three_rows(group):
    return jnp.concatenate(list(pieces(group)) + [jnp.zeros_like(group)], 0).astype(BF16)


def halved(rows):
    return rows[0:8] + rows[8:16]


def joined(rows):
    return halved(rows) + rows[16:24]


def pair_weights(r2, dot):
    inv = lax.rsqrt(r2)
    inv2 = inv * inv
    w = inv * inv2
    out = []
    for value in (w, (w * inv2) * dot):
        high = value.astype(BF16)
        out.append((high, (value - high.astype(F32)).astype(BF16)))
    return out


def force_of(by_w, by_u, target):
    sub = lax.broadcasted_iota(jnp.int32, target.shape, 0)
    by_w, by_u = by_w - target * by_w[3:4, :], by_u - target * by_u[3:4, :]
    return by_w - 3.0 * jnp.where(sub >= 4, pltpu.roll(by_u, 4, 0), 0.0)


def force_apart(group, feature_ref, moment_ref):
    sub = lax.broadcasted_iota(jnp.int32, group.shape, 0)
    target = jnp.where((sub == 3) | (sub == 7), 0.0, group)
    both = mm(feature_ref[...], jnp.concatenate(target_features(target), 1))
    sums = []
    for high, low in pair_weights(both[:, :LANES], both[:, LANES:]):
        halves = mm(moment_ref[...], jnp.concatenate([high, low], 1))
        sums.append(joined(halves[:, :LANES] + halves[:, LANES:]))
    return force_of(*sums, target)


def force_kernel(blocks, early, apart, count_ref, feature_ref, moment_ref, all_ref, rank_ref, out_ref,
                 part_ref, hot, near_ref, along_ref, target_ref, force_ref,
                 first, second, summed, send_sem, recv_sem):
    greet()
    tiles = blocks * BLOCK // LANES
    spot = lax.broadcasted_iota(jnp.int32, (LANES, LANES), 0).astype(F32)
    packed = [jnp.zeros((8, LANES), F32)] * tiles
    for g in range(GROUP):
        hot[g] = jnp.where(spot == rank_ref[0, g:g + 1, :], 1.0, 0.0).astype(BF16)
        chosen = joined(mm_t(three_rows(all_ref[g]), hot[g]))
        tile = rank_ref[1, g:g + 1, :]
        packed = [old + jnp.where(tile == at, chosen, 0.0) for at, old in enumerate(packed)]
    row_id = lax.broadcasted_iota(jnp.int32, (8, LANES), 0)
    for at in range(tiles):
        cols = pl.ds(at * LANES, LANES)
        target_ref[:, cols] = jnp.where((row_id == 3) | (row_id == 7), 0.0, packed[at])

    def weigh(cols):
        near_ref[:, cols], along_ref[:, cols] = target_features(target_ref[:, cols])

    weigh(pl.ds(0, BLOCK))

    def block(index, carry):
        lead = index * BLOCK
        cols = pl.ds(lead if isinstance(index, int) else pl.multiple_of(lead, BLOCK), BLOCK)
        r2 = mm(feature_ref[...], near_ref[:, cols])
        dot = mm(feature_ref[...], along_ref[:, cols])
        sums = [halved(mm(moment_ref[0:16, :], low)) + joined(mm(moment_ref[...], high))
                for high, low in pair_weights(r2, dot)]
        force_ref[:, cols] = force_of(*sums, target_ref[:, cols])
        if not isinstance(index, int):
            weigh(pl.ds(pl.multiple_of(lax.rem(index + 1, blocks) * BLOCK, BLOCK), BLOCK))
        elif index + 1 < blocks:
            weigh(pl.ds((index + 1) * BLOCK, BLOCK))
        return carry

    def unpack(peer, done):
        tile = rank_ref[1, pl.ds(peer, 1), :]
        chosen = jnp.zeros((8, LANES), F32)
        for at in range(done * BLOCK // LANES):
            chosen = jnp.where(tile == at, force_ref[:, at * LANES:(at + 1) * LANES], chosen)
        part_ref[peer] = joined(mm(three_rows(chosen), hot[peer]))

    def send(at, peer, device):
        pltpu.make_async_remote_copy(
            src_ref=part_ref.at[peer], dst_ref=first.at[at],
            send_sem=send_sem.at[0], recv_sem=recv_sem.at[0],
            device_id=device, device_id_type=MESH).start()

    row, z, y_lo, core, zc, xy = place()
    peers = xy_peers()

    def send_far():
        for peer, device in peers[:FAR]:
            unpack(peer, early)
        await_greetings()
        for at in range(FAR):
            send(at, *peers[at])

    def step(index, carry):
        pl.when(index == early)(send_far)
        return block(index, carry)

    if blocks == 3:
        for index in range(blocks):
            if index == early:
                send_far()
            block(index, 0)
    else:
        lax.fori_loop(0, blocks, step, 0)
    if early == blocks:
        send_far()
    for at in range(FAR, GROUP - 1):
        unpack(peers[at][0], blocks)
        send(at, *peers[at])
    if apart:
        total = force_apart(all_ref[xy], feature_ref, moment_ref)
    else:
        unpack(xy, blocks)
        total = part_ref[xy]
    wait_bytes(first, recv_sem.at[0])
    for step in range(1, GROUP):
        total = total + first[step - 1]
    summed[...] = total
    for at, (peer, device) in enumerate(zc_peers()):
        pltpu.make_async_remote_copy(
            src_ref=summed, dst_ref=second.at[at],
            send_sem=send_sem.at[1], recv_sem=recv_sem.at[1],
            device_id=device, device_id_type=MESH).start()
    wait_bytes(second, recv_sem.at[1])
    for step in range(1, GROUP):
        total = total + second[step - 1]
    mine = pltpu.roll(total, lax.rem(LANES - zc * ACT, LANES), 1)
    lane = lax.broadcasted_iota(jnp.int32, (8, LANES), 1)
    out_ref[...] = jnp.where(lane < count_ref[0], mine, 0.0)
    wait_bytes(first, send_sem.at[0])
    wait_bytes(second, send_sem.at[1])


def finish_kernel(force_ref, accel_ref, jerk_ref):
    accel_ref[...] = force_ref[0:3, 0:ACT]
    jerk_ref[...] = force_ref[4:7, 0:ACT]


def local(position, velocity, accel_old, jerk_old, mass, elapsed, active_index, active_count):
    vmem = pl.BlockSpec(memory_space=pltpu.VMEM)
    smem = pl.BlockSpec(memory_space=pltpu.SMEM)
    hbm = pl.BlockSpec(memory_space=pltpu.HBM)
    tiles = (GROUP, 8, LANES)
    features, moments, everyone, rank, choice = pl.pallas_call(
        gather_kernel,
        out_shape=(
            jax.ShapeDtypeStruct((STARS, LANES), BF16),
            jax.ShapeDtypeStruct((32, STARS), BF16),
            jax.ShapeDtypeStruct(tiles, F32),
            jax.ShapeDtypeStruct((2, GROUP, LANES), F32),
            jax.ShapeDtypeStruct((1,), jnp.int32),
        ),
        in_specs=[smem, smem] + [hbm] * 6,
        out_specs=(vmem,) * 4 + (smem,),
        scratch_shapes=[pltpu.VMEM((3, STARS), F32)] * 4 + [pltpu.VMEM((TILES, LANES), F32)] * 2 + [
            pltpu.VMEM((8, STARS), F32),
            pltpu.VMEM((8, LANES), F32),
            pltpu.VMEM((GROUP - 1, 8, LANES), F32),
            pltpu.SemaphoreType.DMA((6,)),
            pltpu.SemaphoreType.DMA((2,)),
            pltpu.SemaphoreType.DMA((2,)),
        ],
        compiler_params=pltpu.CompilerParams(
            collective_id=0, has_side_effects=True, vmem_limit_bytes=56 * 2**20),
        name="gather_targets",
    )(active_index, active_count, position, velocity, accel_old, jerk_old,
      mass.reshape(TILES, LANES), elapsed.reshape(TILES, LANES))

    def forces(at):
        return pl.pallas_call(
            functools.partial(force_kernel, *SIZES[at]),
            out_shape=jax.ShapeDtypeStruct((8, LANES), F32),
            in_specs=[smem] + [vmem] * 4,
            out_specs=vmem,
            scratch_shapes=[
                pltpu.VMEM(tiles, F32),
                pltpu.VMEM((GROUP, LANES, LANES), BF16),
                pltpu.VMEM((LANES, SIZES[at][0] * BLOCK), BF16),
                pltpu.VMEM((LANES, SIZES[at][0] * BLOCK), BF16),
                pltpu.VMEM((8, SIZES[at][0] * BLOCK), F32),
                pltpu.VMEM((8, SIZES[at][0] * BLOCK), F32),
                pltpu.VMEM((GROUP - 1, 8, LANES), F32),
                pltpu.VMEM((GROUP - 1, 8, LANES), F32),
                pltpu.VMEM((8, LANES), F32),
                pltpu.SemaphoreType.DMA((2,)),
                pltpu.SemaphoreType.DMA((2,)),
            ],
            compiler_params=pltpu.CompilerParams(
                collective_id=1 + at, has_side_effects=True, vmem_limit_bytes=24 * 2**20),
            name="forces_%d%s" % (SIZES[at][0], "_apart" if SIZES[at][2] else ""),
        )

    branches = [forces(at) for at in range(len(SIZES))]
    mine = lax.switch(choice[0], branches, active_count, features, moments, everyone, rank)
    return pl.pallas_call(
        finish_kernel,
        out_shape=(jax.ShapeDtypeStruct((3, ACT), F32), jax.ShapeDtypeStruct((3, ACT), F32)),
        in_specs=[vmem],
        out_specs=(vmem, vmem),
        name="finish",
    )(mine)


def solution(mesh):
    split = P(None, ("row", "col"))
    flat = P(("row", "col"))
    return jax.shard_map(
        local,
        mesh=mesh,
        in_specs=(split, split, split, split, flat, flat, flat, flat),
        out_specs=(split, split),
        check_vma=False,
    )
```
